128 devices in a mesh: dom: 16 (over y, z_lo, core), head: 8 (over z_hi, x).
Axes of the slice: x: 4, y: 4, z: 4 (z_hi: 2, z_lo: 2; z = z_hi * 2 + z_lo), core: 2. Of those that a mesh axis runs over, the one named last changes fastest.
Arguments:
- tokens: bfloat16 [16384, 1024], P(('dom', 'head')), may hold values from -6 to 6
- w_qkv: float32 [2, 1024, 3072], P(None, ('dom', 'head')), may hold values from -0.1875 to 0.1875
- w_out: float32 [2, 1024, 1024], P(None, ('dom', 'head')), may hold values from -0.375 to 0.375
- w_up: float32 [2, 1024, 2048], P(None, ('dom', 'head')), may hold values from -0.1875 to 0.1875
- w_down: float32 [2, 2048, 1024], P(None, ('dom', 'head')), may hold values from -0.125 to 0.125
- norm_gain: float32 [2, 2, 1024], P(None, None, ('dom', 'head')), may hold values from 0.5 to 1.5
- norm_bias: float32 [2, 2, 1024], P(None, None, ('dom', 'head')), may hold values from -1.5 to 1.5
- seg_start: int32 [16384], P(('dom', 'head')), may hold values from 0 to 1023, as said below
- live_count: int32 [16], P('dom'), may hold values from 512 to 1024, as said below
- cotangent: bfloat16 [16384, 1024], P(('dom', 'head')), may hold values from -6 to 6
Outputs:
- activations: bfloat16 [16384, 1024], P(('dom', 'head'))
- d_tokens: bfloat16 [16384, 1024], P(('dom', 'head'))
- d_w_qkv: float32 [2, 1024, 3072], P(None, ('dom', 'head'))
- d_w_out: float32 [2, 1024, 1024], P(None, ('dom', 'head'))
- d_w_up: float32 [2, 1024, 2048], P(None, ('dom', 'head'))
- d_w_down: float32 [2, 2048, 1024], P(None, ('dom', 'head'))
- d_norm_gain: float32 [2, 2, 1024], P(None, None, ('dom', 'head'))
- d_norm_bias: float32 [2, 2, 1024], P(None, None, ('dom', 'head'))
The draws below stay inside these ranges and needn't reach their ends.
Inputs may be any that keep to these rules, and one draw needn't show every extreme that they name: `seg_start`: each token's context is a run of 1 to 15 consecutive positions of its domain group; every position at or past the group's live count is a context of its own; the first context of every group holds min(15, live count) tokens. `live_count`: some group is full in every draw.
All inputs are finite; a program needn't handle non-finite values.
Results may differ from the reference program's by a relative error of at most 0.015.
Values may be sent and summed in bfloat16 or wider, within the bound.
A program may use at most 256 MiB of HBM per device.

```python
import jax
import jax.numpy as jnp
from jax import lax

D = 1024
HEADS = 8
HEAD_DIM = 128
FF = 2048
LAYERS = 2
SEGMENT = 15
GROUP = 1024
TOKENS = 16384
N_DOM = 16


def shared_counts(key):
    sub_key = jax.random.fold_in(key, 101)
    counts = jax.random.randint(sub_key, (N_DOM,), GROUP // 2, GROUP + 1)
    full_group = jax.random.randint(jax.random.fold_in(sub_key, 1), (), 0, N_DOM)
    return jnp.where(jnp.arange(N_DOM) == full_group, GROUP, counts).astype(jnp.int32)


def draw_live_count(key, part):
    return shared_counts(key)


def draw_seg_start(key, part):
    counts = shared_counts(key)
    key = jax.random.fold_in(key, 7)
    marks = jax.random.randint(key, (N_DOM, GROUP), 0, 6) == 0
    places = jnp.arange(GROUP, dtype=jnp.int32)

    def one_group(total_live, flags):

        def advance(begin, item):
            place, flag = item
            cut = (place == 0) | flag & (place >= SEGMENT) | (place - begin >= SEGMENT) | (place >= total_live)
            begin = jnp.where(cut, place, begin)
            return (begin, begin)
        _, starts = lax.scan(advance, jnp.int32(0), (places, flags))
        return starts
    return jax.vmap(one_group)(counts, marks).reshape((N_DOM * GROUP,)).astype(jnp.int32)


def steps_of(stream_key, extent, shards, low, largest):
    def one(axis_at, shards_of):
        heights = jax.random.uniform(jax.random.fold_in(jax.random.fold_in(stream_key, 6), axis_at), (shards_of,), jnp.float32, low / len(shards), largest / len(shards))
        return jnp.repeat(jnp.exp(heights), extent[axis_at] // shards_of).reshape((-1,) + (1,) * (len(extent) - axis_at - 1))

    level = one(*shards[0])
    for cut in shards[1:]:
        level = level * one(*cut)
    return level


def noise(rng, extent, scale, reach, shards=(), kind=jnp.bfloat16):
    factor_of = steps_of(rng, extent, shards, -0.22, 0.18) if shards else 1.0
    drawn = jax.random.normal(rng, extent, jnp.float32) * scale * factor_of
    return jnp.minimum(jnp.maximum(drawn, -reach), reach).astype(kind)


def setup_inputs(seed: int = 0) -> dict:
    arg_keys = jax.random.split(jax.random.key(seed), 11)
    tokens = noise(arg_keys[0], (TOKENS, D), 1.0, 6.0, ((0, 128),))
    w_qkv = noise(arg_keys[1], (LAYERS, D, 3 * D), D ** -0.5, 0.1875, ((1, 128),), jnp.float32)
    w_out = noise(arg_keys[2], (LAYERS, D, D), (D // 4) ** -0.5, 0.375, ((1, 128),), jnp.float32)
    w_up = noise(arg_keys[3], (LAYERS, D, FF), D ** -0.5, 0.1875, ((1, 128),), jnp.float32)
    w_down = noise(arg_keys[4], (LAYERS, FF, D), FF ** -0.5, 0.125, ((1, 128),), jnp.float32)
    norm_gain = jnp.clip(1.0 + 0.1 * jax.random.normal(arg_keys[5], (LAYERS, 2, D), jnp.float32), 0.5, 1.5)
    norm_bias = noise(arg_keys[6], (LAYERS, 2, D), 0.3, 1.5, ((2, 128),), jnp.float32)
    seg_start = draw_seg_start(jax.random.fold_in(arg_keys[10], 71), 0)
    live_count = draw_live_count(jax.random.fold_in(arg_keys[10], 71), 0)
    cotangent = noise(arg_keys[9], (TOKENS, D), 1.0, 6.0, ((0, 128),))
    return {"tokens": tokens, "w_qkv": w_qkv, "w_out": w_out, "w_up": w_up, "w_down": w_down, "norm_gain": norm_gain, "norm_bias": norm_bias, "seg_start": seg_start, "live_count": live_count, "cotangent": cotangent}


norm_eps = 1e-05
margin_rows = 16
block_rows = 512
neg_fill = -1000000000.0
highest = lax.Precision.HIGHEST

@jax.custom_vjp
def low(v):
    return lax.optimization_barrier(v.astype(jnp.bfloat16)).astype(jnp.float32)

@jax.custom_vjp
def low_back(v):
    return v

def low_keep(v):
    return (low(v), None)

def low_pass(kept, grad):
    return (grad,)

def back_keep(v):
    return (v, None)

def back_low(kept, grad):
    return (low(grad),)
low.defvjp(low_keep, low_pass)
low_back.defvjp(back_keep, back_low)

def layer_norm(values, gain, shift):
    mean = lax.optimization_barrier(jnp.mean(values, axis=-1, keepdims=True))
    centred = values - mean
    spread = lax.optimization_barrier(jnp.mean(centred * centred, axis=-1, keepdims=True))
    return centred * lax.rsqrt(spread + norm_eps) * gain + shift

def windows(array, block_len):
    num_blocks = array.shape[1] // block_len
    blocks = array.reshape((array.shape[0], num_blocks, block_len) + array.shape[2:])
    tail = blocks[:, :, block_len - margin_rows:]
    before = jnp.concatenate([jnp.zeros_like(tail[:, :1]), tail[:, :-1]], axis=1)
    return (blocks, jnp.concatenate([before, blocks], axis=2))

def attend(query, key_all, val_all, starts):
    block_len = min(block_rows, GROUP)
    num_blocks = GROUP // block_len
    flat_count = N_DOM * num_blocks
    scaling = HEAD_DIM ** (-0.5)
    q_blocks, _ = windows(query, block_len)
    _, k_wins = windows(key_all, block_len)
    _, v_wins = windows(val_all, block_len)
    q_blocks = q_blocks.reshape((flat_count, block_len, HEADS, HEAD_DIM))
    k_wins = k_wins.reshape((flat_count, block_len + margin_rows, HEADS, HEAD_DIM))
    v_wins = v_wins.reshape((flat_count, block_len + margin_rows, HEADS, HEAD_DIM))
    seg_blocks = starts.reshape((flat_count, block_len))
    offsets = jnp.tile(jnp.arange(num_blocks, dtype=jnp.int32) * block_len, N_DOM)

    def one_block(items):
        q_rows, k_rows, v_rows, seg_rows, offset = items
        raw_scores = jnp.einsum('qhd,khd->hqk', q_rows, k_rows, precision=highest) * scaling
        q_pos = offset + jnp.arange(block_len, dtype=jnp.int32)
        k_pos = offset - margin_rows + jnp.arange(block_len + margin_rows, dtype=jnp.int32)
        allowed = (k_pos[None, :] >= seg_rows[:, None]) & (k_pos[None, :] <= q_pos[:, None])
        scores = low_back(jnp.where(allowed[None], raw_scores, neg_fill))
        attn_probs = low(jax.nn.softmax(scores, axis=-1))
        return jnp.einsum('hqk,khd->qhd', attn_probs, v_rows, precision=highest)
    mixed_rows = lax.map(jax.checkpoint(one_block), (q_blocks, k_wins, v_wins, seg_blocks, offsets))
    return mixed_rows.reshape((TOKENS, HEADS * HEAD_DIM))

def one_layer(resid, w_qkv, w_out, w_up, w_down, gain_pair, shift_pair, starts, live):
    normed = low(layer_norm(resid, gain_pair[0], shift_pair[0]))
    qkv_rows = low_back(low(jnp.dot(normed, w_qkv, precision=highest)))
    split_rows = qkv_rows.reshape((N_DOM, GROUP, HEADS, 3, HEAD_DIM))
    attended = attend(split_rows[:, :, :, 0, :], split_rows[:, :, :, 1, :], split_rows[:, :, :, 2, :], starts)
    attended = low_back(low(attended))
    branch = low_back(jnp.dot(attended, w_out, precision=highest))
    middle = resid + live * branch
    second = low(layer_norm(middle, gain_pair[1], shift_pair[1]))
    hidden = low_back(jnp.dot(second, w_up, precision=highest))
    active = low(jax.nn.gelu(hidden, approximate=False))
    result = low_back(jnp.dot(active, w_down, precision=highest))
    return middle + live * result

def reference(tokens, w_qkv, w_out, w_up, w_down, norm_gain, norm_bias, seg_start, live_count, cotangent):
    places = jnp.arange(TOKENS, dtype=jnp.int32)
    live = (places % GROUP < live_count[places // GROUP]).astype(jnp.float32)[:, None]
    starts = seg_start.reshape((N_DOM, GROUP))
    layer_step = jax.checkpoint(one_layer)

    def forward(resid, qkv_all, out_all, up_all, down_all, gain_all, shift_all):
        for layer_index in range(LAYERS):
            resid = layer_step(resid, low(qkv_all[layer_index]), low(out_all[layer_index]), low(up_all[layer_index]), low(down_all[layer_index]), low(gain_all[layer_index]), low(shift_all[layer_index]), starts, live)
        return resid
    result, pull = jax.vjp(forward, tokens.astype(jnp.float32), w_qkv, w_out, w_up, w_down, norm_gain, norm_bias)
    grads = pull(cotangent.astype(jnp.float32))
    return (result.astype(jnp.bfloat16), grads[0].astype(jnp.bfloat16), grads[1], grads[2], grads[3], grads[4], grads[5], grads[6])
```

```python
import jax
import jax.numpy as jnp
from jax import lax
from jax.experimental import pallas as pl
from jax.experimental.pallas import tpu as pltpu
from jax.sharding import PartitionSpec as P

HEADS = 8
HEAD_DIM = 128
eps = 1e-05
neg_fill = -1000000000.0
lead = 16
rows = 128
width = 1024
n_sems = 640

MESH = pl.DeviceIdType.MESH
bf16 = jnp.bfloat16
f32 = jnp.float32
AXES = ("x", "y", "z")

REGION = 1408
ln_cols = 128


def cols_of(layer, part, region):
    shift = ln_cols if (layer == 0 and region == 2) else 0
    base = region * REGION
    if part == "A":
        return base, 512 + shift
    if part == "B":
        return base + 512 + shift, 512
    return base + 1024 + shift, (384, 384, 256)[region]


down_at = (0, 384, 768)
down_len = (384, 384, 256)
sum_base = (0, 896, 1792)


def contract_last(a, b):
    return lax.dot_general(a, b, (((1,), (1,)), ((), ())), preferred_element_type=f32)


def contract_rows(a, b):
    return lax.dot_general(a, b, (((0,), (0,)), ((), ())), preferred_element_type=f32)


def dot(a, b):
    return jnp.dot(a, b, preferred_element_type=f32)


def kernel(
    tokens, w_qkv, w_out, w_up, w_down, ln_in, seg, live_count, cot,
    act_out, dtok_out, d_qkv, d_out, d_up, d_down, d_ln, park,
    W0, W1, DS, RS, DL, RL, FIN, PR, FLN, FLN2,
    TN, TA, TS, TF, UN, UA, US, UF, SN, SA, SS, SF,
    GRES, GHID, GBR, GQKV, QKV, LEAD, RIMS, RIMR, TAIL,
    X1, MID, GR, GS, GP, ACT, ATT, NRM, MASK, LNP, LNG,
    ss, rs, ls, gfree, rfree,
):
    dom = lax.axis_index("dom")
    head = lax.axis_index("head")
    me = {"y": dom // 4, "z": (head // 4) * 2 + (dom // 2) % 2, "x": head % 4, "c": dom % 2}
    core = me["c"]
    par = me["x"] % 2
    W = (W0, W1)

    def device(o):
        return (o["y"] * 4 + (o["z"] % 2) * 2 + o["c"], (o["z"] // 2) * 4 + o["x"])

    def near(axis, step):
        o = dict(me)
        o[axis] = (o[axis] + step + 4) % 4
        return device(o)

    sibling = (dom + 1 - 2 * core, head)
    partner = (dom, head + 1 - 2 * par)
    after = (dom, (head + 1) % 8)
    before = (dom, (head + 7) % 8)
    neighbours = [near(a, s) for a in AXES for s in (1, -1)]

    pending = {}
    count = [0, 0]

    def send(src, dst, to):
        k = count[0]
        count[0] += 1
        c = pltpu.make_async_remote_copy(
            src_ref=src, dst_ref=dst, send_sem=ss.at[k], recv_sem=rs.at[k],
            device_id=to, device_id_type=MESH,
        )
        c.start()
        pending[id(c)] = c
        return c

    def local(src, dst):
        k = count[1]
        count[1] += 1
        c = pltpu.make_async_copy(src, dst, ls.at[k])
        c.start()
        return c

    def drain(copies):
        for c in copies:
            c.wait_send()
            del pending[id(c)]

    def w_slab(layer, region, phase, j, a, n):
        axes = (AXES[(region + 1) % 3], AXES[(region + 2) % 3], AXES[region])
        at = dict(me)
        for k in range(phase):
            at[axes[k]] = None
        at[axes[phase]] = j
        y, z, x = at["y"], at["z"], at["x"]
        full = slice(None)
        return W[layer].at[
            core,
            full if y is None else y,
            full if z is None else z % 2,
            full if z is None else z // 2,
            full if x is None else x // 2,
            full if x is None else x % 2,
            full,
            pl.ds(a, n),
        ]

    class Gather:
        def __init__(self, layer, region, phase, a, n, share):
            self.key = (layer, region, phase)
            self.a, self.n, self.share = a, n, share
            self.axis = (AXES[(region + 1) % 3], AXES[(region + 2) % 3], AXES[region])[phase]
            self.i = me[self.axis]
            self.half = ((n // 128 + 1) // 2) * 128
            self.shares = []
            self.sent = []

        def slab(self, step, a=None, n=None):
            a = self.a if a is None else a
            n = self.n if n is None else n
            return w_slab(*self.key, (self.i + step + 4) % 4, a, n)

        def hand(self, step):
            if self.share:
                s = self.slab(step)
                self.shares.append(send(s, s, sibling))

        def s1(self):
            s = self.slab(0)
            self.c1 = [send(s, s, near(self.axis, 1)), send(s, s, near(self.axis, -1))]
            self.hand(0)

        def s2(self):
            lo = (self.a, self.half)
            hi = (self.a + self.half, self.n - self.half)
            self.c1[0].wait_recv()
            s = self.slab(-1, *lo)
            self.c2 = [send(s, s, near(self.axis, 1))]
            self.c1[1].wait_recv()
            s = self.slab(1, *hi)
            self.c2.append(send(s, s, near(self.axis, -1)))
            self.hand(-1)
            self.hand(1)

        def s3(self):
            for c in self.c2:
                c.wait_recv()
            self.hand(2)
            self.sent = self.c1 + self.c2 + self.shares

        def ready(self):
            for c in self.shares:
                c.wait_recv()

    class Many:
        def __init__(self, items):
            self.items = items

        def __getattr__(self, name):
            def call():
                for item in self.items:
                    getattr(item, name)()
            return call

    first, second, last = {}, {}, {}
    for layer in (0, 1):
        spans = []
        for region in range(3):
            c, cn = cols_of(layer, "C", region)
            spans.append((region * REGION, c + cn - region * REGION))
        first[layer] = Many([Gather(layer, r, 0, *spans[r], False) for r in range(3)])
        second[layer] = Many([Gather(layer, r, 1, *spans[r], False) for r in range(3)])
        for part in "ABC":
            last[layer, part] = Many(
                [Gather(layer, r, 2, *cols_of(layer, part, r), True) for r in range(3)]
            )

    def d_index(prefix, cols):
        full = slice(None)
        at = []
        for k in range(3):
            p = prefix[k] if k < len(prefix) else None
            if k == 0:
                at.append(full if p is None else p)
            else:
                at += [full, full] if p is None else [p // 2, p % 2]
        return tuple(at) + (full, cols)

    class Sums:
        def __init__(self, d, r, a, n):
            self.d, self.r, self.a, self.n = d, r, a, n

        def at(self, which, prefix, cols):
            ref, lead_at = which
            return ref, lead_at + d_index(prefix, cols)

        def D(self, prefix, cols):
            return self.at(self.d, prefix, cols)

        def R(self, prefix, cols):
            return self.at(self.r, prefix, cols)

    def sums_of(layer, part, region):
        if part == "L":
            return Sums((DL, ()), (RL, ()), 0, ln_cols)
        if layer == 0:
            a, n = cols_of(1, part, region)
            return Sums((W1, (0,)), (W1, (1,)), a, n)
        if part == "A":
            a, _ = cols_of(0, part, region)
            return Sums((W0, (0,)), (W0, (1,)), a, 512)
        a = sum_base[region] + (0 if part == "B" else 512)
        return Sums((DS, ()), (RS, ()), a, 512 if part == "B" else down_len[region])

    def joined(layer, region):
        b, c = sums_of(layer, "B", region), sums_of(layer, "C", region)
        return Sums(b.d, b.r, b.a, b.n + c.n)

    class Reduce:
        def __init__(self, sums, region, phase, finish=None):
            self.s, self.region, self.phase, self.finish = sums, region, phase, finish
            self.axes = (AXES[region], AXES[(region + 2) % 3], AXES[(region + 1) % 3])
            self.axis = self.axes[phase]
            self.i = me[self.axis]
            self.own = tuple(me[a] for a in self.axes[:phase])
            self.slots = (3,) * phase
            n = sums.n
            half = ((n // 128 + 1) // 2) * 128
            self.lo = pl.ds(sums.a, half)
            self.hi = pl.ds(sums.a + half, n - half) if half < n else None
            self.all = pl.ds(sums.a, n)

        def d(self, step, cols):
            return self.s.D(self.own + ((self.i + step + 4) % 4,), cols)

        def r(self, slot, cols):
            return self.s.R(self.slots + (slot,), cols)

        def push(self, step, slot, cols, way):
            if cols is None:
                return None
            ref, at = self.d(step, cols)
            to, to_at = self.r(slot, cols)
            return send(ref.at[at], to.at[to_at], near(self.axis, way))

        def s1(self):
            self.c1 = self.push(2, 2, self.lo, 1)
            self.c2 = self.push(2, 2, self.hi, -1)
            self.c3 = self.push(1, 0, self.hi, 1)
            self.c4 = self.push(-1, 1, self.lo, -1)

        def add_in(self, step, slot, cols):
            ref, at = self.d(step, cols)
            other, other_at = self.r(slot, cols)
            ref[at] = (ref[at].astype(f32) + other[other_at].astype(f32)).astype(bf16)

        def s2(self):
            self.c1.wait_recv()
            self.add_in(1, 2, self.lo)
            self.c5 = self.push(1, 0, self.lo, 1)
            self.c6 = None
            if self.hi is not None:
                self.c2.wait_recv()
                self.add_in(-1, 2, self.hi)
                self.c6 = self.push(-1, 1, self.hi, -1)

        def s3(self):
            for c in (self.c3, self.c4, self.c5, self.c6):
                if c is not None:
                    c.wait_recv()
            ref, at = self.d(0, self.all)
            total = ref[at].astype(f32)
            for slot in (0, 1):
                other, other_at = self.r(slot, self.all)
                total = total + other[other_at].astype(f32)
            if self.finish is None:
                ref[at] = total.astype(bf16)
            else:
                self.finish(total)

    def finish_at(layer, a):
        def put(total):
            FIN[layer, :, pl.ds(a, total.shape[-1])] = total
        return put

    reduce1, reduce2, reduce3 = {}, {}, {}
    for layer in (0, 1):
        for part in "ABC":
            for r in range(3):
                reduce1[layer, part, r] = Reduce(sums_of(layer, part, r), r, 0)
        reduce2[layer, "A"] = Many([Reduce(sums_of(layer, "A", r), r, 1) for r in range(3)])
        reduce3[layer, "A"] = Many([
            Reduce(sums_of(layer, "A", r), r, 2, finish_at(layer, cols_of(1, "A", r)[0])) for r in range(3)
        ])
        reduce2[layer, "BC"] = Many([Reduce(joined(layer, r), r, 1) for r in range(3)])
        reduce3[layer, "BC"] = Many([
            Reduce(joined(layer, r), r, 2, finish_at(layer, cols_of(1, "B", r)[0])) for r in range(3)
        ])

    def put_ln(total):
        FLN[...] = total

    ln_steps = [Reduce(sums_of(0, "L", 0), 0, k, put_ln if k == 2 else None) for k in range(3)]

    def many(layer, part, regions=(0, 1, 2)):
        return Many([reduce1[layer, part, r] for r in regions])

    def w_half(layer, h, a, n, ys=(0, 1, 2, 3)):
        parts = [
            W[layer][c, y, z, :, :, h, :, pl.ds(a, n)].reshape(64, n)
            for y in ys for z in (0, 1) for c in (0, 1)
        ]
        return jnp.concatenate(parts, axis=0)

    def w_down_rows(layer, a, n, ys=(0, 1, 2, 3)):
        parts = [
            W[layer][c, y, z, :, :, :, :, pl.ds(a, n)].reshape(128, n)
            for y in ys for z in (0, 1) for c in (0, 1)
        ]
        return jnp.concatenate(parts, axis=0)

    up_at = {}

    block = 32

    def live_rows(r):
        place = lax.broadcasted_iota(jnp.int32, (block, 1), 0) + (head * rows + r * block)
        return (place < live_count[0]).astype(f32)

    def live_all():
        place = lax.broadcasted_iota(jnp.int32, (rows, 1), 0) + head * rows
        return (place < live_count[0]).astype(f32)

    def stats(v):
        mean = jnp.mean(v, axis=-1, keepdims=True)
        centred = v - mean
        spread = jnp.mean(centred * centred, axis=-1, keepdims=True)
        r = lax.rsqrt(spread + eps)
        return centred * r, r

    def norm(load, which, dst):
        gain = LNP[which:which + 1, :]
        shift = LNP[4 + which:5 + which, :]

        @pl.loop(0, rows // block)
        def _(r):
            at = pl.ds(pl.multiple_of(r * block, block), block)
            n, _ = stats(load(at))
            dst[at, :] = (n * gain + shift).astype(bf16)

    def norm_back(load, which, old, new, low):
        gain = LNP[which:which + 1, :]

        def step(r, carry):
            to_gain, to_shift = carry
            at = pl.ds(pl.multiple_of(r * block, block), block)
            n, scale = stats(load(at))
            gs = GS[at, :]
            e = gs * gain
            m1 = jnp.mean(e, axis=-1, keepdims=True)
            m2 = jnp.mean(e * n, axis=-1, keepdims=True)
            g = old(at) + scale * (e - m1 - n * m2)
            new(at, g)
            if low is not None:
                low[at, :] = (live_rows(r) * g).astype(bf16)
            to_gain = to_gain + jnp.sum((gs * n).reshape(block // 8, 8, width), axis=0)
            to_shift = to_shift + jnp.sum(gs.reshape(block // 8, 8, width), axis=0)
            return to_gain, to_shift

        zero = jnp.zeros((8, width), f32)
        to_gain, to_shift = lax.fori_loop(0, rows // block, step, (zero, zero))
        LNG[which:which + 1, :] = jnp.sum(to_gain, axis=0, keepdims=True)
        LNG[4 + which:5 + which, :] = jnp.sum(to_shift, axis=0, keepdims=True)

    def turn(src, keep, stage):
        for b in range(8):
            t = src[:, b * 128:(b + 1) * 128].T
            keep[b] = jnp.where(core == 0, t[:64], t[64:])
            stage[b] = jnp.where(core == 0, t[64:], t[:64])

    def turn_wide(src, keep, stage):
        for b in range(8):
            v0 = src[:, b * 256:b * 256 + 128]
            v1 = src[:, b * 256 + 128:b * 256 + 256]
            keep[b] = jnp.where(core == 0, v0, v1).T
            stage[b] = jnp.where(core == 0, v1, v0).T

    def both(keep, got):
        k, n = keep.shape[0] * keep.shape[1], keep.shape[2]
        return jnp.concatenate([keep[...].reshape(k, n), got[...].reshape(k, n)], axis=1)

    def pair(ref, a, n):
        return jnp.concatenate([ref[0, :, pl.ds(a, n)], ref[1, :, pl.ds(a, n)]], axis=0)

    def put_terms(sums, region, value, tile, y, z, x):
        pos = {"y": y, "z": z, "x": x}
        axes = (AXES[region], AXES[(region + 2) % 3], AXES[(region + 1) % 3])
        ref, at = sums.D(tuple(pos[a] for a in axes), pl.ds(sums.a, sums.n))
        ref[at] = value[tile * 16:(tile + 1) * 16].astype(bf16)

    def terms(layer, part, region, lhs, ref, columns):
        sums = sums_of(layer, part, region)
        if part == "C":
            value = dot(lhs, pair(ref, down_at[region], down_len[region]))
            for y in range(4):
                for zl in range(2):
                    for zh in range(2):
                        for x in range(4):
                            tile = ((y * 2 + zl) * 2 + zh) * 4 + x
                            put_terms(sums, region, value, tile, y, zh * 2 + zl, x)
            return
        for h in (0, 1):
            value = dot(lhs, pair(ref, columns(h), 512))
            for y in range(4):
                for zl in range(2):
                    for zh in range(2):
                        for xp in range(2):
                            tile = ((y * 2 + zl) * 2 + zh) * 2 + xp
                            put_terms(sums, region, value, tile, y, zh * 2 + zl, 2 * xp + h)

    scaling = HEAD_DIM ** (-0.5)

    def window(layer, h, which):
        at = pl.ds(h * 384 + which * 128, 128)
        return jnp.concatenate(
            [QKV[layer, :, at], LEAD[layer, :, at], jnp.zeros((128 - lead, 128), bf16)], axis=0
        )

    def probs(layer, h):
        q = QKV[layer, :, pl.ds(h * 384, 128)]
        k = window(layer, h, 1)
        s = contract_last(q, k) * scaling
        s = jnp.where(MASK[...] > 0, s, neg_fill)
        e = jnp.exp(s - jnp.max(s, axis=-1, keepdims=True))
        return q, k, e / jnp.sum(e, axis=-1, keepdims=True)

    def attend(layer):
        for h in range(HEADS):
            _, _, p = probs(layer, h)
            ATT[:, h * 128:(h + 1) * 128] = dot(p.astype(bf16), window(layer, h, 2)).astype(bf16)

    def attend_back(layer):
        for h in range(HEADS):
            q, k, p = probs(layer, h)
            v = window(layer, h, 2)
            do = ATT[:, h * 128:(h + 1) * 128]
            gv = contract_rows(p.astype(bf16), do)
            gp = contract_last(do, v)
            gs = (p * (gp - jnp.sum(p * gp, axis=-1, keepdims=True))).astype(bf16)
            gq = dot(gs, k) * scaling
            gk = contract_rows(gs, q) * scaling
            GQKV[0, :, h * 384:h * 384 + 128] = gq.astype(bf16)
            GQKV[0, :, h * 384 + 128:h * 384 + 256] = gk[:128].astype(bf16)
            GQKV[0, :, h * 384 + 256:h * 384 + 384] = gv[:128].astype(bf16)
            TAIL[:, h * 256:h * 256 + 128] = gk[112:128]
            TAIL[:, h * 256 + 128:h * 256 + 256] = gv[112:128]
            RIMS[layer, :, h * 256:h * 256 + 128] = gk[128:144].astype(bf16)
            RIMS[layer, :, h * 256 + 128:h * 256 + 256] = gv[128:144].astype(bf16)

    def add_rim(layer):
        for h in range(HEADS):
            at = pl.ds(h * 256, 256)
            total = TAIL[:, at] + RIMR[layer, :, at].astype(f32)
            GQKV[0, 112:128, h * 384 + 128:h * 384 + 384] = total.astype(bf16)

    shared = {}

    def x_at(layer):
        if layer == 0:
            return lambda at: tokens[at, :].astype(f32)
        return lambda at: X1[at, :]

    def forward_qkv(layer):
        norm(x_at(layer), 2 * layer, NRM)
        n = NRM[...]
        for h in (0, 1):
            for r in range(3):
                a, _ = cols_of(layer, "A", r)
                at = pl.ds(h * 1536 + r * 512, 512)
                QKV[layer, :, at] = dot(n, w_half(layer, h, a, 512)).astype(bf16)
        tail = QKV.at[layer, pl.ds(rows - lead, lead), :]
        shared["rim", layer] = send(tail, LEAD.at[layer], after)
        if ("n", 0) in shared and layer == 1:
            drain([shared["n", 0]])
        turn(NRM, TN.at[layer], SN)
        shared["n", layer] = send(SN, UN.at[layer], sibling)

    def forward_attend(layer):
        shared["rim", layer].wait_recv()
        attend(layer)
        if layer == 1:
            drain([shared["a", 0]])
        turn(ATT, TA.at[layer], SA)
        shared["a", layer] = send(SA, UA.at[layer], sibling)

    def forward_up(layer):
        a_in = ATT[...]
        live = live_all()
        load = x_at(layer)
        a, _ = cols_of(layer, "B", 0)
        for h in (0, 1):
            at = pl.ds(h * 512, 512)
            x = tokens[:, at].astype(f32) if layer == 0 else X1[:, at]
            MID[layer, :, at] = x + live * dot(a_in, w_half(layer, h, a, 512))
        norm(lambda at: MID[layer, at, :], 2 * layer + 1, NRM)
        n = NRM[...]
        for h in (0, 1):
            for r in (1, 2):
                a, _ = cols_of(layer, "B", r)
                at = pl.ds(h * 1024 + (r - 1) * 512, 512)
                u = dot(n, w_half(layer, h, a, 512))
                cdf = 0.5 * (1.0 + lax.erf(u * (0.5 ** 0.5)))
                ACT[:, at] = (u * cdf).astype(bf16)
                slope = cdf + u * (jnp.exp(u * u * (-0.5)) * 0.3989422804014327)
                GP[layer, :, at] = slope.astype(bf16)
        if layer == 1:
            drain([shared["s", 0], shared["f", 0]])
        turn_wide(ACT, TF.at[layer], SF)
        shared["f", layer] = send(SF, UF.at[layer], sibling)
        turn(NRM, TS.at[layer], SS)
        shared["s", layer] = send(SS, US.at[layer], sibling)

    def forward_down(layer):
        live = live_all()
        a_in = ACT[...]
        for r in range(3):
            a, n = cols_of(layer, "C", r)
            at = pl.ds(down_at[r], n)
            v = MID[layer, :, at] + live * dot(a_in, w_down_rows(layer, a, n))
            if layer == 0:
                X1[:, at] = v
            else:
                act_out[:, at] = v.astype(bf16)

    def back_result(layer):
        if layer == 1:
            GRES[0] = (live_all() * cot[...].astype(f32)).astype(bf16)
        shared["res", layer] = send(GRES.at[0], GRES.at[1], sibling)

    def terms_down(layer):
        shared["f", layer].wait_recv()
        shared["res", layer].wait_recv()
        lhs = both(TF.at[layer], UF.at[layer])
        for r in range(3):
            terms(layer, "C", r, lhs, GRES, None)

    def back_down(layer):
        g = GRES[0]
        for y in range(4):
            w = jnp.concatenate(
                [w_down_rows(layer, *cols_of(layer, "C", r), ys=(y,)) for r in range(3)], axis=1
            )
            at = pl.ds(y * 512, 512)
            GHID[0, :, at] = (contract_last(g, w) * GP[layer, :, at].astype(f32)).astype(bf16)
        shared["hid", layer] = send(GHID.at[0], GHID.at[1], sibling)

    def terms_up(layer):
        shared["hid", layer].wait_recv()
        shared["s", layer].wait_recv()
        lhs = both(TS.at[layer], US.at[layer])
        for r in (1, 2):
            terms(layer, "B", r, lhs, GHID, lambda h, r=r: h * 1024 + (r - 1) * 512)

    def back_up(layer):
        g = GHID[0]
        for y in range(4):
            w = jnp.concatenate(
                [w_half(layer, h, cols_of(layer, "B", r)[0], 512, ys=(y,)) for h in (0, 1) for r in (1, 2)],
                axis=1,
            )
            GS[:, y * 256:(y + 1) * 256] = contract_last(g, w)

        def old(at):
            return cot[at, :].astype(f32) if layer == 1 else GR[at, :]

        def new(at, g):
            GR[at, :] = g

        norm_back(lambda at: MID[layer, at, :], 2 * layer + 1, old, new, GBR.at[0])
        shared["br", layer] = send(GBR.at[0], GBR.at[1], sibling)

    def terms_out(layer):
        shared["br", layer].wait_recv()
        shared["a", layer].wait_recv()
        terms(layer, "B", 0, both(TA.at[layer], UA.at[layer]), GBR, lambda h: h * 512)

    def back_out(layer):
        g = GBR[0]
        for y in range(4):
            w = jnp.concatenate(
                [w_half(layer, h, cols_of(layer, "B", 0)[0], 512, ys=(y,)) for h in (0, 1)], axis=1
            )
            ATT[:, y * 256:(y + 1) * 256] = contract_last(g, w).astype(bf16)

    def back_attend(layer):
        attend_back(layer)
        shared["back", layer] = send(RIMS.at[layer], RIMR.at[layer], before)

    def back_rim(layer):
        shared["back", layer].wait_recv()
        add_rim(layer)
        shared["qkv", layer] = send(GQKV.at[0], GQKV.at[1], sibling)

    def terms_qkv(layer):
        shared["qkv", layer].wait_recv()
        shared["n", layer].wait_recv()
        lhs = both(TN.at[layer], UN.at[layer])
        for r in range(3):
            terms(layer, "A", r, lhs, GQKV, lambda h, r=r: h * 1536 + r * 512)

    def back_qkv(layer):
        g = GQKV[0]
        for y in range(4):
            w = jnp.concatenate(
                [w_half(layer, h, cols_of(layer, "A", r)[0], 512, ys=(y,)) for h in (0, 1) for r in range(3)],
                axis=1,
            )
            GS[:, y * 256:(y + 1) * 256] = contract_last(g, w)

        def old(at):
            return GR[at, :]

        if layer == 1:
            drain([shared["res", 1]])

            def new(at, g):
                GR[at, :] = g

            norm_back(x_at(1), 2, old, new, GRES.at[0])
        else:
            def new(at, g):
                dtok_out[at, :] = g.astype(bf16)

            norm_back(x_at(0), 0, old, new, None)

    stage = [
        local(w_qkv, FIN.at[:, 0:8, 0:3072]),
        local(w_out, FIN.at[:, 0:8, 3072:4096]),
        local(w_up, FIN.at[:, 8:16, 0:2048]),
        local(w_down.at[:, 0:8], FIN.at[:, 8:16, 2048:3072]),
        local(w_down.at[:, 8:16], FIN.at[:, 8:16, 3072:4096]),
    ]
    barrier = pltpu.get_barrier_semaphore()
    for d in neighbours + [sibling, after, before]:
        pl.semaphore_signal(barrier, inc=1, device_id=d, device_id_type=MESH)
    pl.semaphore_wait(barrier, 9)

    other = 1 - par

    def half_cols(ref, which, n):
        return ref.at[:, :, pl.ds(pl.multiple_of(which * n, n), n)]

    swaps = [
        send(half_cols(w_qkv, other, 1536), PR.at[:, :, 0:1536], partner),
        send(half_cols(w_out, other, 512), PR.at[:, :, 1536:2048], partner),
        send(half_cols(w_up, other, 1024), PR.at[:, :, 2048:3072], partner),
    ]
    for c in stage:
        c.wait()
    mine = (core, me["y"], me["z"] % 2, me["z"] // 2, me["x"] // 2, par)

    def pack(layer, a, own, n, got):
        theirs = PR[layer, :, pl.ds(got, n)]
        low = jnp.where(par == 0, own, theirs)
        high = jnp.where(par == 0, theirs, own)
        W[layer][mine + (slice(None), pl.ds(a, n))] = jnp.concatenate([low, high], axis=0).astype(bf16)

    for layer in (0, 1):
        for r in range(3):
            a, n = cols_of(layer, "C", r)
            own = jnp.concatenate(
                [FIN[layer, 8:16, pl.ds(2048 + k * 1024 + down_at[r], n)] for k in (0, 1)], axis=0
            )
            W[layer][mine + (slice(None), pl.ds(a, n))] = own.astype(bf16)
    W0[mine + (slice(None), pl.ds(cols_of(0, "A", 2)[0] + 512, ln_cols))] = ln_in[...].astype(bf16)
    for c in swaps:
        c.wait_recv()

    def own_half(layer, top, base, n, at):
        start = pl.multiple_of(par * n + (base + at), 128)
        return FIN[layer, pl.ds(top, 8), pl.ds(start, 512)]

    for layer in (0, 1):
        for r in range(3):
            a, _ = cols_of(layer, "A", r)
            pack(layer, a, own_half(layer, 0, 0, 1536, r * 512), 512, r * 512)
        a, _ = cols_of(layer, "B", 0)
        pack(layer, a, own_half(layer, 0, 3072, 512, 0), 512, 1536)
        for r in (1, 2):
            a, _ = cols_of(layer, "B", r)
            pack(layer, a, own_half(layer, 8, 0, 1024, (r - 1) * 512), 512, 2048 + (r - 1) * 512)
        first[layer].s1()

    back_result(1)
    q_pos = head * rows + lax.broadcasted_iota(jnp.int32, (rows, 256), 0)
    col = lax.broadcasted_iota(jnp.int32, (rows, 256), 1)
    k_pos = jnp.where(col < rows, col, jnp.where(col < rows + lead, col - rows - lead, -rows * 16))
    k_pos = k_pos + head * rows
    MASK[...] = ((k_pos >= seg[...]) & (k_pos <= q_pos)).astype(f32)

    first[0].s2()
    first[0].s3()
    second[0].s1()
    first[1].s2()
    second[0].s2()
    second[0].s3()
    last[0, "A"].s1()
    first[1].s3()
    second[1].s1()
    last[0, "B"].s1()
    last[0, "A"].s2()
    second[1].s2()
    last[0, "C"].s1()
    last[0, "A"].s3()
    last[0, "A"].ready()

    ln_at = pl.ds(cols_of(0, "A", 2)[0] + 512, ln_cols)
    for y in range(4):
        for z in range(2):
            total = jnp.zeros((16, ln_cols), f32)
            for c in (0, 1):
                total = total + jnp.sum(
                    W0[c, y, z, :, :, :, :, ln_at].reshape(8, 16, ln_cols).astype(f32), axis=0
                )
            b = y * 2 + z
            LNP[:, b * 128:(b + 1) * 128] = total[:8]

    forward_qkv(0)
    last[0, "B"].s2()
    second[1].s3()
    last[1, "A"].s1()
    forward_attend(0)
    last[0, "B"].s3()
    last[0, "C"].s2()
    last[1, "B"].s1()
    last[0, "B"].ready()
    forward_up(0)
    last[0, "C"].s3()
    last[1, "A"].s2()
    last[1, "C"].s1()
    last[0, "C"].ready()
    forward_down(0)
    last[1, "A"].s3()
    last[1, "B"].s2()

    for item in last[0, "A"].items:
        drain(item.sent)
    for item in first[0].items + second[0].items:
        drain(item.c1 + item.c2)
    a_cols = [pl.ds(cols_of(0, "A", r)[0], 512) for r in range(3)]
    everything = (slice(None),) * 7
    parked = [
        local(W0.at[everything + (a_cols[r],)], park.at[everything + (pl.ds(r * 512, 512),)])
        for r in range(3)
    ]
    last[1, "A"].ready()
    forward_qkv(1)
    forward_attend(1)
    last[1, "B"].s3()
    last[1, "C"].s2()
    last[1, "B"].ready()
    forward_up(1)
    last[1, "C"].s3()
    for c in parked:
        c.wait()
    for d in neighbours:
        pl.semaphore_signal(rfree.at[1], inc=1, device_id=d, device_id_type=MESH)

    terms_down(1)
    many(1, "C").s1()
    last[1, "C"].ready()
    back_down(1)
    forward_down(1)
    terms_up(1)
    many(1, "B", (1, 2)).s1()
    back_up(1)
    many(1, "C").s2()
    terms_out(1)
    many(1, "B", (0,)).s1()
    back_out(1)
    many(1, "B", (1, 2)).s2()
    many(1, "C").s3()
    back_attend(1)
    many(1, "B", (0,)).s2()
    many(1, "B", (1, 2)).s3()
    back_rim(1)
    many(1, "B", (0,)).s3()
    reduce2[1, "BC"].s1()
    pl.semaphore_wait(rfree.at[1], 6)
    terms_qkv(1)
    many(1, "A").s1()
    back_qkv(1)

    for part in "ABC":
        for item in last[1, part].items:
            drain(item.sent)
    for item in first[1].items + second[1].items:
        drain(item.c1 + item.c2)
    for d in neighbours:
        pl.semaphore_signal(rfree.at[0], inc=1, device_id=d, device_id_type=MESH)
    drain([shared[k, 1] for k in ("hid", "br", "qkv")])
    pl.semaphore_signal(gfree, inc=1, device_id=sibling, device_id_type=MESH)

    pl.semaphore_wait(gfree, 1)
    back_result(0)
    back_down(0)
    pl.semaphore_wait(rfree.at[0], 6)
    terms_down(0)
    many(0, "C").s1()
    reduce2[1, "BC"].s2()
    many(1, "A").s2()
    terms_up(0)
    many(0, "B", (1, 2)).s1()
    back_up(0)
    reduce2[1, "BC"].s3()
    reduce3[1, "BC"].s1()
    many(1, "A").s3()
    reduce2[1, "A"].s1()
    terms_out(0)
    many(0, "B", (0,)).s1()
    many(0, "C").s2()
    reduce3[1, "BC"].s2()
    back_out(0)
    reduce2[1, "A"].s2()
    back_attend(0)
    reduce3[1, "BC"].s3()
    many(0, "B", (1, 2)).s2()
    reduce2[1, "A"].s3()
    reduce3[1, "A"].s1()
    many(0, "C").s3()
    back_rim(0)
    many(0, "B", (0,)).s2()
    terms_qkv(0)
    many(0, "A").s1()
    reduce3[1, "A"].s2()
    many(0, "B", (1, 2)).s3()
    many(0, "B", (0,)).s3()
    reduce2[0, "BC"].s1()
    reduce3[1, "A"].s3()
    for item in many(1, "A").items + reduce2[1, "A"].items + reduce3[1, "A"].items:
        drain([c for c in (item.c1, item.c2, item.c3, item.c4, item.c5, item.c6) if c is not None])
    restored = [
        local(park.at[everything + (pl.ds(r * 512, 512),)], W0.at[everything + (a_cols[r],)])
        for r in range(3)
    ]
    swapped = {}

    def swap(layer):
        rows_at = pl.ds(pl.multiple_of((1 - par) * 8, 8), 8)
        swapped[layer] = send(FIN.at[layer, rows_at, :], PR.at[layer], partner)

    outs = []

    def write_out(layer):
        swapped[layer].wait_recv()
        rows_at = pl.ds(pl.multiple_of(par * 8, 8), 8)

        def put(dst, a, n, total, base):
            mine_at = pl.ds(pl.multiple_of(par * total + base, 128), n)
            other_at = pl.ds(pl.multiple_of((1 - par) * total + base, 128), n)
            outs.append(local(FIN.at[layer, rows_at, pl.ds(a, n)], dst.at[layer, :, mine_at]))
            outs.append(local(PR.at[layer, :, pl.ds(a, n)], dst.at[layer, :, other_at]))

        for r in range(3):
            put(d_qkv, cols_of(1, "A", r)[0], 512, 1536, r * 512)
            a, n = cols_of(1, "C", r)
            outs.append(local(FIN.at[layer, :, pl.ds(a, n)], d_down.at[layer, :, pl.ds(down_at[r], n)]))
        put(d_out, cols_of(1, "B", 0)[0], 512, 512, 0)
        for r in (1, 2):
            put(d_up, cols_of(1, "B", r)[0], 512, 1024, (r - 1) * 512)

    swap(1)
    many(0, "A").s2()
    reduce2[0, "BC"].s2()
    for c in restored:
        c.wait()
    back_qkv(0)
    for y in range(4):
        for z in range(2):
            b = y * 2 + z
            tile = jnp.concatenate([LNG[:, b * 128:(b + 1) * 128], jnp.zeros((8, 128), f32)], axis=0)
            tile = tile.astype(bf16)
            for zh in range(2):
                for x in range(4):
                    pos = {"y": y, "z": zh * 2 + z, "x": x}
                    ref, at = ln_steps[0].s.D(tuple(pos[a] for a in ln_steps[0].axes), slice(None))
                    ref[at] = tile
    ln_steps[0].s1()
    many(0, "A").s3()
    reduce2[0, "A"].s1()
    ln_steps[0].s2()
    reduce2[0, "BC"].s3()
    reduce3[0, "BC"].s1()
    reduce2[0, "A"].s2()
    ln_steps[0].s3()
    ln_steps[1].s1()
    reduce3[0, "BC"].s2()
    ln_steps[1].s2()
    reduce2[0, "A"].s3()
    reduce3[0, "A"].s1()
    write_out(1)
    reduce3[0, "BC"].s3()
    ln_steps[1].s3()
    ln_steps[2].s1()
    reduce3[0, "A"].s2()
    ln_steps[2].s2()
    reduce3[0, "A"].s3()
    swap(0)
    ln_steps[2].s3()
    ln_swap = send(FLN, FLN2, sibling)
    write_out(0)
    ln_swap.wait_recv()
    d_ln[...] = FLN[...] + FLN2[...]
    for c in outs:
        c.wait()
    for c in pending.values():
        c.wait_send()


def shards(
    tokens, w_qkv, w_out, w_up, w_down, norm_gain, norm_bias, seg_start, live_count, cotangent
):
    place = (lax.axis_index("dom") * 8 + lax.axis_index("head")) % 16
    vectors = jnp.concatenate([norm_gain.reshape(4, 8), norm_bias.reshape(4, 8)], axis=0)
    lanes = lax.broadcasted_iota(jnp.int32, (8, 128), 1) // 8
    tile = jnp.where(lanes == place, jnp.tile(vectors, (1, 16)), 0.0)
    ln_in = jnp.concatenate([tile, jnp.zeros((8, 128), f32)], axis=0)
    seg = jnp.broadcast_to(seg_start.reshape(rows, 1), (rows, 256))

    vmem = pl.BlockSpec(memory_space=pltpu.VMEM)
    smem = pl.BlockSpec(memory_space=pltpu.SMEM)
    hbm = pl.BlockSpec(memory_space=pl.ANY)
    grid = (4, 2, 2, 2, 2, 16)

    def v(shape, kind=bf16):
        return pltpu.VMEM(shape, kind)

    def s(shape, kind):
        return jax.ShapeDtypeStruct(shape, kind)

    narrow, wide = (8, 64, 128), (8, 128, 128)
    out = pl.pallas_call(
        kernel,
        out_shape=(
            s((rows, width), bf16), s((rows, width), bf16),
            s(w_qkv.shape, f32), s(w_out.shape, f32), s(w_up.shape, f32), s(w_down.shape, f32),
            s((16, 128), f32), s((2,) + grid + (1536,), bf16),
        ),
        in_specs=[vmem, hbm, hbm, hbm, hbm, vmem, vmem, smem, vmem],
        out_specs=(vmem, vmem, hbm, hbm, hbm, hbm, vmem, hbm),
        scratch_shapes=[
            v((2,) + grid + (4096 + ln_cols,)), v((2,) + grid + (4096,)),
            v(grid + (2560,)), v(grid + (2560,)), v(grid + (ln_cols,)), v(grid + (ln_cols,)),
            v((2, 16, 4096), f32), v((2, 8, 4096), f32), v((16, 128), f32), v((16, 128), f32),
            v((2,) + narrow), v((2,) + narrow), v((2,) + narrow), v((2,) + wide),
            v((2,) + narrow), v((2,) + narrow), v((2,) + narrow), v((2,) + wide),
            v(narrow), v(narrow), v(narrow), v(wide),
            v((2, rows, 1024)), v((2, rows, 2048)), v((2, rows, 1024)), v((2, rows, 3072)),
            v((2, rows, 3072)), v((2, lead, 3072)), v((2, lead, 2048)), v((2, lead, 2048)),
            v((lead, 2048), f32),
            v((rows, width), f32), v((2, rows, width), f32), v((rows, width), f32), v((rows, width), f32),
            v((2, rows, 2048)), v((rows, 2048)), v((rows, width)), v((rows, width)),
            v((rows, 256), f32), v((8, width), f32), v((8, width), f32),
            pltpu.SemaphoreType.DMA((n_sems,)), pltpu.SemaphoreType.DMA((n_sems,)),
            pltpu.SemaphoreType.DMA((64,)), pltpu.SemaphoreType.REGULAR,
            pltpu.SemaphoreType.REGULAR((2,)),
        ],
        name="layers",
        compiler_params=pltpu.CompilerParams(
            collective_id=0, has_side_effects=True, vmem_limit_bytes=64 * 2 ** 20
        ),
    )(tokens, w_qkv, w_out, w_up, w_down, ln_in, seg, live_count, cotangent)
    d_ln = lax.dynamic_slice(out[6][:8], (0, place * 8), (8, 8))
    return (
        out[0], out[1], out[2], out[3], out[4], out[5],
        d_ln[:4].reshape(2, 2, 8), d_ln[4:].reshape(2, 2, 8),
    )


def solution(mesh):
    return jax.shard_map(
        shards,
        mesh=mesh,
        in_specs=(
            P(("dom", "head"), None),
            P(None, ("dom", "head"), None),
            P(None, ("dom", "head"), None),
            P(None, ("dom", "head"), None),
            P(None, ("dom", "head"), None),
            P(None, None, ("dom", "head")),
            P(None, None, ("dom", "head")),
            P(("dom", "head")),
            P("dom"),
            P(("dom", "head"), None),
        ),
        out_specs=(
            P(("dom", "head"), None),
            P(("dom", "head"), None),
            P(None, ("dom", "head"), None),
            P(None, ("dom", "head"), None),
            P(None, ("dom", "head"), None),
            P(None, ("dom", "head"), None),
            P(None, None, ("dom", "head")),
            P(None, None, ("dom", "head")),
        ),
        check_vma=False,
    )
```

```python
import jax
import jax.numpy as jnp
from jax import lax
from jax.experimental import pallas as pl
from jax.experimental.pallas import tpu as pltpu
from jax.sharding import PartitionSpec as P

HEADS = 8
HEAD_DIM = 128
eps = 1e-05
neg_fill = -1000000000.0
lead = 16
rows = 128
width = 1024
n_send = 64
n_recv = 22
n_share = 34
n_misc = 10

MESH = pl.DeviceIdType.MESH
bf16 = jnp.bfloat16
f32 = jnp.float32
AXES = ("x", "y", "z")

REGION = 1408
ln_cols = 128


def cols_of(layer, part, region):
    shift = ln_cols if (layer == 0 and region == 2) else 0
    base = region * REGION
    if part == "A":
        return base, 512 + shift
    if part == "B":
        return base + 512 + shift, 512
    return base + 1024 + shift, (384, 384, 256)[region]


down_at = (0, 384, 768)
down_len = (384, 384, 256)
sum_base = (0, 896, 1792)


def contract_last(a, b):
    return lax.dot_general(a, b, (((1,), (1,)), ((), ())), preferred_element_type=f32)


def contract_rows(a, b):
    return lax.dot_general(a, b, (((0,), (0,)), ((), ())), preferred_element_type=f32)


def dot(a, b):
    return jnp.dot(a, b, preferred_element_type=f32)


def kernel(
    tokens, w_qkv, w_out, w_up, w_down, norm_gain, norm_bias, seg, live_count, cot,
    act_out, dtok_out, FIN, PR, FLN, park,
    W0, W1, DS, RS, DL, RL, FLN2,
    TN, TA, TS, TF, UN, UA, US, UF, SN, SA, SS, SF,
    GRES, GHID, GBR, GQKV, QKV, LEAD, RIMS, RIMR, TAIL,
    X1, MID, GR, GS, GP, ACT, ATT, NRM, MASK, LNP, LNG,
    ss, rs, ls, gfree, rfree,
):
    dom = lax.axis_index("dom")
    head = lax.axis_index("head")
    me = {"y": dom // 4, "z": (head // 4) * 2 + (dom // 2) % 2, "x": head % 4, "c": dom % 2}
    core = me["c"]
    par = me["x"] % 2
    W = (W0, W1)

    def device(o):
        return (o["y"] * 4 + (o["z"] % 2) * 2 + o["c"], (o["z"] // 2) * 4 + o["x"])

    def near(axis, step):
        o = dict(me)
        o[axis] = (o[axis] + step + 4) % 4
        return device(o)

    sibling = (dom + 1 - 2 * core, head)
    partner = (dom, head + 1 - 2 * par)
    after = (dom, (head + 1) % 8)
    before = (dom, (head + 7) % 8)
    neighbours = [near(a, s) for a in AXES for s in (1, -1)]

    pending = {}
    order = []
    turns = {}
    count = [0, 0]
    pools = {}
    for k, a in enumerate(AXES):
        pools[a, 1] = (2 * k * n_recv, n_recv)
        pools[a, -1] = ((2 * k + 1) * n_recv, n_recv)
    pools["share"] = (6 * n_recv, n_share)
    pools["misc"] = (6 * n_recv + n_share, n_misc)

    def turn_of(way):
        k = turns.get(way, 0)
        turns[way] = k + 1
        base, size = pools[way]
        return base + k % size

    def send(src, dst, to, way, recv=None):
        k = count[0] % n_send
        count[0] += 1
        if len(order) >= n_send:
            drain([order[-n_send]])
        c = pltpu.make_async_remote_copy(
            src_ref=src, dst_ref=dst, send_sem=ss.at[k],
            recv_sem=rs.at[turn_of(way) if recv is None else recv],
            device_id=to, device_id_type=MESH,
        )
        c.start()
        pending[id(c)] = c
        order.append(c)
        return c

    def step_to(src, dst, axis, way):
        return send(src, dst, near(axis, way), (axis, way))

    def local(src, dst):
        k = count[1] % 12
        count[1] += 1
        c = pltpu.make_async_copy(src, dst, ls.at[k])
        c.start()
        return c

    def drain(copies):
        for c in copies:
            if id(c) in pending:
                c.wait_send()
                del pending[id(c)]

    def w_slab(layer, region, phase, j, a, n):
        axes = (AXES[(region + 1) % 3], AXES[(region + 2) % 3], AXES[region])
        at = dict(me)
        for k in range(phase):
            at[axes[k]] = None
        at[axes[phase]] = j
        y, z, x = at["y"], at["z"], at["x"]
        full = slice(None)
        return W[layer].at[
            core,
            full if y is None else y,
            full if z is None else z % 2,
            full if z is None else z // 2,
            full if x is None else x // 2,
            full if x is None else x % 2,
            full,
            pl.ds(a, n),
        ]

    class Gather:
        def __init__(self, layer, region, phase, a, n, share):
            self.key = (layer, region, phase)
            self.a, self.n, self.share = a, n, share
            self.axis = (AXES[(region + 1) % 3], AXES[(region + 2) % 3], AXES[region])[phase]
            self.i = me[self.axis]
            self.half = ((n // 128 + 1) // 2) * 128
            self.shares = []
            self.sent = []

        def slab(self, step, a=None, n=None):
            a = self.a if a is None else a
            n = self.n if n is None else n
            return w_slab(*self.key, (self.i + step + 4) % 4, a, n)

        def hand(self, step):
            if self.share:
                s = self.slab(step)
                self.shares.append(send(s, s, sibling, "share", self.share_sem))

        def s1(self):
            if self.share:
                self.share_sem = turn_of("share")
            s = self.slab(0)
            self.c1 = [step_to(s, s, self.axis, 1), step_to(s, s, self.axis, -1)]
            self.hand(0)

        def s2(self):
            lo = (self.a, self.half)
            hi = (self.a + self.half, self.n - self.half)
            self.c1[0].wait_recv()
            s = self.slab(-1, *lo)
            self.c2 = [step_to(s, s, self.axis, 1)]
            self.c1[1].wait_recv()
            s = self.slab(1, *hi)
            self.c2.append(step_to(s, s, self.axis, -1))
            self.hand(-1)
            self.hand(1)

        def s3(self):
            for c in self.c2:
                c.wait_recv()
            self.hand(2)
            self.sent = self.c1 + self.c2 + self.shares

        def ready(self):
            layer, a, n = self.key[0], self.a, self.n
            got = W[layer].at[1 - core, :, :, :, :, :, :, pl.ds(a, n)]
            pltpu.make_async_remote_copy(
                src_ref=got, dst_ref=got, send_sem=ss.at[0], recv_sem=rs.at[self.share_sem],
                device_id=sibling, device_id_type=MESH,
            ).wait_recv()

    class Many:
        def __init__(self, items):
            self.items = items

        def __getattr__(self, name):
            def call():
                for item in self.items:
                    getattr(item, name)()
            return call

    first, second, last = {}, {}, {}
    for layer in (0, 1):
        spans = []
        for region in range(3):
            c, cn = cols_of(layer, "C", region)
            spans.append((region * REGION, c + cn - region * REGION))
        first[layer] = Many([Gather(layer, r, 0, *spans[r], False) for r in range(3)])
        second[layer] = Many([Gather(layer, r, 1, *spans[r], False) for r in range(3)])
        for part in "ABC":
            last[layer, part] = Many(
                [Gather(layer, r, 2, *cols_of(layer, part, r), True) for r in range(3)]
            )

    def d_index(prefix, cols):
        full = slice(None)
        at = []
        for k in range(3):
            p = prefix[k] if k < len(prefix) else None
            if k == 0:
                at.append(full if p is None else p)
            else:
                at += [full, full] if p is None else [p // 2, p % 2]
        return tuple(at) + (full, cols)

    class Sums:
        def __init__(self, d, r, a, n):
            self.d, self.r, self.a, self.n = d, r, a, n

        def at(self, which, prefix, cols):
            ref, lead_at = which
            return ref, lead_at + d_index(prefix, cols)

        def D(self, prefix, cols):
            return self.at(self.d, prefix, cols)

        def R(self, prefix, cols):
            return self.at(self.r, prefix, cols)

    def sums_of(layer, part, region):
        if part == "L":
            return Sums((DL, ()), (RL, ()), 0, ln_cols)
        if layer == 0:
            a, n = cols_of(1, part, region)
            return Sums((W1, (0,)), (W1, (1,)), a, n)
        if part == "A":
            a, _ = cols_of(0, part, region)
            return Sums((W0, (0,)), (W0, (1,)), a, 512)
        a = sum_base[region] + (0 if part == "B" else 512)
        return Sums((DS, ()), (RS, ()), a, 512 if part == "B" else down_len[region])

    def joined(layer, region):
        b, c = sums_of(layer, "B", region), sums_of(layer, "C", region)
        return Sums(b.d, b.r, b.a, b.n + c.n)

    class Reduce:
        def __init__(self, sums, region, phase, finish=None):
            self.s, self.region, self.phase, self.finish = sums, region, phase, finish
            self.axes = (AXES[region], AXES[(region + 2) % 3], AXES[(region + 1) % 3])
            self.axis = self.axes[phase]
            self.i = me[self.axis]
            self.own = tuple(me[a] for a in self.axes[:phase])
            self.slots = (3,) * phase
            n = sums.n
            half = ((n // 128 + 1) // 2) * 128
            self.lo = pl.ds(sums.a, half)
            self.hi = pl.ds(sums.a + half, n - half) if half < n else None
            self.all = pl.ds(sums.a, n)

        def d(self, step, cols):
            return self.s.D(self.own + ((self.i + step + 4) % 4,), cols)

        def r(self, slot, cols):
            return self.s.R(self.slots + (slot,), cols)

        def push(self, step, slot, cols, way):
            if cols is None:
                return None
            ref, at = self.d(step, cols)
            to, to_at = self.r(slot, cols)
            return step_to(ref.at[at], to.at[to_at], self.axis, way)

        def s1(self):
            self.c1 = self.push(2, 2, self.lo, 1)
            self.c2 = self.push(2, 2, self.hi, -1)
            self.c3 = self.push(1, 0, self.hi, 1)
            self.c4 = self.push(-1, 1, self.lo, -1)

        def add_in(self, step, slot, cols):
            ref, at = self.d(step, cols)
            other, other_at = self.r(slot, cols)
            ref[at] = (ref[at].astype(f32) + other[other_at].astype(f32)).astype(bf16)

        def s2(self):
            self.c1.wait_recv()
            self.add_in(1, 2, self.lo)
            self.c5 = self.push(1, 0, self.lo, 1)
            self.c6 = None
            if self.hi is not None:
                self.c2.wait_recv()
                self.add_in(-1, 2, self.hi)
                self.c6 = self.push(-1, 1, self.hi, -1)

        def s3(self):
            for c in (self.c3, self.c4, self.c5, self.c6):
                if c is not None:
                    c.wait_recv()
            ref, at = self.d(0, self.all)
            total = ref[at].astype(f32)
            for slot in (0, 1):
                other, other_at = self.r(slot, self.all)
                total = total + other[other_at].astype(f32)
            if self.finish is None:
                ref[at] = total.astype(bf16)
            else:
                self.finish(total)

    def finish_at(layer, a):
        def put(total):
            FIN[layer, :, pl.ds(a, total.shape[-1])] = total
        return put

    reduce1, reduce2, reduce3 = {}, {}, {}
    for layer in (0, 1):
        for part in "ABC":
            for r in range(3):
                reduce1[layer, part, r] = Reduce(sums_of(layer, part, r), r, 0)
        reduce2[layer, "A"] = Many([Reduce(sums_of(layer, "A", r), r, 1) for r in range(3)])
        reduce3[layer, "A"] = Many([
            Reduce(sums_of(layer, "A", r), r, 2, finish_at(layer, cols_of(1, "A", r)[0])) for r in range(3)
        ])
        reduce2[layer, "BC"] = Many([Reduce(joined(layer, r), r, 1) for r in range(3)])
        reduce3[layer, "BC"] = Many([
            Reduce(joined(layer, r), r, 2, finish_at(layer, cols_of(1, "B", r)[0])) for r in range(3)
        ])

    def put_ln(total):
        FLN[...] = total

    ln_steps = [Reduce(sums_of(0, "L", 0), 0, k, put_ln if k == 2 else None) for k in range(3)]

    def many(layer, part, regions=(0, 1, 2)):
        return Many([reduce1[layer, part, r] for r in regions])

    def w_half(layer, h, a, n, ys=(0, 1, 2, 3)):
        parts = [
            W[layer][c, y, z, :, :, h, :, pl.ds(a, n)].reshape(64, n)
            for y in ys for z in (0, 1) for c in (0, 1)
        ]
        return jnp.concatenate(parts, axis=0)

    def w_down_rows(layer, a, n, ys=(0, 1, 2, 3)):
        parts = [
            W[layer][c, y, z, :, :, :, :, pl.ds(a, n)].reshape(128, n)
            for y in ys for z in (0, 1) for c in (0, 1)
        ]
        return jnp.concatenate(parts, axis=0)

    up_at = {}

    block = 32

    def live_rows(r):
        place = lax.broadcasted_iota(jnp.int32, (block, 1), 0) + (head * rows + r * block)
        return (place < live_count[0]).astype(f32)

    def live_all():
        place = lax.broadcasted_iota(jnp.int32, (rows, 1), 0) + head * rows
        return (place < live_count[0]).astype(f32)

    def stats(v):
        mean = jnp.mean(v, axis=-1, keepdims=True)
        centred = v - mean
        spread = jnp.mean(centred * centred, axis=-1, keepdims=True)
        r = lax.rsqrt(spread + eps)
        return centred * r, r

    def norm(load, which, dst):
        gain = LNP[which:which + 1, :]
        shift = LNP[4 + which:5 + which, :]

        @pl.loop(0, rows // block)
        def _(r):
            at = pl.ds(pl.multiple_of(r * block, block), block)
            n, _ = stats(load(at))
            dst[at, :] = (n * gain + shift).astype(bf16)

    def norm_back(load, which, old, new, low):
        gain = LNP[which:which + 1, :]

        def step(r, carry):
            to_gain, to_shift = carry
            at = pl.ds(pl.multiple_of(r * block, block), block)
            n, scale = stats(load(at))
            gs = GS[at, :]
            e = gs * gain
            m1 = jnp.mean(e, axis=-1, keepdims=True)
            m2 = jnp.mean(e * n, axis=-1, keepdims=True)
            g = old(at) + scale * (e - m1 - n * m2)
            new(at, g)
            if low is not None:
                low[at, :] = (live_rows(r) * g).astype(bf16)
            to_gain = to_gain + jnp.sum((gs * n).reshape(block // 8, 8, width), axis=0)
            to_shift = to_shift + jnp.sum(gs.reshape(block // 8, 8, width), axis=0)
            return to_gain, to_shift

        zero = jnp.zeros((8, width), f32)
        to_gain, to_shift = lax.fori_loop(0, rows // block, step, (zero, zero))
        LNG[which:which + 1, :] = jnp.sum(to_gain, axis=0, keepdims=True)
        LNG[4 + which:5 + which, :] = jnp.sum(to_shift, axis=0, keepdims=True)

    def turn(src, keep, stage):
        for b in range(8):
            t = src[:, b * 128:(b + 1) * 128].T
            keep[b] = jnp.where(core == 0, t[:64], t[64:])
            stage[b] = jnp.where(core == 0, t[64:], t[:64])

    def turn_wide(src, keep, stage):
        for b in range(8):
            v0 = src[:, b * 256:b * 256 + 128]
            v1 = src[:, b * 256 + 128:b * 256 + 256]
            keep[b] = jnp.where(core == 0, v0, v1).T
            stage[b] = jnp.where(core == 0, v1, v0).T

    def both(keep, got):
        k, n = keep.shape[0] * keep.shape[1], keep.shape[2]
        return jnp.concatenate([keep[...].reshape(k, n), got[...].reshape(k, n)], axis=1)

    def pair(ref, a, n):
        return jnp.concatenate([ref[0, :, pl.ds(a, n)], ref[1, :, pl.ds(a, n)]], axis=0)

    def put_terms(sums, region, value, tile, y, z, x):
        pos = {"y": y, "z": z, "x": x}
        axes = (AXES[region], AXES[(region + 2) % 3], AXES[(region + 1) % 3])
        ref, at = sums.D(tuple(pos[a] for a in axes), pl.ds(sums.a, sums.n))
        ref[at] = value[tile * 16:(tile + 1) * 16].astype(bf16)

    def terms(layer, part, region, lhs, ref, columns):
        sums = sums_of(layer, part, region)
        if part == "C":
            value = dot(lhs, pair(ref, down_at[region], down_len[region]))
            for y in range(4):
                for zl in range(2):
                    for zh in range(2):
                        for x in range(4):
                            tile = ((y * 2 + zl) * 2 + zh) * 4 + x
                            put_terms(sums, region, value, tile, y, zh * 2 + zl, x)
            return
        for h in (0, 1):
            value = dot(lhs, pair(ref, columns(h), 512))
            for y in range(4):
                for zl in range(2):
                    for zh in range(2):
                        for xp in range(2):
                            tile = ((y * 2 + zl) * 2 + zh) * 2 + xp
                            put_terms(sums, region, value, tile, y, zh * 2 + zl, 2 * xp + h)

    scaling = HEAD_DIM ** (-0.5)

    def window(layer, h, which):
        at = pl.ds(h * 384 + which * 128, 128)
        return jnp.concatenate(
            [QKV[layer, :, at], LEAD[layer, :, at], jnp.zeros((128 - lead, 128), bf16)], axis=0
        )

    def probs(layer, h):
        q = QKV[layer, :, pl.ds(h * 384, 128)]
        k = window(layer, h, 1)
        s = contract_last(q, k) * scaling
        s = jnp.where(MASK[...] > 0, s, neg_fill)
        e = jnp.exp(s - jnp.max(s, axis=-1, keepdims=True))
        return q, k, e / jnp.sum(e, axis=-1, keepdims=True)

    def attend(layer):
        for h in range(HEADS):
            _, _, p = probs(layer, h)
            ATT[:, h * 128:(h + 1) * 128] = dot(p.astype(bf16), window(layer, h, 2)).astype(bf16)

    def attend_back(layer):
        for h in range(HEADS):
            q, k, p = probs(layer, h)
            v = window(layer, h, 2)
            do = ATT[:, h * 128:(h + 1) * 128]
            gv = contract_rows(p.astype(bf16), do)
            gp = contract_last(do, v)
            gs = (p * (gp - jnp.sum(p * gp, axis=-1, keepdims=True))).astype(bf16)
            gq = dot(gs, k) * scaling
            gk = contract_rows(gs, q) * scaling
            GQKV[0, :, h * 384:h * 384 + 128] = gq.astype(bf16)
            GQKV[0, :, h * 384 + 128:h * 384 + 256] = gk[:128].astype(bf16)
            GQKV[0, :, h * 384 + 256:h * 384 + 384] = gv[:128].astype(bf16)
            TAIL[:, h * 256:h * 256 + 128] = gk[112:128]
            TAIL[:, h * 256 + 128:h * 256 + 256] = gv[112:128]
            RIMS[layer, :, h * 256:h * 256 + 128] = gk[128:144].astype(bf16)
            RIMS[layer, :, h * 256 + 128:h * 256 + 256] = gv[128:144].astype(bf16)

    def add_rim(layer):
        for h in range(HEADS):
            at = pl.ds(h * 256, 256)
            total = TAIL[:, at] + RIMR[layer, :, at].astype(f32)
            GQKV[0, 112:128, h * 384 + 128:h * 384 + 384] = total.astype(bf16)

    shared = {}

    def x_at(layer):
        if layer == 0:
            return lambda at: tokens[at, :].astype(f32)
        return lambda at: X1[at, :]

    def forward_qkv(layer):
        norm(x_at(layer), 2 * layer, NRM)
        n = NRM[...]
        for h in (0, 1):
            for r in range(3):
                a, _ = cols_of(layer, "A", r)
                at = pl.ds(h * 1536 + r * 512, 512)
                QKV[layer, :, at] = dot(n, w_half(layer, h, a, 512)).astype(bf16)
        tail = QKV.at[layer, pl.ds(rows - lead, lead), :]
        shared["rim", layer] = send(tail, LEAD.at[layer], after, "misc")
        if layer == 1:
            drain([shared["n", 0]])
        turn(NRM, TN.at[layer], SN)
        shared["n", layer] = send(SN, UN.at[layer], sibling, "share")

    def forward_attend(layer):
        shared["rim", layer].wait_recv()
        attend(layer)
        if layer == 1:
            drain([shared["a", 0]])
        turn(ATT, TA.at[layer], SA)
        shared["a", layer] = send(SA, UA.at[layer], sibling, "share")

    def forward_up(layer):
        a_in = ATT[...]
        live = live_all()
        load = x_at(layer)
        a, _ = cols_of(layer, "B", 0)
        for h in (0, 1):
            at = pl.ds(h * 512, 512)
            x = tokens[:, at].astype(f32) if layer == 0 else X1[:, at]
            MID[layer, :, at] = x + live * dot(a_in, w_half(layer, h, a, 512))
        norm(lambda at: MID[layer, at, :], 2 * layer + 1, NRM)
        n = NRM[...]
        for h in (0, 1):
            for r in (1, 2):
                a, _ = cols_of(layer, "B", r)
                at = pl.ds(h * 1024 + (r - 1) * 512, 512)
                u = dot(n, w_half(layer, h, a, 512))
                cdf = 0.5 * (1.0 + lax.erf(u * (0.5 ** 0.5)))
                ACT[:, at] = (u * cdf).astype(bf16)
                slope = cdf + u * (jnp.exp(u * u * (-0.5)) * 0.3989422804014327)
                GP[layer, :, at] = slope.astype(bf16)
        if layer == 1:
            drain([shared["s", 0], shared["f", 0]])
        turn_wide(ACT, TF.at[layer], SF)
        shared["f", layer] = send(SF, UF.at[layer], sibling, "share")
        turn(NRM, TS.at[layer], SS)
        shared["s", layer] = send(SS, US.at[layer], sibling, "share")

    def forward_down(layer):
        live = live_all()
        a_in = ACT[...]
        for r in range(3):
            a, n = cols_of(layer, "C", r)
            at = pl.ds(down_at[r], n)
            v = MID[layer, :, at] + live * dot(a_in, w_down_rows(layer, a, n))
            if layer == 0:
                X1[:, at] = v
            else:
                act_out[:, at] = v.astype(bf16)

    def back_result(layer):
        if layer == 1:
            GRES[0] = (live_all() * cot[...].astype(f32)).astype(bf16)
        shared["res", layer] = send(GRES.at[0], GRES.at[1], sibling, "share")

    def terms_down(layer):
        shared["f", layer].wait_recv()
        shared["res", layer].wait_recv()
        lhs = both(TF.at[layer], UF.at[layer])
        for r in range(3):
            terms(layer, "C", r, lhs, GRES, None)

    def back_down(layer):
        g = GRES[0]
        for y in range(4):
            w = jnp.concatenate(
                [w_down_rows(layer, *cols_of(layer, "C", r), ys=(y,)) for r in range(3)], axis=1
            )
            at = pl.ds(y * 512, 512)
            GHID[0, :, at] = (contract_last(g, w) * GP[layer, :, at].astype(f32)).astype(bf16)
        shared["hid", layer] = send(GHID.at[0], GHID.at[1], sibling, "share")

    def terms_up(layer):
        shared["hid", layer].wait_recv()
        shared["s", layer].wait_recv()
        lhs = both(TS.at[layer], US.at[layer])
        for r in (1, 2):
            terms(layer, "B", r, lhs, GHID, lambda h, r=r: h * 1024 + (r - 1) * 512)

    def back_up(layer):
        g = GHID[0]
        for y in range(4):
            w = jnp.concatenate(
                [w_half(layer, h, cols_of(layer, "B", r)[0], 512, ys=(y,)) for h in (0, 1) for r in (1, 2)],
                axis=1,
            )
            GS[:, y * 256:(y + 1) * 256] = contract_last(g, w)

        def old(at):
            return cot[at, :].astype(f32) if layer == 1 else GR[at, :]

        def new(at, g):
            GR[at, :] = g

        norm_back(lambda at: MID[layer, at, :], 2 * layer + 1, old, new, GBR.at[0])
        shared["br", layer] = send(GBR.at[0], GBR.at[1], sibling, "share")

    def terms_out(layer):
        shared["br", layer].wait_recv()
        shared["a", layer].wait_recv()
        terms(layer, "B", 0, both(TA.at[layer], UA.at[layer]), GBR, lambda h: h * 512)

    def back_out(layer):
        g = GBR[0]
        for y in range(4):
            w = jnp.concatenate(
                [w_half(layer, h, cols_of(layer, "B", 0)[0], 512, ys=(y,)) for h in (0, 1)], axis=1
            )
            ATT[:, y * 256:(y + 1) * 256] = contract_last(g, w).astype(bf16)

    def back_attend(layer):
        attend_back(layer)
        shared["back", layer] = send(RIMS.at[layer], RIMR.at[layer], before, "misc")

    def back_rim(layer):
        shared["back", layer].wait_recv()
        add_rim(layer)
        shared["qkv", layer] = send(GQKV.at[0], GQKV.at[1], sibling, "share")

    def terms_qkv(layer):
        shared["qkv", layer].wait_recv()
        shared["n", layer].wait_recv()
        lhs = both(TN.at[layer], UN.at[layer])
        for r in range(3):
            terms(layer, "A", r, lhs, GQKV, lambda h, r=r: h * 1536 + r * 512)

    def back_qkv(layer):
        g = GQKV[0]
        for y in range(4):
            w = jnp.concatenate(
                [w_half(layer, h, cols_of(layer, "A", r)[0], 512, ys=(y,)) for h in (0, 1) for r in range(3)],
                axis=1,
            )
            GS[:, y * 256:(y + 1) * 256] = contract_last(g, w)

        def old(at):
            return GR[at, :]

        if layer == 1:
            drain([shared["res", 1]])

            def new(at, g):
                GR[at, :] = g

            norm_back(x_at(1), 2, old, new, GRES.at[0])
        else:
            def new(at, g):
                dtok_out[at, :] = g.astype(bf16)

            norm_back(x_at(0), 0, old, new, None)

    stage = [
        local(w_qkv, FIN.at[:, 0:8, 0:3072]),
        local(w_out, FIN.at[:, 0:8, 3072:4096]),
        local(w_up, FIN.at[:, 8:16, 0:2048]),
        local(w_down.at[:, 0:8], FIN.at[:, 8:16, 2048:3072]),
        local(w_down.at[:, 8:16], FIN.at[:, 8:16, 3072:4096]),
    ]
    barrier = pltpu.get_barrier_semaphore()
    for d in neighbours + [sibling, after, before]:
        pl.semaphore_signal(barrier, inc=1, device_id=d, device_id_type=MESH)
    pl.semaphore_wait(barrier, 9)

    other = 1 - par

    def half_cols(ref, which, n):
        return ref.at[:, :, pl.ds(pl.multiple_of(which * n, n), n)]

    swaps = [
        send(half_cols(w_qkv, other, 1536), PR.at[:, :, 0:1536], partner, "misc"),
        send(half_cols(w_out, other, 512), PR.at[:, :, 1536:2048], partner, "misc"),
        send(half_cols(w_up, other, 1024), PR.at[:, :, 2048:3072], partner, "misc"),
    ]
    for c in stage:
        c.wait()
    mine = (core, me["y"], me["z"] % 2, me["z"] // 2, me["x"] // 2, par)

    place = (dom * 8 + head) % 16

    def ln_tile():
        LNG[...] = jnp.zeros((8, width), f32)
        for k in range(4):
            LNG[k:k + 1, 0:8] = norm_gain[k // 2, k % 2:k % 2 + 1, :]
            LNG[4 + k:5 + k, 0:8] = norm_bias[k // 2, k % 2:k % 2 + 1, :]
        moved = pltpu.roll(LNG[:, 0:128], place * 8, 1)
        return jnp.concatenate([moved, jnp.zeros((8, 128), f32)], axis=0)

    def pack(layer, a, own, n, got):
        theirs = PR[layer, :, pl.ds(got, n)]
        low = jnp.where(par == 0, own, theirs)
        high = jnp.where(par == 0, theirs, own)
        W[layer][mine + (slice(None), pl.ds(a, n))] = jnp.concatenate([low, high], axis=0).astype(bf16)

    for layer in (0, 1):
        for r in range(3):
            a, n = cols_of(layer, "C", r)
            own = jnp.concatenate(
                [FIN[layer, 8:16, pl.ds(2048 + k * 1024 + down_at[r], n)] for k in (0, 1)], axis=0
            )
            W[layer][mine + (slice(None), pl.ds(a, n))] = own.astype(bf16)
    W0[mine + (slice(None), pl.ds(cols_of(0, "A", 2)[0] + 512, ln_cols))] = ln_tile().astype(bf16)
    for c in swaps:
        c.wait_recv()

    def own_half(layer, top, base, n, at):
        start = pl.multiple_of(par * n + (base + at), 128)
        return FIN[layer, pl.ds(top, 8), pl.ds(start, 512)]

    for layer in (0, 1):
        for r in range(3):
            a, _ = cols_of(layer, "A", r)
            pack(layer, a, own_half(layer, 0, 0, 1536, r * 512), 512, r * 512)
        a, _ = cols_of(layer, "B", 0)
        pack(layer, a, own_half(layer, 0, 3072, 512, 0), 512, 1536)
        for r in (1, 2):
            a, _ = cols_of(layer, "B", r)
            pack(layer, a, own_half(layer, 8, 0, 1024, (r - 1) * 512), 512, 2048 + (r - 1) * 512)
        first[layer].s1()

    back_result(1)
    q_pos = head * rows + lax.broadcasted_iota(jnp.int32, (rows, 256), 0)
    col = lax.broadcasted_iota(jnp.int32, (rows, 256), 1)
    k_pos = jnp.where(col < rows, col, jnp.where(col < rows + lead, col - rows - lead, -rows * 16))
    k_pos = k_pos + head * rows
    begins = jnp.broadcast_to(seg[...].astype(f32), (rows, rows)).T
    begins = jnp.concatenate([begins, begins], axis=1)
    MASK[...] = ((k_pos.astype(f32) >= begins) & (k_pos <= q_pos)).astype(f32)

    first[0].s2()
    first[0].s3()
    second[0].s1()
    first[1].s2()
    second[0].s2()
    second[0].s3()
    last[0, "A"].s1()
    first[1].s3()
    second[1].s1()
    last[0, "B"].s1()
    last[0, "A"].s2()
    second[1].s2()
    last[0, "C"].s1()
    last[0, "A"].s3()
    last[0, "A"].ready()

    ln_at = pl.ds(cols_of(0, "A", 2)[0] + 512, ln_cols)
    for y in range(4):
        for z in range(2):
            total = jnp.zeros((16, ln_cols), f32)
            for c in (0, 1):
                total = total + jnp.sum(
                    W0[c, y, z, :, :, :, :, ln_at].reshape(8, 16, ln_cols).astype(f32), axis=0
                )
            b = y * 2 + z
            LNP[:, b * 128:(b + 1) * 128] = total[:8]

    forward_qkv(0)
    last[0, "B"].s2()
    second[1].s3()
    last[1, "A"].s1()
    forward_attend(0)
    last[0, "B"].s3()
    last[0, "C"].s2()
    last[1, "B"].s1()
    last[0, "B"].ready()
    forward_up(0)
    last[0, "C"].s3()
    last[1, "A"].s2()
    last[1, "C"].s1()
    last[0, "C"].ready()
    forward_down(0)
    last[1, "A"].s3()
    last[1, "B"].s2()

    for item in last[0, "A"].items:
        drain(item.sent)
    for item in first[0].items + second[0].items:
        drain(item.c1 + item.c2)
    a_cols = [pl.ds(cols_of(0, "A", r)[0], 512) for r in range(3)]
    everything = (slice(None),) * 7
    parked = [
        local(W0.at[everything + (a_cols[r],)], park.at[everything + (pl.ds(r * 512, 512),)])
        for r in range(3)
    ]
    last[1, "A"].ready()
    forward_qkv(1)
    forward_attend(1)
    last[1, "B"].s3()
    last[1, "C"].s2()
    last[1, "B"].ready()
    forward_up(1)
    last[1, "C"].s3()
    for c in parked:
        c.wait()
    for d in neighbours:
        pl.semaphore_signal(rfree.at[1], inc=1, device_id=d, device_id_type=MESH)

    terms_down(1)
    many(1, "C").s1()
    last[1, "C"].ready()
    back_down(1)
    forward_down(1)
    terms_up(1)
    many(1, "B", (1, 2)).s1()
    back_up(1)
    many(1, "C").s2()
    terms_out(1)
    many(1, "B", (0,)).s1()
    back_out(1)
    many(1, "B", (1, 2)).s2()
    many(1, "C").s3()
    back_attend(1)
    many(1, "B", (0,)).s2()
    many(1, "B", (1, 2)).s3()
    back_rim(1)
    many(1, "B", (0,)).s3()
    reduce2[1, "BC"].s1()
    pl.semaphore_wait(rfree.at[1], 6)
    terms_qkv(1)
    many(1, "A").s1()
    back_qkv(1)

    for part in "ABC":
        for item in last[1, part].items:
            drain(item.sent)
    for item in first[1].items + second[1].items:
        drain(item.c1 + item.c2)
    for d in neighbours:
        pl.semaphore_signal(rfree.at[0], inc=1, device_id=d, device_id_type=MESH)
    drain([shared[k, 1] for k in ("hid", "br", "qkv")])
    pl.semaphore_signal(gfree, inc=1, device_id=sibling, device_id_type=MESH)

    pl.semaphore_wait(gfree, 1)
    back_result(0)
    back_down(0)
    pl.semaphore_wait(rfree.at[0], 6)
    terms_down(0)
    many(0, "C").s1()
    reduce2[1, "BC"].s2()
    many(1, "A").s2()
    terms_up(0)
    many(0, "B", (1, 2)).s1()
    back_up(0)
    reduce2[1, "BC"].s3()
    reduce3[1, "BC"].s1()
    many(1, "A").s3()
    reduce2[1, "A"].s1()
    terms_out(0)
    many(0, "B", (0,)).s1()
    many(0, "C").s2()
    reduce3[1, "BC"].s2()
    back_out(0)
    reduce2[1, "A"].s2()
    back_attend(0)
    reduce3[1, "BC"].s3()
    many(0, "B", (1, 2)).s2()
    reduce2[1, "A"].s3()
    reduce3[1, "A"].s1()
    many(0, "C").s3()
    back_rim(0)
    many(0, "B", (0,)).s2()
    terms_qkv(0)
    many(0, "A").s1()
    reduce3[1, "A"].s2()
    many(0, "B", (1, 2)).s3()
    many(0, "B", (0,)).s3()
    reduce2[0, "BC"].s1()
    reduce3[1, "A"].s3()
    for item in many(1, "A").items + reduce2[1, "A"].items + reduce3[1, "A"].items:
        drain([c for c in (item.c1, item.c2, item.c3, item.c4, item.c5, item.c6) if c is not None])
    restored = [
        local(park.at[everything + (pl.ds(r * 512, 512),)], W0.at[everything + (a_cols[r],)])
        for r in range(3)
    ]
    swapped = {}

    def swap(layer):
        rows_at = pl.ds(pl.multiple_of((1 - par) * 8, 8), 8)
        swapped[layer] = send(FIN.at[layer, rows_at, :], PR.at[layer], partner, "misc")

    swap(1)
    many(0, "A").s2()
    reduce2[0, "BC"].s2()
    for c in restored:
        c.wait()
    back_qkv(0)
    for y in range(4):
        for z in range(2):
            b = y * 2 + z
            tile = jnp.concatenate([LNG[:, b * 128:(b + 1) * 128], jnp.zeros((8, 128), f32)], axis=0)
            tile = tile.astype(bf16)
            for zh in range(2):
                for x in range(4):
                    pos = {"y": y, "z": zh * 2 + z, "x": x}
                    ref, at = ln_steps[0].s.D(tuple(pos[a] for a in ln_steps[0].axes), slice(None))
                    ref[at] = tile
    ln_steps[0].s1()
    many(0, "A").s3()
    reduce2[0, "A"].s1()
    ln_steps[0].s2()
    reduce2[0, "BC"].s3()
    reduce3[0, "BC"].s1()
    reduce2[0, "A"].s2()
    ln_steps[0].s3()
    ln_steps[1].s1()
    reduce3[0, "BC"].s2()
    ln_steps[1].s2()
    reduce2[0, "A"].s3()
    reduce3[0, "A"].s1()
    reduce3[0, "BC"].s3()
    ln_steps[1].s3()
    ln_steps[2].s1()
    reduce3[0, "A"].s2()
    ln_steps[2].s2()
    reduce3[0, "A"].s3()
    swap(0)
    ln_steps[2].s3()
    ln_swap = send(FLN, FLN2, sibling, "misc")
    swapped[1].wait_recv()
    swapped[0].wait_recv()
    ln_swap.wait_recv()
    drain(list(pending.values()))
    FLN[...] = FLN[...] + FLN2[...]


def results(act, dtok, fin, got, fln, act_out, dtok_out, d_qkv, d_out, d_up, d_down, d_gain, d_bias, turned):
    dom = lax.axis_index("dom")
    head = lax.axis_index("head")
    par = head % 2
    act_out[...] = act[...]
    dtok_out[...] = dtok[...]

    def put(dst, a, n, total, base):
        for layer in (0, 1):
            sums = fin[layer, :, pl.ds(a, n)]
            mine = jnp.where(par == 0, sums[:8], sums[8:])
            other = got[layer, :, pl.ds(a, n)]
            dst[layer, :, pl.ds(base, n)] = jnp.where(par == 0, mine, other)
            dst[layer, :, pl.ds(total + base, n)] = jnp.where(par == 0, other, mine)

    for r in range(3):
        put(d_qkv, cols_of(1, "A", r)[0], 512, 1536, r * 512)
        a, n = cols_of(1, "C", r)
        d_down[:, :, pl.ds(down_at[r], n)] = fin[:, :, pl.ds(a, n)]
    put(d_out, cols_of(1, "B", 0)[0], 512, 512, 0)
    for r in (1, 2):
        put(d_up, cols_of(1, "B", r)[0], 512, 1024, (r - 1) * 512)
    place = (dom * 8 + head) % 16
    turned[...] = pltpu.roll(fln[0:8, :], (128 - place * 8) % 128, 1)
    for k in range(4):
        d_gain[k // 2, k % 2:k % 2 + 1, :] = turned[k:k + 1, 0:8]
        d_bias[k // 2, k % 2:k % 2 + 1, :] = turned[4 + k:5 + k, 0:8]


def shards(
    tokens, w_qkv, w_out, w_up, w_down, norm_gain, norm_bias, seg_start, live_count, cotangent
):
    seg = seg_start.reshape(1, rows)
    vmem = pl.BlockSpec(memory_space=pltpu.VMEM)
    smem = pl.BlockSpec(memory_space=pltpu.SMEM)
    hbm = pl.BlockSpec(memory_space=pl.ANY)
    grid = (4, 2, 2, 2, 2, 16)

    def v(shape, kind=bf16):
        return pltpu.VMEM(shape, kind)

    def s(shape, kind):
        return jax.ShapeDtypeStruct(shape, kind)

    narrow, wide = (8, 64, 128), (8, 128, 128)
    out = pl.pallas_call(
        kernel,
        out_shape=(
            s((rows, width), bf16), s((rows, width), bf16), s((2, 16, 4096), f32),
            s((2, 8, 4096), f32), s((16, 128), f32), s((2,) + grid + (1536,), bf16),
        ),
        in_specs=[vmem, hbm, hbm, hbm, hbm, vmem, vmem, vmem, smem, vmem],
        out_specs=(vmem, vmem, vmem, vmem, vmem, hbm),
        scratch_shapes=[
            v((2,) + grid + (4096 + ln_cols,)), v((2,) + grid + (4096,)),
            v(grid + (2560,)), v(grid + (2560,)), v(grid + (ln_cols,)), v(grid + (ln_cols,)),
            v((16, 128), f32),
            v((2,) + narrow), v((2,) + narrow), v((2,) + narrow), v((2,) + wide),
            v((2,) + narrow), v((2,) + narrow), v((2,) + narrow), v((2,) + wide),
            v(narrow), v(narrow), v(narrow), v(wide),
            v((2, rows, 1024)), v((2, rows, 2048)), v((2, rows, 1024)), v((2, rows, 3072)),
            v((2, rows, 3072)), v((2, lead, 3072)), v((2, lead, 2048)), v((2, lead, 2048)),
            v((lead, 2048), f32),
            v((rows, width), f32), v((2, rows, width), f32), v((rows, width), f32), v((rows, width), f32),
            v((2, rows, 2048)), v((rows, 2048)), v((rows, width)), v((rows, width)),
            v((rows, 256), f32), v((8, width), f32), v((8, width), f32),
            pltpu.SemaphoreType.DMA((n_send,)), pltpu.SemaphoreType.DMA((6 * n_recv + n_share + n_misc,)),
            pltpu.SemaphoreType.DMA((12,)), pltpu.SemaphoreType.REGULAR,
            pltpu.SemaphoreType.REGULAR((2,)),
        ],
        name="layers",
        compiler_params=pltpu.CompilerParams(
            collective_id=0, has_side_effects=True, vmem_limit_bytes=64 * 2 ** 20
        ),
    )(tokens, w_qkv, w_out, w_up, w_down, norm_gain, norm_bias, seg, live_count, cotangent)
    act, dtok, fin, got, fln, _ = out
    shapes = [a.shape for a in (w_qkv, w_out, w_up, w_down, norm_gain, norm_bias)]
    return pl.pallas_call(
        results,
        out_shape=(s((rows, width), bf16), s((rows, width), bf16)) + tuple(s(a, f32) for a in shapes),
        in_specs=[vmem] * 5,
        out_specs=(vmem,) * 8,
        scratch_shapes=[v((8, 128), f32)],
        name="results",
    )(act, dtok, fin, got, fln)


def solution(mesh):
    return jax.shard_map(
        shards,
        mesh=mesh,
        in_specs=(
            P(("dom", "head"), None),
            P(None, ("dom", "head"), None),
            P(None, ("dom", "head"), None),
            P(None, ("dom", "head"), None),
            P(None, ("dom", "head"), None),
            P(None, None, ("dom", "head")),
            P(None, None, ("dom", "head")),
            P(("dom", "head")),
            P("dom"),
            P(("dom", "head"), None),
        ),
        out_specs=(
            P(("dom", "head"), None),
            P(("dom", "head"), None),
            P(None, ("dom", "head"), None),
            P(None, ("dom", "head"), None),
            P(None, ("dom", "head"), None),
            P(None, ("dom", "head"), None),
            P(None, None, ("dom", "head")),
            P(None, None, ("dom", "head")),
        ),
        check_vma=False,
    )
```

```python
import jax
import jax.numpy as jnp
from jax import lax
from jax.experimental import pallas as pl
from jax.experimental.pallas import tpu as pltpu
from jax.sharding import PartitionSpec as P

HEADS = 8
HEAD_DIM = 128
eps = 1e-05
neg_fill = -1000000000.0
lead = 16
rows = 128
width = 1024
n_send = 64
n_recv = 22
n_share = 34
n_far = 8
n_misc = 28

MESH = pl.DeviceIdType.MESH
bf16 = jnp.bfloat16
f32 = jnp.float32
AXES = ("x", "y", "z")

REGION = 1408
ln_cols = 128


def cols_of(layer, part, region):
    shift = ln_cols if (layer == 0 and region == 2) else 0
    base = region * REGION
    if part == "A":
        return base, 512 + shift
    if part == "B":
        return base + 512 + shift, 512
    return base + 1024 + shift, (384, 384, 256)[region]


down_at = (0, 384, 768)
down_len = (384, 384, 256)
sum_base = (0, 896, 1792)


def contract_last(a, b):
    return lax.dot_general(a, b, (((1,), (1,)), ((), ())), preferred_element_type=f32)


def contract_rows(a, b):
    return lax.dot_general(a, b, (((0,), (0,)), ((), ())), preferred_element_type=f32)


def dot(a, b):
    return jnp.dot(a, b, preferred_element_type=f32)


def kernel(
    tokens, w_qkv, w_out, w_up, w_down, norm_gain, norm_bias, seg, live_count, cot,
    act_out, dtok_out, FIN, FLN, park,
    W0, W1, DS, RS, LY, LZ, LX,
    TN, TA, TS, TF, UN, UA, US, UF, SN, SA, SS, SF,
    GRES, GHID, GBR, GQKV, QKV, LEAD, RIMS, RIMR, TAIL, XL, NL,
    X1, MID, GR, GS, GP, ACT, ATT, NRM, MASK, LNP, LNG,
    ss, rs, ls, gfree, rfree,
):
    dom = lax.axis_index("dom")
    head = lax.axis_index("head")
    me = {"y": dom // 4, "z": (head // 4) * 2 + (dom // 2) % 2, "x": head % 4, "c": dom % 2}
    core = me["c"]
    W = (W0, W1)

    def device(o):
        return (o["y"] * 4 + (o["z"] % 2) * 2 + o["c"], (o["z"] // 2) * 4 + o["x"])

    def near(axis, step):
        o = dict(me)
        o[axis] = (o[axis] + step + 4) % 4
        return device(o)

    sibling = (dom + 1 - 2 * core, head)
    after = (dom, (head + 1) % 8)
    before = (dom, (head + 7) % 8)
    neighbours = [near(a, s) for a in AXES for s in (1, -1)]

    pending = {}
    order = []
    turns = {}
    count = [0, 0]
    pools = {}
    for k, a in enumerate(AXES):
        pools[a, 1] = (2 * k * n_recv, n_recv)
        pools[a, -1] = ((2 * k + 1) * n_recv, n_recv)
        pools[a, 2] = (6 * n_recv + n_share + n_misc + k * n_far, n_far)
    pools["share"] = (6 * n_recv, n_share)
    pools["misc"] = (6 * n_recv + n_share, n_misc)

    def turn_of(way):
        k = turns.get(way, 0)
        turns[way] = k + 1
        base, size = pools[way]
        return base + k % size

    def send(src, dst, to, way, recv=None):
        k = count[0] % n_send
        count[0] += 1
        if len(order) >= n_send:
            drain([order[-n_send]])
        c = pltpu.make_async_remote_copy(
            src_ref=src, dst_ref=dst, send_sem=ss.at[k],
            recv_sem=rs.at[turn_of(way) if recv is None else recv],
            device_id=to, device_id_type=MESH,
        )
        c.start()
        pending[id(c)] = c
        order.append(c)
        return c

    def step_to(src, dst, axis, way):
        return send(src, dst, near(axis, way), (axis, way))

    def local(src, dst):
        k = count[1] % 12
        count[1] += 1
        c = pltpu.make_async_copy(src, dst, ls.at[k])
        c.start()
        return c

    def drain(copies):
        for c in copies:
            if id(c) in pending:
                c.wait_send()
                del pending[id(c)]

    def w_slab(layer, region, phase, j, a, n):
        axes = (AXES[(region + 1) % 3], AXES[(region + 2) % 3], AXES[region])
        at = dict(me)
        for k in range(phase):
            at[axes[k]] = None
        at[axes[phase]] = j
        y, z, x = at["y"], at["z"], at["x"]
        full = slice(None)
        return W[layer].at[
            core,
            full if y is None else y,
            full if z is None else z % 2,
            full if z is None else z // 2,
            full if x is None else x // 2,
            full if x is None else x % 2,
            full,
            pl.ds(a, n),
        ]

    class Gather:
        def __init__(self, layer, region, phase, a, n, share):
            self.key = (layer, region, phase)
            self.a, self.n, self.share = a, n, share
            self.axis = (AXES[(region + 1) % 3], AXES[(region + 2) % 3], AXES[region])[phase]
            self.i = me[self.axis]
            self.half = ((n // 128 + 1) // 2) * 128
            self.shares = []
            self.sent = []
            self.c2 = []

        def spread(self):
            s = self.slab(0)
            self.c1 = [step_to(s, s, self.axis, k) for k in (1, -1, 2)]

        def gathered(self):
            for c in self.c1:
                c.wait_recv()

        def slab(self, step, a=None, n=None):
            a = self.a if a is None else a
            n = self.n if n is None else n
            return w_slab(*self.key, (self.i + step + 4) % 4, a, n)

        def hand(self, step):
            if self.share:
                s = self.slab(step)
                self.shares.append(send(s, s, sibling, "share", self.share_sem))

        def s1(self):
            if self.share:
                self.share_sem = turn_of("share")
            s = self.slab(0)
            self.c1 = [step_to(s, s, self.axis, 1), step_to(s, s, self.axis, -1)]
            self.hand(0)

        def s2(self):
            lo = (self.a, self.half)
            hi = (self.a + self.half, self.n - self.half)
            self.c1[0].wait_recv()
            s = self.slab(-1, *lo)
            self.c2 = [step_to(s, s, self.axis, 1)]
            self.c1[1].wait_recv()
            s = self.slab(1, *hi)
            self.c2.append(step_to(s, s, self.axis, -1))
            self.hand(-1)
            self.hand(1)

        def s3(self):
            for c in self.c2:
                c.wait_recv()
            self.hand(2)
            self.sent = self.c1 + self.c2 + self.shares

        def ready(self):
            layer, a, n = self.key[0], self.a, self.n
            got = W[layer].at[1 - core, :, :, :, :, :, :, pl.ds(a, n)]
            pltpu.make_async_remote_copy(
                src_ref=got, dst_ref=got, send_sem=ss.at[0], recv_sem=rs.at[self.share_sem],
                device_id=sibling, device_id_type=MESH,
            ).wait_recv()

    class Many:
        def __init__(self, items):
            self.items = items

        def __getattr__(self, name):
            def call():
                for item in self.items:
                    getattr(item, name)()
            return call

    first, second, last = {}, {}, {}
    for layer in (0, 1):
        spans = []
        for region in range(3):
            c, cn = cols_of(layer, "C", region)
            spans.append((region * REGION, c + cn - region * REGION))
        first[layer] = Many([Gather(layer, r, 0, *spans[r], False) for r in range(3)])
        second[layer] = Many([Gather(layer, r, 1, *spans[r], False) for r in range(3)])
        for part in "ABC":
            last[layer, part] = Many(
                [Gather(layer, r, 2, *cols_of(layer, part, r), True) for r in range(3)]
            )

    def d_index(prefix, cols):
        full = slice(None)
        at = []
        for k in range(3):
            p = prefix[k] if k < len(prefix) else None
            if k == 0:
                at.append(full if p is None else p)
            else:
                at += [full, full] if p is None else [p // 2, p % 2]
        return tuple(at) + (full, cols)

    class Sums:
        def __init__(self, d, r, a, n):
            self.d, self.r, self.a, self.n = d, r, a, n

        def at(self, which, prefix, cols):
            ref, lead_at = which
            return ref, lead_at + d_index(prefix, cols)

        def D(self, prefix, cols):
            return self.at(self.d, prefix, cols)

        def R(self, prefix, cols):
            return self.at(self.r, prefix, cols)

    def sums_of(layer, part, region):
        if layer == 0:
            a, n = cols_of(1, part, region)
            return Sums((W1, (0,)), (W1, (1,)), a, n)
        if part == "A":
            a, _ = cols_of(0, part, region)
            return Sums((W0, (0,)), (W0, (1,)), a, 512)
        a = sum_base[region] + (0 if part == "B" else 512)
        return Sums((DS, ()), (RS, ()), a, 512 if part == "B" else down_len[region])

    def joined(layer, region):
        b, c = sums_of(layer, "B", region), sums_of(layer, "C", region)
        return Sums(b.d, b.r, b.a, b.n + c.n)

    class Reduce:
        def __init__(self, sums, region, phase, finish=None):
            self.s, self.region, self.phase, self.finish = sums, region, phase, finish
            self.axes = (AXES[region], AXES[(region + 2) % 3], AXES[(region + 1) % 3])
            self.axis = self.axes[phase]
            self.i = me[self.axis]
            self.own = tuple(me[a] for a in self.axes[:phase])
            self.slots = (3,) * phase
            n = sums.n
            half = ((n // 128 + 1) // 2) * 128
            self.lo = pl.ds(sums.a, half)
            self.hi = pl.ds(sums.a + half, n - half) if half < n else None
            self.all = pl.ds(sums.a, n)

        def d(self, step, cols):
            return self.s.D(self.own + ((self.i + step + 4) % 4,), cols)

        def r(self, slot, cols):
            return self.s.R(self.slots + (slot,), cols)

        def push(self, step, slot, cols, way):
            if cols is None:
                return None
            ref, at = self.d(step, cols)
            to, to_at = self.r(slot, cols)
            return step_to(ref.at[at], to.at[to_at], self.axis, way)

        def s1(self):
            self.c1 = self.push(2, 2, self.lo, 1)
            self.c2 = self.push(2, 2, self.hi, -1)
            self.c3 = self.push(1, 0, self.hi, 1)
            self.c4 = self.push(-1, 1, self.lo, -1)

        def spread(self):
            self.c1 = self.push(1, 0, self.all, 1)
            self.c2 = self.push(-1, 1, self.all, -1)
            self.c3 = self.push(2, 2, self.all, 2)
            self.c4 = self.c5 = self.c6 = None

        def collect(self):
            for c in (self.c1, self.c2, self.c3):
                c.wait_recv()
            self.total((0, 1, 2))

        def add_in(self, step, slot, cols):
            ref, at = self.d(step, cols)
            other, other_at = self.r(slot, cols)
            ref[at] = (ref[at].astype(f32) + other[other_at].astype(f32)).astype(bf16)

        def s2(self):
            self.c1.wait_recv()
            self.add_in(1, 2, self.lo)
            self.c5 = self.push(1, 0, self.lo, 1)
            self.c6 = None
            if self.hi is not None:
                self.c2.wait_recv()
                self.add_in(-1, 2, self.hi)
                self.c6 = self.push(-1, 1, self.hi, -1)

        def s3(self):
            for c in (self.c3, self.c4, self.c5, self.c6):
                if c is not None:
                    c.wait_recv()
            self.total((0, 1))

        def total(self, slots):
            ref, at = self.d(0, self.all)
            total = ref[at].astype(f32)
            for slot in slots:
                other, other_at = self.r(slot, self.all)
                total = total + other[other_at].astype(f32)
            if self.finish is None:
                ref[at] = total.astype(bf16)
            else:
                self.finish(total)

    def finish_at(layer, a):
        def put(total):
            FIN[layer, :, pl.ds(a, total.shape[-1])] = total
        return put

    reduce1, reduce2, reduce3 = {}, {}, {}
    for layer in (0, 1):
        for part in "ABC":
            for r in range(3):
                reduce1[layer, part, r] = Reduce(sums_of(layer, part, r), r, 0)
        reduce2[layer, "A"] = Many([Reduce(sums_of(layer, "A", r), r, 1) for r in range(3)])
        reduce3[layer, "A"] = Many([
            Reduce(sums_of(layer, "A", r), r, 2, finish_at(layer, cols_of(1, "A", r)[0])) for r in range(3)
        ])
        reduce2[layer, "BC"] = Many([Reduce(joined(layer, r), r, 1) for r in range(3)])
        reduce3[layer, "BC"] = Many([
            Reduce(joined(layer, r), r, 2, finish_at(layer, cols_of(1, "B", r)[0])) for r in range(3)
        ])

    def ln_send(src, dst, **moves):
        o = dict(me)
        for axis, step in moves.items():
            o[axis] = (o[axis] + step) % (2 if axis == "c" else 4)
        return send(src, dst, device(o), "misc")

    def ln_y():
        for k in (1, 2, 3):
            to = lax.rem(me["y"] + k, 4)
            src = LNG.at[:, pl.ds(pl.multiple_of(to * 256, 256), 256)]
            shared["ln_y", k] = ln_send(src, LY.at[k - 1], y=k)

    def ln_z():
        total = LNG[:, pl.ds(pl.multiple_of(me["y"] * 256, 256), 256)]
        for k in (1, 2, 3):
            shared["ln_y", k].wait_recv()
            total = total + LY[k - 1]
        LY[3] = total
        for k in (1, 2, 3):
            to = lax.rem(me["z"] + k, 2)
            src = LY.at[3, :, pl.ds(pl.multiple_of(to * 128, 128), 128)]
            shared["ln_z", k] = ln_send(src, LZ.at[k - 1], z=k)

    others = [(x, c) for x in range(4) for c in range(2) if x or c]

    def ln_x():
        total = LY[3, :, pl.ds(pl.multiple_of(lax.rem(me["z"], 2) * 128, 128), 128)]
        for k in (1, 2, 3):
            shared["ln_z", k].wait_recv()
            total = total + LZ[k - 1]
        LZ[3] = total
        for k, (x, c) in enumerate(others):
            shared["ln_x", k] = ln_send(LZ.at[3], LX.at[k], x=x, c=c)

    def ln_end():
        total = LZ[3]
        for k in range(7):
            shared["ln_x", k].wait_recv()
            total = total + LX[k]
        FLN[...] = total

    def many(layer, part, regions=(0, 1, 2)):
        return Many([reduce1[layer, part, r] for r in regions])

    def w_half(layer, h, a, n, ys=(0, 1, 2, 3)):
        parts = [
            W[layer][c, y, z, :, :, h, :, pl.ds(a, n)].reshape(64, n)
            for y in ys for z in (0, 1) for c in (0, 1)
        ]
        return jnp.concatenate(parts, axis=0)

    def w_down_rows(layer, a, n, ys=(0, 1, 2, 3)):
        parts = [
            W[layer][c, y, z, :, :, :, :, pl.ds(a, n)].reshape(128, n)
            for y in ys for z in (0, 1) for c in (0, 1)
        ]
        return jnp.concatenate(parts, axis=0)

    def settle(layer, part):
        drain(sum([item.sent for item in last[layer, part].items], []))
        for r in range(3):
            if part == "B" or part == "A":
                a, _ = cols_of(layer, part, r)

                @pl.loop(0, 16)
                def _(k):
                    c, y, z = k // 8, (k // 2) % 4, k % 2
                    for zh in (0, 1):
                        for xp in (0, 1):
                            even = W[layer][c, y, z, zh, xp, 0, :, pl.ds(a, 512)].astype(f32)
                            odd = W[layer][c, y, z, zh, xp, 1, :, pl.ds(a, 512)].astype(f32)
                            W[layer][c, y, z, zh, xp, 0, :, pl.ds(a, 512)] = jnp.concatenate(
                                [even[:8], odd[:8]], axis=0).astype(bf16)
                            W[layer][c, y, z, zh, xp, 1, :, pl.ds(a, 512)] = jnp.concatenate(
                                [even[8:], odd[8:]], axis=0).astype(bf16)

    block = 32

    def live_rows(r):
        place = lax.broadcasted_iota(jnp.int32, (block, 1), 0) + (head * rows + r * block)
        return (place < live_count[0]).astype(f32)

    def live_all():
        place = lax.broadcasted_iota(jnp.int32, (rows, 1), 0) + head * rows
        return (place < live_count[0]).astype(f32)

    def stats(v):
        mean = jnp.mean(v, axis=-1, keepdims=True)
        centred = v - mean
        spread = jnp.mean(centred * centred, axis=-1, keepdims=True)
        r = lax.rsqrt(spread + eps)
        return centred * r, r

    def norm(load, which, dst):
        gain = LNP[which:which + 1, :]
        shift = LNP[4 + which:5 + which, :]

        @pl.loop(0, rows // block)
        def _(r):
            at = pl.ds(pl.multiple_of(r * block, block), block)
            n, _ = stats(load(at))
            dst[at, :] = (n * gain + shift).astype(bf16)

    def norm_back(load, which, old, new, low):
        gain = LNP[which:which + 1, :]

        def step(r, carry):
            to_gain, to_shift = carry
            at = pl.ds(pl.multiple_of(r * block, block), block)
            n, scale = stats(load(at))
            gs = GS[at, :]
            e = gs * gain
            m1 = jnp.mean(e, axis=-1, keepdims=True)
            m2 = jnp.mean(e * n, axis=-1, keepdims=True)
            g = old(at) + scale * (e - m1 - n * m2)
            new(at, g)
            if low is not None:
                low[at, :] = (live_rows(r) * g).astype(bf16)
            to_gain = to_gain + jnp.sum((gs * n).reshape(block // 8, 8, width), axis=0)
            to_shift = to_shift + jnp.sum(gs.reshape(block // 8, 8, width), axis=0)
            return to_gain, to_shift

        zero = jnp.zeros((8, width), f32)
        to_gain, to_shift = lax.fori_loop(0, rows // block, step, (zero, zero))
        LNG[which:which + 1, :] = jnp.sum(to_gain, axis=0, keepdims=True)
        LNG[4 + which:5 + which, :] = jnp.sum(to_shift, axis=0, keepdims=True)

    def turn(src, keep, stage):
        for b in range(8):
            t = src[:, b * 128:(b + 1) * 128].T
            keep[b] = jnp.where(core == 0, t[:64], t[64:])
            stage[b] = jnp.where(core == 0, t[64:], t[:64])

    def turn_wide(src, keep, stage):
        for b in range(8):
            v0 = src[:, b * 256:b * 256 + 128]
            v1 = src[:, b * 256 + 128:b * 256 + 256]
            keep[b] = jnp.where(core == 0, v0, v1).T
            stage[b] = jnp.where(core == 0, v1, v0).T

    def both(keep, got):
        k, n = keep.shape[0] * keep.shape[1], keep.shape[2]
        return jnp.concatenate([keep[...].reshape(k, n), got[...].reshape(k, n)], axis=1)

    def pair(ref, a, n):
        return jnp.concatenate([ref[0, :, pl.ds(a, n)], ref[1, :, pl.ds(a, n)]], axis=0)

    def put_terms(sums, region, tile, y, z, x):
        pos = {"y": y, "z": z, "x": x}
        axes = (AXES[region], AXES[(region + 2) % 3], AXES[(region + 1) % 3])
        ref, at = sums.D(tuple(pos[a] for a in axes), pl.ds(sums.a, sums.n))
        ref[at] = tile.astype(bf16)

    def terms(layer, part, region, lhs, ref, columns):
        sums = sums_of(layer, part, region)
        if part == "C":
            value = dot(lhs, pair(ref, down_at[region], down_len[region]))
        else:
            left, right = (dot(lhs, pair(ref, columns(h), 512)) for h in (0, 1))
        for y in range(4):
            for zl in range(2):
                for zh in range(2):
                    for x in range(4):
                        k = ((y * 2 + zl) * 2 + zh) * 4 + x
                        if part == "C":
                            tile = value[k * 16:k * 16 + 16]
                        else:
                            tile = jnp.concatenate([left[k * 8:k * 8 + 8], right[k * 8:k * 8 + 8]], axis=0)
                        put_terms(sums, region, tile, y, zh * 2 + zl, x)

    scaling = HEAD_DIM ** (-0.5)

    def window(layer, h, which):
        at = pl.ds(h * 384 + which * 128, 128)
        return jnp.concatenate(
            [QKV[layer, :, at], LEAD[layer, :, at], jnp.zeros((128 - lead, 128), bf16)], axis=0
        )

    def probs(layer, h):
        q = QKV[layer, :, pl.ds(h * 384, 128)]
        k = window(layer, h, 1)
        s = contract_last(q, k) * scaling
        s = jnp.where(MASK[...] > 0, s, neg_fill)
        e = jnp.exp(s - jnp.max(s, axis=-1, keepdims=True))
        return q, k, e / jnp.sum(e, axis=-1, keepdims=True)

    def attend(layer, heads):
        for h in heads:
            _, _, p = probs(layer, h)
            ATT[:, h * 128:(h + 1) * 128] = dot(p.astype(bf16), window(layer, h, 2)).astype(bf16)

    def attend_back(layer):
        for h in range(HEADS):
            q, k, p = probs(layer, h)
            v = window(layer, h, 2)
            do = ATT[:, h * 128:(h + 1) * 128]
            gv = contract_rows(p.astype(bf16), do)
            gp = contract_last(do, v)
            gs = (p * (gp - jnp.sum(p * gp, axis=-1, keepdims=True))).astype(bf16)
            gq = dot(gs, k) * scaling
            gk = contract_rows(gs, q) * scaling
            GQKV[0, :, h * 384:h * 384 + 128] = gq.astype(bf16)
            GQKV[0, :, h * 384 + 128:h * 384 + 256] = gk[:128].astype(bf16)
            GQKV[0, :, h * 384 + 256:h * 384 + 384] = gv[:128].astype(bf16)
            TAIL[:, h * 256:h * 256 + 128] = gk[112:128]
            TAIL[:, h * 256 + 128:h * 256 + 256] = gv[112:128]
            RIMS[layer, :, h * 256:h * 256 + 128] = gk[128:144].astype(bf16)
            RIMS[layer, :, h * 256 + 128:h * 256 + 256] = gv[128:144].astype(bf16)

    def add_rim(layer):
        for h in range(HEADS):
            at = pl.ds(h * 256, 256)
            total = TAIL[:, at] + RIMR[layer, :, at].astype(f32)
            GQKV[0, 112:128, h * 384 + 128:h * 384 + 384] = total.astype(bf16)

    shared = {}

    def x_at(layer):
        if layer == 0:
            return lambda at: tokens[at, :].astype(f32)
        return lambda at: X1[at, :]

    def forward_norm(layer):
        norm(x_at(layer), 2 * layer, NRM)
        if layer == 0:
            shared["x", 0].wait_recv()
            n, _ = stats(XL[...].astype(f32))
            NL[0] = (n * LNP[0:1, :] + LNP[4:5, :]).astype(bf16)
        else:
            shared["x", 1] = send(NRM.at[pl.ds(rows - lead, lead), :], NL.at[1], after, "misc")
            drain([shared["n", 0]])
        turn(NRM, TN.at[layer], SN)
        shared["n", layer] = send(SN, UN.at[layer], sibling, "share")

    def forward_qkv(layer):
        if layer == 1:
            shared["x", 1].wait_recv()
        n = jnp.concatenate([NRM[...], NL[layer]], axis=0)
        for h in (0, 1):
            for r in range(3):
                a, _ = cols_of(layer, "A", r)
                at = pl.ds(h * 1536 + r * 512, 512)
                value = dot(n, w_half(layer, h, a, 512)).astype(bf16)
                QKV[layer, :, at] = value[:rows]
                LEAD[layer, :, at] = value[rows:]

    def forward_attend(layer, between=None):
        attend(layer, range(4))
        if between is not None:
            between()
        attend(layer, range(4, 8))
        if layer == 1:
            drain([shared["a", 0]])
        turn(ATT, TA.at[layer], SA)
        shared["a", layer] = send(SA, UA.at[layer], sibling, "share")

    def forward_up(layer):
        a_in = ATT[...]
        live = live_all()
        load = x_at(layer)
        a, _ = cols_of(layer, "B", 0)
        for h in (0, 1):
            at = pl.ds(h * 512, 512)
            x = tokens[:, at].astype(f32) if layer == 0 else X1[:, at]
            MID[layer, :, at] = x + live * dot(a_in, w_half(layer, h, a, 512))
        if layer == 1:
            drain([shared["x", 1]])
        norm(lambda at: MID[layer, at, :], 2 * layer + 1, NRM)
        n = NRM[...]
        for h in (0, 1):
            for r in (1, 2):
                a, _ = cols_of(layer, "B", r)
                at = pl.ds(h * 1024 + (r - 1) * 512, 512)
                u = dot(n, w_half(layer, h, a, 512))
                cdf = 0.5 * (1.0 + lax.erf(u * (0.5 ** 0.5)))
                ACT[:, at] = (u * cdf).astype(bf16)
                slope = cdf + u * (jnp.exp(u * u * (-0.5)) * 0.3989422804014327)
                GP[layer, :, at] = slope.astype(bf16)
        if layer == 1:
            drain([shared["s", 0], shared["f", 0]])
        turn_wide(ACT, TF.at[layer], SF)
        shared["f", layer] = send(SF, UF.at[layer], sibling, "share")
        turn(NRM, TS.at[layer], SS)
        shared["s", layer] = send(SS, US.at[layer], sibling, "share")

    def forward_down(layer):
        live = live_all()
        a_in = ACT[...]
        for r in range(3):
            a, n = cols_of(layer, "C", r)
            at = pl.ds(down_at[r], n)
            v = MID[layer, :, at] + live * dot(a_in, w_down_rows(layer, a, n))
            if layer == 0:
                X1[:, at] = v
            else:
                act_out[:, at] = v.astype(bf16)

    def back_result(layer):
        if layer == 1:
            GRES[0] = (live_all() * cot[...].astype(f32)).astype(bf16)
        shared["res", layer] = send(GRES.at[0], GRES.at[1], sibling, "share")

    def terms_down(layer):
        shared["f", layer].wait_recv()
        shared["res", layer].wait_recv()
        lhs = both(TF.at[layer], UF.at[layer])
        for r in range(3):
            terms(layer, "C", r, lhs, GRES, None)
            reduce1[layer, "C", r].s1()

    def back_down(layer):
        g = GRES[0]
        for y in range(4):
            w = jnp.concatenate(
                [w_down_rows(layer, *cols_of(layer, "C", r), ys=(y,)) for r in range(3)], axis=1
            )
            at = pl.ds(y * 512, 512)
            GHID[0, :, at] = (contract_last(g, w) * GP[layer, :, at].astype(f32)).astype(bf16)
        shared["hid", layer] = send(GHID.at[0], GHID.at[1], sibling, "share")

    def terms_up(layer):
        shared["hid", layer].wait_recv()
        shared["s", layer].wait_recv()
        lhs = both(TS.at[layer], US.at[layer])
        for r in (1, 2):
            terms(layer, "B", r, lhs, GHID, lambda h, r=r: h * 1024 + (r - 1) * 512)
            reduce1[layer, "B", r].s1()

    def back_up_dot(layer):
        g = GHID[0]
        for y in range(4):
            w = jnp.concatenate(
                [w_half(layer, h, cols_of(layer, "B", r)[0], 512, ys=(y,)) for h in (0, 1) for r in (1, 2)],
                axis=1,
            )
            GS[:, y * 256:(y + 1) * 256] = contract_last(g, w)

    def back_up_norm(layer):
        def old(at):
            return cot[at, :].astype(f32) if layer == 1 else GR[at, :]

        def new(at, g):
            GR[at, :] = g

        norm_back(lambda at: MID[layer, at, :], 2 * layer + 1, old, new, GBR.at[0])
        shared["br", layer] = send(GBR.at[0], GBR.at[1], sibling, "share")

    def terms_out(layer):
        shared["br", layer].wait_recv()
        shared["a", layer].wait_recv()
        terms(layer, "B", 0, both(TA.at[layer], UA.at[layer]), GBR, lambda h: h * 512)
        reduce1[layer, "B", 0].s1()

    def back_out(layer):
        g = GBR[0]
        for y in range(4):
            w = jnp.concatenate(
                [w_half(layer, h, cols_of(layer, "B", 0)[0], 512, ys=(y,)) for h in (0, 1)], axis=1
            )
            ATT[:, y * 256:(y + 1) * 256] = contract_last(g, w).astype(bf16)

    def back_attend(layer):
        attend_back(layer)
        shared["back", layer] = send(RIMS.at[layer], RIMR.at[layer], before, "misc")

    def back_rim(layer):
        shared["back", layer].wait_recv()
        add_rim(layer)
        shared["qkv", layer] = send(GQKV.at[0], GQKV.at[1], sibling, "share")

    def terms_qkv(layer):
        shared["qkv", layer].wait_recv()
        shared["n", layer].wait_recv()
        lhs = both(TN.at[layer], UN.at[layer])
        for r in range(3):
            terms(layer, "A", r, lhs, GQKV, lambda h, r=r: h * 1536 + r * 512)
            reduce1[layer, "A", r].s1()

    def w_qkv_back(layer, h, r, y):
        if layer == 1:
            return w_half(1, h, cols_of(1, "A", r)[0], 512, ys=(y,))
        parts = [
            ref[y, z, :, :, h, :, pl.ds(r * 512, 512)].reshape(64, 512)
            for z in (0, 1) for ref in (DS, RS)
        ]
        return jnp.concatenate(parts, axis=0)

    def back_qkv_dot(layer):
        g = GQKV[0]
        for y in range(4):
            w = jnp.concatenate([w_qkv_back(layer, h, r, y) for h in (0, 1) for r in range(3)], axis=1)
            GS[:, y * 256:(y + 1) * 256] = contract_last(g, w)

    def back_qkv_norm(layer):
        def old(at):
            return GR[at, :]

        if layer == 1:
            drain([shared["res", 1]])

            def new(at, g):
                GR[at, :] = g

            norm_back(x_at(1), 2, old, new, GRES.at[0])
        else:
            def new(at, g):
                dtok_out[at, :] = g.astype(bf16)

            norm_back(x_at(0), 0, old, new, None)

    stage = [
        local(w_qkv, FIN.at[:, 0:8, 0:3072]),
        local(w_out, FIN.at[:, 0:8, 3072:4096]),
        local(w_up, FIN.at[:, 8:16, 0:2048]),
        local(w_down.at[:, 0:8], FIN.at[:, 8:16, 2048:3072]),
        local(w_down.at[:, 8:16], FIN.at[:, 8:16, 3072:4096]),
    ]
    greeted = neighbours + [sibling, after, before] + [near(a, 2) for a in AXES]
    greeted += [device({**me, "x": (me["x"] + k) % 4, "c": 1 - core}) for k in (1, 2, 3)]
    barrier = pltpu.get_barrier_semaphore()
    for d in greeted:
        pl.semaphore_signal(barrier, inc=1, device_id=d, device_id_type=MESH)
    for c in stage:
        c.wait()
    mine = (core, me["y"], me["z"] % 2, me["z"] // 2, me["x"] // 2, me["x"] % 2)

    place = (dom * 8 + head) % 16

    def ln_tile():
        LNG[...] = jnp.zeros((8, width), f32)
        for k in range(4):
            LNG[k:k + 1, 0:8] = norm_gain[k // 2, k % 2:k % 2 + 1, :]
            LNG[4 + k:5 + k, 0:8] = norm_bias[k // 2, k % 2:k % 2 + 1, :]
        moved = pltpu.roll(LNG[:, 0:128], place * 8, 1)
        return jnp.concatenate([moved, jnp.zeros((8, 128), f32)], axis=0)

    def pack(layer, a, value):
        W[layer][mine + (slice(None), pl.ds(a, value.shape[-1]))] = value.astype(bf16)

    def halves(layer, top, base, n, at):
        return jnp.concatenate(
            [FIN[layer, top:top + 8, pl.ds(base + h * n + at, 512)] for h in (0, 1)], axis=0
        )

    for layer in (0, 1):
        for r in range(3):
            a, n = cols_of(layer, "C", r)
            pack(layer, a, jnp.concatenate(
                [FIN[layer, 8:16, pl.ds(2048 + k * 1024 + down_at[r], n)] for k in (0, 1)], axis=0
            ))
            pack(layer, cols_of(layer, "A", r)[0], halves(layer, 0, 0, 1536, r * 512))
        pack(layer, cols_of(layer, "B", 0)[0], halves(layer, 0, 3072, 512, 0))
        for r in (1, 2):
            pack(layer, cols_of(layer, "B", r)[0], halves(layer, 8, 0, 1024, (r - 1) * 512))
    pack(0, cols_of(0, "A", 2)[0] + 512, ln_tile())
    pl.semaphore_wait(barrier, len(greeted))
    first[0].spread()
    shared["x", 0] = send(tokens.at[pl.ds(rows - lead, lead), :], XL, after, "misc")
    first[1].spread()

    back_result(1)
    q_pos = head * rows + lax.broadcasted_iota(jnp.int32, (rows, 256), 0)
    col = lax.broadcasted_iota(jnp.int32, (rows, 256), 1)
    k_pos = jnp.where(col < rows, col, jnp.where(col < rows + lead, col - rows - lead, -rows * 16))
    k_pos = k_pos + head * rows
    begins = jnp.broadcast_to(seg[...].astype(f32), (rows, rows)).T
    begins = jnp.concatenate([begins, begins], axis=1)
    MASK[...] = ((k_pos.astype(f32) >= begins) & (k_pos <= q_pos)).astype(f32)

    first[0].gathered()
    second[0].s1()
    first[1].gathered()
    second[1].s1()
    second[0].s2()
    second[0].s3()
    last[0, "A"].s1()
    second[1].s2()
    last[0, "B"].s1()
    second[1].s3()
    last[0, "A"].s2()
    last[0, "C"].s1()
    last[0, "A"].s3()
    last[0, "B"].s2()
    last[0, "A"].ready()
    for item in first[0].items + second[0].items:
        drain(item.c1 + item.c2)
    settle(0, "A")

    ln_at = pl.ds(cols_of(0, "A", 2)[0] + 512, ln_cols)
    for y in range(4):
        for z in range(2):
            total = jnp.zeros((16, ln_cols), f32)
            for c in (0, 1):
                total = total + jnp.sum(
                    W0[c, y, z, :, :, :, :, ln_at].reshape(8, 16, ln_cols).astype(f32), axis=0
                )
            b = y * 2 + z
            LNP[:, b * 128:(b + 1) * 128] = total[:8]

    forward_norm(0)
    forward_qkv(0)
    last[1, "A"].s1()
    forward_attend(0, last[0, "C"].s2)
    last[0, "B"].s3()
    last[1, "B"].s1()
    last[0, "B"].ready()
    settle(0, "B")
    forward_up(0)
    last[0, "C"].s3()
    last[1, "A"].s2()
    last[1, "C"].s1()
    last[0, "C"].ready()
    forward_down(0)
    forward_norm(1)
    last[1, "A"].s3()
    last[1, "B"].s2()

    a_cols = [pl.ds(cols_of(0, "A", r)[0], 512) for r in range(3)]
    everything = (slice(None),) * 7
    parked = [
        local(W0.at[everything + (a_cols[r],)], park.at[everything + (pl.ds(r * 512, 512),)])
        for r in range(3)
    ]
    last[1, "A"].ready()
    for item in first[1].items + second[1].items:
        drain(item.c1 + item.c2)
    settle(1, "A")
    forward_qkv(1)
    last[1, "B"].s3()
    forward_attend(1, last[1, "C"].s2)
    last[1, "B"].ready()
    settle(1, "B")
    forward_up(1)
    last[1, "C"].s3()
    for c in parked:
        c.wait()
    for d in neighbours:
        pl.semaphore_signal(rfree.at[1], inc=1, device_id=d, device_id_type=MESH)

    terms_down(1)
    last[1, "C"].ready()
    back_down(1)
    back_up_dot(1)
    terms_up(1)
    back_up_norm(1)
    back_out(1)
    back_attend(1)
    many(1, "C").s2()
    terms_out(1)
    back_rim(1)
    back_qkv_dot(1)
    many(1, "B", (1, 2)).s2()
    pl.semaphore_wait(rfree.at[1], 6)
    terms_qkv(1)
    many(1, "C").s3()
    back_qkv_norm(1)
    forward_down(1)

    drain(sum([item.sent for item in last[1, "C"].items], []))
    for d in neighbours:
        pl.semaphore_signal(rfree.at[0], inc=1, device_id=d, device_id_type=MESH)
    drain([shared[k, 1] for k in ("hid", "br", "qkv")])
    pl.semaphore_signal(gfree, inc=1, device_id=sibling, device_id_type=MESH)

    pl.semaphore_wait(gfree, 1)
    back_result(0)
    back_down(0)
    many(1, "B", (0,)).s2()
    pl.semaphore_wait(rfree.at[0], 6)
    terms_down(0)
    back_up_dot(0)
    many(1, "B", (1, 2)).s3()
    terms_up(0)
    back_up_norm(0)
    many(1, "A").s2()
    back_out(0)
    many(1, "B", (0,)).s3()
    reduce2[1, "BC"].s1()
    back_attend(0)
    terms_out(0)
    many(0, "C").s2()
    many(1, "A").s3()
    reduce2[1, "A"].s1()
    back_rim(0)
    many(0, "B", (1, 2)).s2()
    terms_qkv(0)
    reduce2[1, "BC"].s2()
    many(0, "C").s3()
    reduce2[1, "A"].s2()
    many(0, "B", (0,)).s2()
    reduce2[1, "BC"].s3()
    reduce3[1, "BC"].spread()
    many(0, "B", (1, 2)).s3()
    reduce2[1, "A"].s3()
    reduce3[1, "A"].spread()
    many(0, "A").s2()
    reduce3[1, "BC"].collect()
    for item in sum((many(1, p).items for p in "BC"), []) + reduce2[1, "BC"].items + reduce3[1, "BC"].items:
        drain([c for c in (item.c1, item.c2, item.c3, item.c4, item.c5, item.c6) if c is not None])
    everything = (slice(None),) * 6
    restored = [
        local(park.at[0], DS.at[everything + (pl.ds(0, 1536),)]),
        local(park.at[1], RS.at[everything + (pl.ds(0, 1536),)]),
    ]
    many(0, "B", (0,)).s3()
    reduce2[0, "BC"].s1()
    for c in restored:
        c.wait()
    back_qkv_dot(0)
    back_qkv_norm(0)
    ln_y()
    many(0, "A").s3()
    reduce2[0, "A"].spread()
    reduce2[0, "BC"].s2()
    reduce3[1, "A"].collect()
    ln_z()
    reduce2[0, "A"].collect()
    reduce3[0, "A"].spread()
    reduce2[0, "BC"].s3()
    reduce3[0, "BC"].spread()
    ln_x()
    reduce3[0, "A"].collect()
    reduce3[0, "BC"].collect()
    ln_end()
    drain(list(pending.values()))


def results(act, dtok, fin, fln, act_out, dtok_out, d_qkv, d_out, d_up, d_down, d_gain, d_bias, turned):
    dom = lax.axis_index("dom")
    head = lax.axis_index("head")
    act_out[...] = act[...]
    dtok_out[...] = dtok[...]

    def put(dst, a, n, total, base):
        dst[:, :, pl.ds(base, n)] = fin[:, 0:8, pl.ds(a, n)]
        dst[:, :, pl.ds(total + base, n)] = fin[:, 8:16, pl.ds(a, n)]

    for r in range(3):
        put(d_qkv, cols_of(1, "A", r)[0], 512, 1536, r * 512)
        a, n = cols_of(1, "C", r)
        d_down[:, :, pl.ds(down_at[r], n)] = fin[:, :, pl.ds(a, n)]
    put(d_out, cols_of(1, "B", 0)[0], 512, 512, 0)
    for r in (1, 2):
        put(d_up, cols_of(1, "B", r)[0], 512, 1024, (r - 1) * 512)
    place = (dom * 8 + head) % 16
    turned[...] = pltpu.roll(fln[...], (128 - place * 8) % 128, 1)
    for k in range(4):
        d_gain[k // 2, k % 2:k % 2 + 1, :] = turned[k:k + 1, 0:8]
        d_bias[k // 2, k % 2:k % 2 + 1, :] = turned[4 + k:5 + k, 0:8]


def shards(
    tokens, w_qkv, w_out, w_up, w_down, norm_gain, norm_bias, seg_start, live_count, cotangent
):
    seg = seg_start.reshape(1, rows)
    vmem = pl.BlockSpec(memory_space=pltpu.VMEM)
    smem = pl.BlockSpec(memory_space=pltpu.SMEM)
    hbm = pl.BlockSpec(memory_space=pl.ANY)
    grid = (4, 2, 2, 2, 2, 16)

    def v(shape, kind=bf16):
        return pltpu.VMEM(shape, kind)

    def s(shape, kind):
        return jax.ShapeDtypeStruct(shape, kind)

    narrow, wide = (8, 64, 128), (8, 128, 128)
    out = pl.pallas_call(
        kernel,
        out_shape=(
            s((rows, width), bf16), s((rows, width), bf16), s((2, 16, 4096), f32),
            s((8, 128), f32), s((2,) + grid + (1536,), bf16),
        ),
        in_specs=[vmem, hbm, hbm, hbm, hbm, vmem, vmem, vmem, smem, vmem],
        out_specs=(vmem, vmem, vmem, vmem, hbm),
        scratch_shapes=[
            v((2,) + grid + (4096 + ln_cols,)), v((2,) + grid + (4096,)),
            v(grid + (2560,)), v(grid + (2560,)),
            v((4, 8, 256), f32), v((4, 8, 128), f32), v((7, 8, 128), f32),
            v((2,) + narrow), v((2,) + narrow), v((2,) + narrow), v((2,) + wide),
            v((2,) + narrow), v((2,) + narrow), v((2,) + narrow), v((2,) + wide),
            v(narrow), v(narrow), v(narrow), v(wide),
            v((2, rows, 1024)), v((2, rows, 2048)), v((2, rows, 1024)), v((2, rows, 3072)),
            v((2, rows, 3072)), v((2, lead, 3072)), v((2, lead, 2048)), v((2, lead, 2048)),
            v((lead, 2048), f32), v((lead, width)), v((2, lead, width)),
            v((rows, width), f32), v((2, rows, width), f32), v((rows, width), f32), v((rows, width), f32),
            v((2, rows, 2048)), v((rows, 2048)), v((rows, width)), v((rows, width)),
            v((rows, 256), f32), v((8, width), f32), v((8, width), f32),
            pltpu.SemaphoreType.DMA((n_send,)), pltpu.SemaphoreType.DMA((6 * n_recv + n_share + n_misc + 3 * n_far,)),
            pltpu.SemaphoreType.DMA((12,)), pltpu.SemaphoreType.REGULAR,
            pltpu.SemaphoreType.REGULAR((2,)),
        ],
        name="layers",
        compiler_params=pltpu.CompilerParams(
            collective_id=0, has_side_effects=True, vmem_limit_bytes=64 * 2 ** 20
        ),
    )(tokens, w_qkv, w_out, w_up, w_down, norm_gain, norm_bias, seg, live_count, cotangent)
    act, dtok, fin, fln, _ = out
    shapes = [a.shape for a in (w_qkv, w_out, w_up, w_down, norm_gain, norm_bias)]
    return pl.pallas_call(
        results,
        out_shape=(s((rows, width), bf16), s((rows, width), bf16)) + tuple(s(a, f32) for a in shapes),
        in_specs=[vmem] * 4,
        out_specs=(vmem,) * 8,
        scratch_shapes=[v((8, 128), f32)],
        name="results",
    )(act, dtok, fin, fln)


def solution(mesh):
    return jax.shard_map(
        shards,
        mesh=mesh,
        in_specs=(
            P(("dom", "head"), None),
            P(None, ("dom", "head"), None),
            P(None, ("dom", "head"), None),
            P(None, ("dom", "head"), None),
            P(None, ("dom", "head"), None),
            P(None, None, ("dom", "head")),
            P(None, None, ("dom", "head")),
            P(("dom", "head")),
            P("dom"),
            P(("dom", "head"), None),
        ),
        out_specs=(
            P(("dom", "head"), None),
            P(("dom", "head"), None),
            P(None, ("dom", "head"), None),
            P(None, ("dom", "head"), None),
            P(None, ("dom", "head"), None),
            P(None, ("dom", "head"), None),
            P(None, None, ("dom", "head")),
            P(None, None, ("dom", "head")),
        ),
        check_vma=False,
    )
```

```python
import jax
import jax.numpy as jnp
from jax import lax
from jax.experimental import pallas as pl
from jax.experimental.pallas import tpu as pltpu
from jax.sharding import PartitionSpec as P

HEADS = 8
HEAD_DIM = 128
eps = 1e-05
neg_fill = -1000000000.0
lead = 16
rows = 128
width = 1024
n_send = 48
n_recv = 24
n_share = 40
n_far = 7
n_misc = 18

MESH = pl.DeviceIdType.MESH
bf16 = jnp.bfloat16
f32 = jnp.float32
AXES = ("x", "y", "z")

REGION = 1408
OUT, UP = 1, ((0, 0), (2, 512))
ln_cols = 128


def cols_of(layer, part, region):
    shift = ln_cols if (layer == 0 and region == 2) else 0
    base = region * REGION
    if part == "A":
        return base, 512 + shift
    if part == "B":
        return base + 512 + shift, 512
    return base + 1024 + shift, (384, 384, 256)[region]


down_at = (0, 384, 768)
down_len = (384, 384, 256)
sum_base = (0, 896, 1792)


def contract_last(a, b):
    return lax.dot_general(a, b, (((1,), (1,)), ((), ())), preferred_element_type=f32)


def contract_rows(a, b):
    return lax.dot_general(a, b, (((0,), (0,)), ((), ())), preferred_element_type=f32)


def dot(a, b):
    return jnp.dot(a, b, preferred_element_type=f32)


def kernel(
    tokens, w_qkv, w_out, w_up, w_down, norm_gain, norm_bias, seg, live_count, cot,
    act_out, dtok_out, FIN, FLN, park,
    W0, W1, DS, RS, LY, LZ, LX,
    TN, TA, TS, TF, UN, UA, US, UF, SN, SA, SS, SF,
    GRES, GHID, GBR, GQKV, QKV, LEAD, RIMS, RIMR, TAIL, XL, NL,
    X1, MID, GR, GS, GP, ACT, ATT, NRM, MASK, LNP, LNG,
    ss, rs, ls, gfree, rfree,
):
    dom = lax.axis_index("dom")
    head = lax.axis_index("head")
    me = {"y": dom // 4, "z": (head // 4) * 2 + (dom // 2) % 2, "x": head % 4, "c": dom % 2}
    core = me["c"]
    W = (W0, W1)

    def device(o):
        return (o["y"] * 4 + (o["z"] % 2) * 2 + o["c"], (o["z"] // 2) * 4 + o["x"])

    def near(axis, step):
        o = dict(me)
        o[axis] = (o[axis] + step + 4) % 4
        return device(o)

    sibling = (dom + 1 - 2 * core, head)
    after = (dom, (head + 1) % 8)
    before = (dom, (head + 7) % 8)
    neighbours = [near(a, s) for a in AXES for s in (1, -1)]

    pending = {}
    order = []
    turns = {}
    count = [0, 0]
    pools = {}
    for k, a in enumerate(AXES):
        pools[a, 1] = (2 * k * n_recv, n_recv)
        pools[a, -1] = ((2 * k + 1) * n_recv, n_recv)
        pools[a, 2] = (6 * n_recv + n_share + n_misc + k * n_far, n_far)
    pools["share"] = (6 * n_recv, n_share)
    pools["misc"] = (6 * n_recv + n_share, n_misc)

    def turn_of(way):
        k = turns.get(way, 0)
        turns[way] = k + 1
        base, size = pools[way]
        return base + k % size

    def send(src, dst, to, way, recv=None):
        k = count[0] % n_send
        count[0] += 1
        if len(order) >= n_send:
            drain([order[-n_send]])
        c = pltpu.make_async_remote_copy(
            src_ref=src, dst_ref=dst, send_sem=ss.at[k],
            recv_sem=rs.at[turn_of(way) if recv is None else recv],
            device_id=to, device_id_type=MESH,
        )
        c.start()
        pending[id(c)] = c
        order.append(c)
        return c

    def step_to(src, dst, axis, way):
        return send(src, dst, near(axis, way), (axis, way))

    def local(src, dst):
        k = count[1] % 12
        count[1] += 1
        c = pltpu.make_async_copy(src, dst, ls.at[k])
        c.start()
        return c

    def drain(copies):
        for c in copies:
            if id(c) in pending:
                c.wait_send()
                del pending[id(c)]

    def w_slab(layer, region, phase, j, a, n):
        axes = (AXES[(region + 1) % 3], AXES[(region + 2) % 3], AXES[region])
        at = dict(me)
        for k in range(phase):
            at[axes[k]] = None
        at[axes[phase]] = j
        y, z, x = at["y"], at["z"], at["x"]
        full = slice(None)
        return W[layer].at[
            core,
            full if y is None else y,
            full if z is None else z % 2,
            full if z is None else z // 2,
            full if x is None else x // 2,
            full if x is None else x % 2,
            full,
            pl.ds(a, n),
        ]

    class Gather:
        def __init__(self, layer, region, phase, a, n, share):
            self.key = (layer, region, phase)
            self.a, self.n, self.share = a, n, share
            self.axis = (AXES[(region + 1) % 3], AXES[(region + 2) % 3], AXES[region])[phase]
            self.i = me[self.axis]
            self.half = ((n // 128 + 1) // 2) * 128
            self.shares = []
            self.sent = []
            self.c2 = []

        def spread(self):
            s = self.slab(0)
            self.c1 = [step_to(s, s, self.axis, k) for k in (1, -1, 2)]

        def gathered(self):
            for c in self.c1:
                c.wait_recv()

        def slab(self, step, a=None, n=None):
            a = self.a if a is None else a
            n = self.n if n is None else n
            return w_slab(*self.key, (self.i + step + 4) % 4, a, n)

        def hand(self, step):
            if self.share:
                s = self.slab(step)
                self.shares.append(send(s, s, sibling, "share", self.share_sem))

        def s1(self):
            if self.share:
                self.share_sem = turn_of("share")
            s = self.slab(0)
            self.c1 = [step_to(s, s, self.axis, 1), step_to(s, s, self.axis, -1)]
            self.hand(0)

        def s2(self):
            lo = (self.a, self.half)
            hi = (self.a + self.half, self.n - self.half)
            self.c1[0].wait_recv()
            s = self.slab(-1, *lo)
            self.c2 = [step_to(s, s, self.axis, 1)]
            self.c1[1].wait_recv()
            s = self.slab(1, *hi)
            self.c2.append(step_to(s, s, self.axis, -1))
            self.hand(-1)
            self.hand(1)

        def s3(self):
            for c in self.c2:
                c.wait_recv()
            self.hand(2)
            self.sent = self.c1 + self.c2 + self.shares

        def ready(self):
            layer, a, n = self.key[0], self.a, self.n
            got = W[layer].at[1 - core, :, :, :, :, :, :, pl.ds(a, n)]
            pltpu.make_async_remote_copy(
                src_ref=got, dst_ref=got, send_sem=ss.at[0], recv_sem=rs.at[self.share_sem],
                device_id=sibling, device_id_type=MESH,
            ).wait_recv()

    class Many:
        def __init__(self, items):
            self.items = items

        def __getattr__(self, name):
            def call():
                for item in self.items:
                    getattr(item, name)()
            return call

    first, second, last = {}, {}, {}
    for layer in (0, 1):
        spans = []
        for region in range(3):
            c, cn = cols_of(layer, "C", region)
            spans.append((region * REGION, c + cn - region * REGION))
        first[layer] = Many([Gather(layer, r, 0, *spans[r], False) for r in range(3)])
        second[layer] = Many([Gather(layer, r, 1, *spans[r], False) for r in range(3)])
        for part in "ABC":
            last[layer, part] = Many(
                [Gather(layer, r, 2, *cols_of(layer, part, r), True) for r in range(3)]
            )

    def d_index(prefix, cols):
        full = slice(None)
        at = []
        for k in range(3):
            p = prefix[k] if k < len(prefix) else None
            if k == 0:
                at.append(full if p is None else p)
            else:
                at += [full, full] if p is None else [p // 2, p % 2]
        return tuple(at) + (full, cols)

    class Sums:
        def __init__(self, d, r, a, n):
            self.d, self.r, self.a, self.n = d, r, a, n

        def at(self, which, prefix, cols):
            ref, lead_at = which
            return ref, lead_at + d_index(prefix, cols)

        def D(self, prefix, cols):
            return self.at(self.d, prefix, cols)

        def R(self, prefix, cols):
            return self.at(self.r, prefix, cols)

    def sums_of(layer, part, region):
        if layer == 0:
            a, n = cols_of(1, part, region)
            return Sums((W1, (0,)), (W1, (1,)), a, n)
        if part == "A":
            a, _ = cols_of(0, part, region)
            return Sums((W0, (0,)), (W0, (1,)), a, 512)
        a = sum_base[region] + (0 if part == "B" else 512)
        return Sums((DS, ()), (RS, ()), a, 512 if part == "B" else down_len[region])

    def joined(layer, region):
        b, c = sums_of(layer, "B", region), sums_of(layer, "C", region)
        return Sums(b.d, b.r, b.a, b.n + c.n)

    class Reduce:
        def __init__(self, sums, region, phase, finish=None):
            self.s, self.region, self.phase, self.finish = sums, region, phase, finish
            self.axes = (AXES[region], AXES[(region + 2) % 3], AXES[(region + 1) % 3])
            self.axis = self.axes[phase]
            self.i = me[self.axis]
            self.own = tuple(me[a] for a in self.axes[:phase])
            self.slots = (3,) * phase
            n = sums.n
            half = ((n // 128 + 1) // 2) * 128
            self.lo = pl.ds(sums.a, half)
            self.hi = pl.ds(sums.a + half, n - half) if half < n else None
            self.all = pl.ds(sums.a, n)

        def d(self, step, cols):
            return self.s.D(self.own + ((self.i + step + 4) % 4,), cols)

        def r(self, slot, cols):
            return self.s.R(self.slots + (slot,), cols)

        def push(self, step, slot, cols, way):
            if cols is None:
                return None
            ref, at = self.d(step, cols)
            to, to_at = self.r(slot, cols)
            return step_to(ref.at[at], to.at[to_at], self.axis, way)

        def s1(self):
            self.c1 = self.push(2, 2, self.lo, 1)
            self.c2 = self.push(2, 2, self.hi, -1)
            self.c3 = self.push(1, 0, self.hi, 1)
            self.c4 = self.push(-1, 1, self.lo, -1)

        def spread(self):
            self.c1 = self.push(1, 0, self.all, 1)
            self.c2 = self.push(-1, 1, self.all, -1)
            self.c3 = self.push(2, 2, self.all, 2)
            self.c4 = self.c5 = self.c6 = None

        def collect(self):
            for c in (self.c1, self.c2, self.c3):
                c.wait_recv()
            self.total((0, 1, 2))

        def add_in(self, step, slot, cols):
            ref, at = self.d(step, cols)
            other, other_at = self.r(slot, cols)
            ref[at] = (ref[at].astype(f32) + other[other_at].astype(f32)).astype(bf16)

        def s2(self):
            self.c1.wait_recv()
            self.add_in(1, 2, self.lo)
            self.c5 = self.push(1, 0, self.lo, 1)
            self.c6 = None
            if self.hi is not None:
                self.c2.wait_recv()
                self.add_in(-1, 2, self.hi)
                self.c6 = self.push(-1, 1, self.hi, -1)

        def s3(self):
            for c in (self.c3, self.c4, self.c5, self.c6):
                if c is not None:
                    c.wait_recv()
            self.total((0, 1))

        def total(self, slots):
            ref, at = self.d(0, self.all)
            total = ref[at].astype(f32)
            for slot in slots:
                other, other_at = self.r(slot, self.all)
                total = total + other[other_at].astype(f32)
            if self.finish is None:
                ref[at] = total.astype(bf16)
            else:
                self.finish(total)

    def finish_at(layer, a):
        def put(total):
            FIN[layer, :, pl.ds(a, total.shape[-1])] = total
        return put

    reduce1, reduce2, reduce3 = {}, {}, {}
    for layer in (0, 1):
        for part in "ABC":
            for r in range(3):
                reduce1[layer, part, r] = Reduce(sums_of(layer, part, r), r, 0)
        reduce2[layer, "A"] = Many([Reduce(sums_of(layer, "A", r), r, 1) for r in range(3)])
        reduce3[layer, "A"] = Many([
            Reduce(sums_of(layer, "A", r), r, 2, finish_at(layer, cols_of(1, "A", r)[0])) for r in range(3)
        ])
        reduce2[layer, "BC"] = Many([Reduce(joined(layer, r), r, 1) for r in range(3)])
        reduce3[layer, "BC"] = Many([
            Reduce(joined(layer, r), r, 2, finish_at(layer, cols_of(1, "B", r)[0])) for r in range(3)
        ])

    def ln_send(src, dst, **moves):
        o = dict(me)
        for axis, step in moves.items():
            o[axis] = (o[axis] + step) % (2 if axis == "c" else 4)
        return send(src, dst, device(o), "misc")

    def ln_y():
        for k in (1, 2, 3):
            to = lax.rem(me["y"] + k, 4)
            src = LNG.at[:, pl.ds(pl.multiple_of(to * 256, 256), 256)]
            shared["ln_y", k] = ln_send(src, LY.at[k - 1], y=k)

    def ln_z():
        total = LNG[:, pl.ds(pl.multiple_of(me["y"] * 256, 256), 256)]
        for k in (1, 2, 3):
            shared["ln_y", k].wait_recv()
            total = total + LY[k - 1]
        LY[3] = total
        for k in (1, 2, 3):
            to = lax.rem(me["z"] + k, 2)
            src = LY.at[3, :, pl.ds(pl.multiple_of(to * 128, 128), 128)]
            shared["ln_z", k] = ln_send(src, LZ.at[k - 1], z=k)

    others = [(x, c) for x in range(4) for c in range(2) if x or c]

    def ln_x():
        total = LY[3, :, pl.ds(pl.multiple_of(lax.rem(me["z"], 2) * 128, 128), 128)]
        for k in (1, 2, 3):
            shared["ln_z", k].wait_recv()
            total = total + LZ[k - 1]
        LZ[3] = total
        for k, (x, c) in enumerate(others):
            shared["ln_x", k] = ln_send(LZ.at[3], LX.at[k], x=x, c=c)

    def ln_end():
        total = LZ[3]
        for k in range(7):
            shared["ln_x", k].wait_recv()
            total = total + LX[k]
        FLN[...] = total

    def many(layer, part, regions=(0, 1, 2)):
        return Many([reduce1[layer, part, r] for r in regions])

    def w_half(layer, h, a, n, ys=(0, 1, 2, 3)):
        parts = [
            W[layer][c, y, z, :, :, h, :, pl.ds(a, n)].reshape(64, n)
            for y in ys for z in (0, 1) for c in (0, 1)
        ]
        return jnp.concatenate(parts, axis=0)

    def w_down_rows(layer, a, n, ys=(0, 1, 2, 3)):
        parts = [
            W[layer][c, y, z, :, :, :, :, pl.ds(a, n)].reshape(128, n)
            for y in ys for z in (0, 1) for c in (0, 1)
        ]
        return jnp.concatenate(parts, axis=0)

    def settle(layer, part):
        drain(sum([item.sent for item in last[layer, part].items], []))
        for r in range(3):
            if part == "B" or part == "A":
                a, _ = cols_of(layer, part, r)

                @pl.loop(0, 16)
                def _(k):
                    c, y, z = k // 8, (k // 2) % 4, k % 2
                    for zh in (0, 1):
                        for xp in (0, 1):
                            even = W[layer][c, y, z, zh, xp, 0, :, pl.ds(a, 512)].astype(f32)
                            odd = W[layer][c, y, z, zh, xp, 1, :, pl.ds(a, 512)].astype(f32)
                            W[layer][c, y, z, zh, xp, 0, :, pl.ds(a, 512)] = jnp.concatenate(
                                [even[:8], odd[:8]], axis=0).astype(bf16)
                            W[layer][c, y, z, zh, xp, 1, :, pl.ds(a, 512)] = jnp.concatenate(
                                [even[8:], odd[8:]], axis=0).astype(bf16)

    block = 32

    def live_rows(r):
        place = lax.broadcasted_iota(jnp.int32, (block, 1), 0) + (head * rows + r * block)
        return (place < live_count[0]).astype(f32)

    def live_all():
        place = lax.broadcasted_iota(jnp.int32, (rows, 1), 0) + head * rows
        return (place < live_count[0]).astype(f32)

    def stats(v):
        mean = jnp.mean(v, axis=-1, keepdims=True)
        centred = v - mean
        spread = jnp.mean(centred * centred, axis=-1, keepdims=True)
        r = lax.rsqrt(spread + eps)
        return centred * r, r

    def norm(load, which, dst):
        gain = LNP[which:which + 1, :]
        shift = LNP[4 + which:5 + which, :]

        @pl.loop(0, rows // block)
        def _(r):
            at = pl.ds(pl.multiple_of(r * block, block), block)
            n, _ = stats(load(at))
            dst[at, :] = (n * gain + shift).astype(bf16)

    def norm_back(load, which, old, new, low):
        gain = LNP[which:which + 1, :]

        def step(r, carry):
            to_gain, to_shift = carry
            at = pl.ds(pl.multiple_of(r * block, block), block)
            n, scale = stats(load(at))
            gs = GS[at, :]
            e = gs * gain
            m1 = jnp.mean(e, axis=-1, keepdims=True)
            m2 = jnp.mean(e * n, axis=-1, keepdims=True)
            g = old(at) + scale * (e - m1 - n * m2)
            new(at, g)
            if low is not None:
                low[at, :] = (live_rows(r) * g).astype(bf16)
            to_gain = to_gain + jnp.sum((gs * n).reshape(block // 8, 8, width), axis=0)
            to_shift = to_shift + jnp.sum(gs.reshape(block // 8, 8, width), axis=0)
            return to_gain, to_shift

        zero = jnp.zeros((8, width), f32)
        to_gain, to_shift = lax.fori_loop(0, rows // block, step, (zero, zero))
        LNG[which:which + 1, :] = jnp.sum(to_gain, axis=0, keepdims=True)
        LNG[4 + which:5 + which, :] = jnp.sum(to_shift, axis=0, keepdims=True)

    def turn(src, keep, stage):
        for b in range(8):
            t = src[:, b * 128:(b + 1) * 128].T
            keep[b] = jnp.where(core == 0, t[:64], t[64:])
            stage[b] = jnp.where(core == 0, t[64:], t[:64])

    def turn_wide(src, keep, stage, blocks):
        for b in blocks:
            v0 = src[:, b * 256:b * 256 + 128]
            v1 = src[:, b * 256 + 128:b * 256 + 256]
            keep[b] = jnp.where(core == 0, v0, v1).T
            stage[b] = jnp.where(core == 0, v1, v0).T

    def both(keep, got):
        k, n = keep.shape[0] * keep.shape[1], keep.shape[2]
        return jnp.concatenate([keep[...].reshape(k, n), got[...].reshape(k, n)], axis=1)

    def pair(ref, a, n):
        return jnp.concatenate([ref[0, :, pl.ds(a, n)], ref[1, :, pl.ds(a, n)]], axis=0)

    def put_terms(sums, region, tile, y, z, x):
        pos = {"y": y, "z": z, "x": x}
        axes = (AXES[region], AXES[(region + 2) % 3], AXES[(region + 1) % 3])
        ref, at = sums.D(tuple(pos[a] for a in axes), pl.ds(sums.a, sums.n))
        ref[at] = tile.astype(bf16)

    def terms(layer, part, region, lhs, ref, columns):
        sums = sums_of(layer, part, region)
        if part == "C":
            value = dot(lhs, pair(ref, down_at[region], down_len[region]))
        else:
            left, right = (dot(lhs, pair(ref, columns(h), 512)) for h in (0, 1))
        for y in range(4):
            for zl in range(2):
                for zh in range(2):
                    for x in range(4):
                        k = ((y * 2 + zl) * 2 + zh) * 4 + x
                        if part == "C":
                            tile = value[k * 16:k * 16 + 16]
                        else:
                            tile = jnp.concatenate([left[k * 8:k * 8 + 8], right[k * 8:k * 8 + 8]], axis=0)
                        put_terms(sums, region, tile, y, zh * 2 + zl, x)

    scaling = HEAD_DIM ** (-0.5)

    def window(layer, h, which):
        at = pl.ds(h * 384 + which * 128, 128)
        return jnp.concatenate(
            [QKV[layer, :, at], LEAD[layer, :, at], jnp.zeros((128 - lead, 128), bf16)], axis=0
        )

    def probs(layer, h):
        q = QKV[layer, :, pl.ds(h * 384, 128)]
        k = window(layer, h, 1)
        s = contract_last(q, k) * scaling
        s = jnp.where(MASK[...] > 0, s, neg_fill)
        e = jnp.exp(s - jnp.max(s, axis=-1, keepdims=True))
        return q, k, e / jnp.sum(e, axis=-1, keepdims=True)

    def attend(layer, heads):
        for h in heads:
            _, _, p = probs(layer, h)
            ATT[:, h * 128:(h + 1) * 128] = dot(p.astype(bf16), window(layer, h, 2)).astype(bf16)

    def attend_back(layer):
        for h in range(HEADS):
            q, k, p = probs(layer, h)
            v = window(layer, h, 2)
            do = ATT[:, h * 128:(h + 1) * 128]
            gv = contract_rows(p.astype(bf16), do)
            gp = contract_last(do, v)
            gs = (p * (gp - jnp.sum(p * gp, axis=-1, keepdims=True))).astype(bf16)
            gq = dot(gs, k) * scaling
            gk = contract_rows(gs, q) * scaling
            GQKV[0, :, h * 384:h * 384 + 128] = gq.astype(bf16)
            GQKV[0, :, h * 384 + 128:h * 384 + 256] = gk[:128].astype(bf16)
            GQKV[0, :, h * 384 + 256:h * 384 + 384] = gv[:128].astype(bf16)
            TAIL[:, h * 256:h * 256 + 128] = gk[112:128]
            TAIL[:, h * 256 + 128:h * 256 + 256] = gv[112:128]
            RIMS[layer, :, h * 256:h * 256 + 128] = gk[128:144].astype(bf16)
            RIMS[layer, :, h * 256 + 128:h * 256 + 256] = gv[128:144].astype(bf16)

    def add_rim(layer):
        for h in range(HEADS):
            at = pl.ds(h * 256, 256)
            total = TAIL[:, at] + RIMR[layer, :, at].astype(f32)
            GQKV[0, 112:128, h * 384 + 128:h * 384 + 384] = total.astype(bf16)

    shared = {}

    def x_at(layer):
        if layer == 0:
            return lambda at: tokens[at, :].astype(f32)
        return lambda at: X1[at, :]

    def forward_norm(layer):
        norm(x_at(layer), 2 * layer, NRM)
        if layer == 0:
            shared["x", 0].wait_recv()
            n, _ = stats(XL[...].astype(f32))
            NL[0] = (n * LNP[0:1, :] + LNP[4:5, :]).astype(bf16)
        else:
            shared["x", 1] = send(NRM.at[pl.ds(rows - lead, lead), :], NL.at[1], after, "misc")
            drain([shared["n", 0]])
        turn(NRM, TN.at[layer], SN)
        shared["n", layer] = send(SN, UN.at[layer], sibling, "share")

    def forward_qkv(layer):
        if layer == 1:
            shared["x", 1].wait_recv()
        n = jnp.concatenate([NRM[...], NL[layer]], axis=0)
        for h in (0, 1):
            for r in range(3):
                a, _ = cols_of(layer, "A", r)
                at = pl.ds(h * 1536 + r * 512, 512)
                value = dot(n, w_half(layer, h, a, 512)).astype(bf16)
                QKV[layer, :, at] = value[:rows]
                LEAD[layer, :, at] = value[rows:]

    def forward_attend(layer):
        attend(layer, range(4, 8))
        if layer == 1:
            drain([shared["a", 0]])
        turn(ATT, TA.at[layer], SA)
        shared["a", layer] = send(SA, UA.at[layer], sibling, "share")

    def forward_up(layer):
        a_in = ATT[...]
        live = live_all()
        load = x_at(layer)
        a, _ = cols_of(layer, "B", OUT)
        for h in (0, 1):
            at = pl.ds(h * 512, 512)
            x = tokens[:, at].astype(f32) if layer == 0 else X1[:, at]
            MID[layer, :, at] = x + live * dot(a_in, w_half(layer, h, a, 512))
        if layer == 1:
            drain([shared["x", 1]])
        norm(lambda at: MID[layer, at, :], 2 * layer + 1, NRM)
        n = NRM[...]
        if layer == 1:
            drain([shared["f", 0, 0], shared["f", 0, 1]])
        for h in (0, 1):
            for r, base in UP:
                a, _ = cols_of(layer, "B", r)
                at = pl.ds(h * 1024 + base, 512)
                u = dot(n, w_half(layer, h, a, 512))
                cdf = 0.5 * (1.0 + lax.erf(u * (0.5 ** 0.5)))
                ACT[:, at] = (u * cdf).astype(bf16)
                slope = cdf + u * (jnp.exp(u * u * (-0.5)) * 0.3989422804014327)
                GP[layer, :, at] = slope.astype(bf16)
            turn_wide(ACT, TF.at[layer], SF, range(4 * h, 4 * h + 4))
            part = pl.ds(4 * h, 4)
            shared["f", layer, h] = send(SF.at[part], UF.at[layer, part], sibling, "share")
        if layer == 1:
            drain([shared["s", 0]])
        turn(NRM, TS.at[layer], SS)
        shared["s", layer] = send(SS, US.at[layer], sibling, "share")

    def forward_down(layer):
        live = live_all()
        a_in = ACT[...]
        for r in range(3):
            a, n = cols_of(layer, "C", r)
            at = pl.ds(down_at[r], n)
            v = MID[layer, :, at] + live * dot(a_in, w_down_rows(layer, a, n))
            if layer == 0:
                X1[:, at] = v
            else:
                act_out[:, at] = v.astype(bf16)

    def back_result(layer):
        if layer == 1:
            GRES[0] = (live_all() * cot[...].astype(f32)).astype(bf16)
        shared["res", layer] = send(GRES.at[0], GRES.at[1], sibling, "share")

    def terms_down(layer):
        shared["f", layer, 0].wait_recv()
        shared["f", layer, 1].wait_recv()
        shared["res", layer].wait_recv()
        lhs = both(TF.at[layer], UF.at[layer])
        for r in range(3):
            terms(layer, "C", r, lhs, GRES, None)
            reduce1[layer, "C", r].s1()

    def back_down(layer):
        g = GRES[0]
        for y in range(4):
            w = jnp.concatenate(
                [w_down_rows(layer, *cols_of(layer, "C", r), ys=(y,)) for r in range(3)], axis=1
            )
            at = pl.ds(y * 512, 512)
            GHID[0, :, at] = (contract_last(g, w) * GP[layer, :, at].astype(f32)).astype(bf16)
            if y % 2:
                part = pl.ds((y // 2) * 1024, 1024)
                shared["hid", layer, y // 2] = send(
                    GHID.at[0, :, part], GHID.at[1, :, part], sibling, "share")

    def terms_up(layer):
        shared["hid", layer, 0].wait_recv()
        shared["hid", layer, 1].wait_recv()
        shared["s", layer].wait_recv()
        lhs = both(TS.at[layer], US.at[layer])
        for r, base in UP:
            terms(layer, "B", r, lhs, GHID, lambda h, base=base: h * 1024 + base)
            reduce1[layer, "B", r].s1()

    def back_up_dot(layer):
        g = GHID[0]
        for y in range(4):
            w = jnp.concatenate(
                [w_half(layer, h, cols_of(layer, "B", r)[0], 512, ys=(y,)) for h in (0, 1) for r, _ in UP],
                axis=1,
            )
            GS[:, y * 256:(y + 1) * 256] = contract_last(g, w)

    def back_up_norm(layer):
        def old(at):
            return cot[at, :].astype(f32) if layer == 1 else GR[at, :]

        def new(at, g):
            GR[at, :] = g

        norm_back(lambda at: MID[layer, at, :], 2 * layer + 1, old, new, GBR.at[0])
        shared["br", layer] = send(GBR.at[0], GBR.at[1], sibling, "share")

    def terms_out(layer):
        shared["br", layer].wait_recv()
        shared["a", layer].wait_recv()
        terms(layer, "B", OUT, both(TA.at[layer], UA.at[layer]), GBR, lambda h: h * 512)
        reduce1[layer, "B", OUT].s1()

    def back_out(layer):
        g = GBR[0]
        for y in range(4):
            w = jnp.concatenate(
                [w_half(layer, h, cols_of(layer, "B", OUT)[0], 512, ys=(y,)) for h in (0, 1)], axis=1
            )
            ATT[:, y * 256:(y + 1) * 256] = contract_last(g, w).astype(bf16)

    def back_attend(layer):
        attend_back(layer)
        shared["back", layer] = send(RIMS.at[layer], RIMR.at[layer], before, "misc")
        part = pl.ds(0, rows - lead)
        shared["qkv", layer, 0] = send(GQKV.at[0, part], GQKV.at[1, part], sibling, "share")

    def back_rim(layer):
        shared["back", layer].wait_recv()
        add_rim(layer)
        part = pl.ds(rows - lead, lead)
        shared["qkv", layer, 1] = send(GQKV.at[0, part], GQKV.at[1, part], sibling, "share")

    def terms_qkv(layer):
        shared["qkv", layer, 0].wait_recv()
        shared["qkv", layer, 1].wait_recv()
        shared["n", layer].wait_recv()
        lhs = both(TN.at[layer], UN.at[layer])
        for r in range(3):
            terms(layer, "A", r, lhs, GQKV, lambda h, r=r: h * 1536 + r * 512)
            reduce1[layer, "A", r].s1()

    def w_qkv_back(layer, h, r, y):
        if layer == 1:
            return w_half(1, h, cols_of(1, "A", r)[0], 512, ys=(y,))
        parts = [
            ref[y, z, :, :, h, :, pl.ds(r * 512, 512)].reshape(64, 512)
            for z in (0, 1) for ref in (DS, RS)
        ]
        return jnp.concatenate(parts, axis=0)

    def back_qkv_dot(layer):
        g = GQKV[0]
        for y in range(4):
            w = jnp.concatenate([w_qkv_back(layer, h, r, y) for h in (0, 1) for r in range(3)], axis=1)
            GS[:, y * 256:(y + 1) * 256] = contract_last(g, w)

    def back_qkv_norm(layer):
        def old(at):
            return GR[at, :]

        if layer == 1:
            drain([shared["res", 1]])

            def new(at, g):
                GR[at, :] = g

            norm_back(x_at(1), 2, old, new, GRES.at[0])
        else:
            def new(at, g):
                dtok_out[at, :] = g.astype(bf16)

            norm_back(x_at(0), 0, old, new, None)

    stage = [
        local(w_qkv, FIN.at[:, 0:8, 0:3072]),
        local(w_out, FIN.at[:, 0:8, 3072:4096]),
        local(w_up, FIN.at[:, 8:16, 0:2048]),
        local(w_down.at[:, 0:8], FIN.at[:, 8:16, 2048:3072]),
        local(w_down.at[:, 8:16], FIN.at[:, 8:16, 3072:4096]),
    ]
    greeted = neighbours + [sibling, after, before] + [near(a, 2) for a in AXES]
    greeted += [device({**me, "x": (me["x"] + k) % 4, "c": 1 - core}) for k in (1, 2, 3)]
    barrier = pltpu.get_barrier_semaphore()
    for d in greeted:
        pl.semaphore_signal(barrier, inc=1, device_id=d, device_id_type=MESH)
    for c in stage:
        c.wait()
    mine = (core, me["y"], me["z"] % 2, me["z"] // 2, me["x"] // 2, me["x"] % 2)

    place = (dom * 8 + head) % 16

    def ln_tile():
        LNG[...] = jnp.zeros((8, width), f32)
        for k in range(4):
            LNG[k:k + 1, 0:8] = norm_gain[k // 2, k % 2:k % 2 + 1, :]
            LNG[4 + k:5 + k, 0:8] = norm_bias[k // 2, k % 2:k % 2 + 1, :]
        moved = pltpu.roll(LNG[:, 0:128], place * 8, 1)
        return jnp.concatenate([moved, jnp.zeros((8, 128), f32)], axis=0)

    def pack(layer, a, value):
        W[layer][mine + (slice(None), pl.ds(a, value.shape[-1]))] = value.astype(bf16)

    def halves(layer, top, base, n, at):
        return jnp.concatenate(
            [FIN[layer, top:top + 8, pl.ds(base + h * n + at, 512)] for h in (0, 1)], axis=0
        )

    for layer in (0, 1):
        for r in range(3):
            a, n = cols_of(layer, "C", r)
            pack(layer, a, jnp.concatenate(
                [FIN[layer, 8:16, pl.ds(2048 + k * 1024 + down_at[r], n)] for k in (0, 1)], axis=0
            ))
            pack(layer, cols_of(layer, "A", r)[0], halves(layer, 0, 0, 1536, r * 512))
        pack(layer, cols_of(layer, "B", OUT)[0], halves(layer, 0, 3072, 512, 0))
        for r, at in UP:
            pack(layer, cols_of(layer, "B", r)[0], halves(layer, 8, 0, 1024, at))
    pack(0, cols_of(0, "A", 2)[0] + 512, ln_tile())
    pl.semaphore_wait(barrier, len(greeted))
    first[0].spread()
    shared["x", 0] = send(tokens.at[pl.ds(rows - lead, lead), :], XL, after, "misc")
    first[1].spread()

    first[0].items[1].gathered()
    second[0].items[1].s1()
    first[0].items[0].gathered()
    second[0].items[0].s1()
    back_result(1)
    q_pos = head * rows + lax.broadcasted_iota(jnp.int32, (rows, 256), 0)
    col = lax.broadcasted_iota(jnp.int32, (rows, 256), 1)
    first[0].items[2].gathered()
    second[0].items[2].s1()
    first[1].items[1].gathered()
    first[1].items[0].gathered()
    first[1].items[2].gathered()
    second[1].items[2].s1()
    second[1].items[1].s1()
    second[1].items[0].s1()
    second[0].items[0].s2()
    second[0].items[2].s2()
    k_pos = jnp.where(col < rows, col, jnp.where(col < rows + lead, col - rows - lead, -rows * 16))
    second[0].items[1].s2()
    second[1].items[0].s2()
    k_pos = k_pos + head * rows
    second[1].items[2].s2()
    second[1].items[1].s2()
    second[0].items[2].s3()
    second[0].items[1].s3()
    last[0, "B"].items[1].s1()
    begins = jnp.broadcast_to(seg[...].astype(f32), (rows, rows)).T
    begins = jnp.concatenate([begins, begins], axis=1)
    second[0].items[0].s3()
    last[0, "A"].items[2].s1()
    last[0, "A"].items[1].s1()
    last[0, "A"].items[0].s1()
    last[0, "B"].items[2].s1()
    second[1].items[2].s3()
    last[0, "B"].items[0].s1()
    last[0, "A"].items[0].s2()
    second[1].items[1].s3()
    last[1, "A"].items[1].s1()
    last[0, "C"].items[1].s1()
    last[0, "C"].items[2].s1()
    MASK[...] = ((k_pos.astype(f32) >= begins) & (k_pos <= q_pos)).astype(f32)

    last[0, "A"].items[2].s2()
    last[0, "A"].items[1].s2()
    last[1, "A"].items[2].s1()
    second[1].items[0].s3()
    last[0, "B"].items[0].s2()
    last[1, "A"].items[0].s1()
    last[0, "C"].items[0].s1()
    last[0, "C"].items[2].s2()
    last[0, "B"].items[2].s2()
    last[0, "B"].items[1].s2()
    last[0, "C"].items[1].s2()
    last[1, "A"].items[0].s2()
    last[0, "A"].items[0].s3()
    last[0, "A"].items[1].s3()
    last[0, "A"].items[2].s3()
    last[1, "A"].items[2].s2()
    last[0, "A"].ready()
    for item in first[0].items + second[0].items:
        drain(item.c1 + item.c2)
    settle(0, "A")

    last[0, "B"].items[1].s3()
    ln_at = pl.ds(cols_of(0, "A", 2)[0] + 512, ln_cols)
    last[1, "B"].items[1].s1()
    last[0, "C"].items[0].s2()
    last[1, "B"].items[0].s1()
    for y in range(4):
        for z in range(2):
            total = jnp.zeros((16, ln_cols), f32)
            for c in (0, 1):
                total = total + jnp.sum(
                    W0[c, y, z, :, :, :, :, ln_at].reshape(8, 16, ln_cols).astype(f32), axis=0
                )
            b = y * 2 + z
            LNP[:, b * 128:(b + 1) * 128] = total[:8]

    forward_norm(0)
    forward_qkv(0)
    last[1, "C"].items[0].s1()
    attend(0, range(4))
    last[0, "B"].items[2].s3()
    last[0, "B"].items[0].s3()
    last[1, "B"].items[2].s1()
    last[0, "C"].items[2].s3()
    last[1, "A"].items[1].s2()
    last[0, "C"].items[1].s3()
    forward_attend(0)
    last[1, "A"].items[0].s3()
    last[1, "A"].items[2].s3()
    last[0, "C"].items[0].s3()
    last[0, "B"].ready()
    last[1, "C"].items[2].s1()
    settle(0, "B")
    forward_up(0)
    last[1, "B"].items[1].s2()
    last[0, "C"].ready()
    forward_down(0)
    forward_norm(1)
    last[1, "A"].items[1].s3()
    a_cols = [pl.ds(cols_of(0, "A", r)[0], 512) for r in range(3)]
    last[1, "C"].items[1].s1()
    last[1, "B"].items[0].s2()
    last[1, "B"].items[2].s2()

    everything = (slice(None),) * 7
    last[1, "B"].items[1].s3()
    parked = [
        local(W0.at[everything + (a_cols[r],)], park.at[everything + (pl.ds(r * 512, 512),)])
        for r in range(3)
    ]
    last[1, "C"].items[2].s2()
    last[1, "A"].ready()
    for item in first[1].items + second[1].items:
        drain(item.c1 + item.c2)
    settle(1, "A")
    forward_qkv(1)
    last[1, "C"].items[0].s2()
    attend(1, range(4))
    last[1, "B"].items[2].s3()
    last[1, "B"].items[0].s3()
    last[1, "C"].items[1].s2()
    forward_attend(1)
    last[1, "B"].ready()
    settle(1, "B")
    last[1, "C"].items[2].s3()
    forward_up(1)
    last[1, "C"].items[0].s3()
    for c in parked:
        c.wait()
    for d in neighbours:
        pl.semaphore_signal(rfree.at[1], inc=1, device_id=d, device_id_type=MESH)

    last[1, "C"].items[1].s3()
    terms_down(1)
    last[1, "C"].ready()
    back_down(1)
    back_up_dot(1)
    terms_up(1)
    back_up_norm(1)
    reduce1[1, "C", 1].s2()
    back_out(1)
    terms_out(1)
    back_attend(1)
    reduce1[1, "C", 0].s2()
    reduce1[1, "B", 1].s2()
    reduce1[1, "B", 2].s2()
    reduce1[1, "B", 0].s2()
    reduce1[1, "C", 2].s2()
    back_rim(1)
    back_qkv_dot(1)
    pl.semaphore_wait(rfree.at[1], 6)
    terms_qkv(1)
    back_qkv_norm(1)
    forward_down(1)

    drain(sum([item.sent for item in last[1, "C"].items], []))
    reduce1[1, "C", 2].s3()
    for d in neighbours:
        pl.semaphore_signal(rfree.at[0], inc=1, device_id=d, device_id_type=MESH)
    drain([shared[k, 1, h] for k in ("hid", "qkv") for h in (0, 1)] + [shared["br", 1]])
    pl.semaphore_signal(gfree, inc=1, device_id=sibling, device_id_type=MESH)

    pl.semaphore_wait(gfree, 1)
    reduce1[1, "B", 2].s3()
    reduce1[1, "C", 0].s3()
    reduce1[1, "A", 1].s2()
    back_result(0)
    reduce1[1, "B", 0].s3()
    reduce1[1, "C", 1].s3()
    reduce1[1, "B", 1].s3()
    reduce2[1, "BC"].items[1].s1()
    reduce1[1, "A", 0].s2()
    reduce2[1, "BC"].items[0].s1()
    back_down(0)
    pl.semaphore_wait(rfree.at[0], 6)
    reduce2[1, "BC"].items[2].s1()
    terms_down(0)
    reduce2[1, "BC"].items[1].s2()
    reduce2[1, "BC"].items[0].s2()
    back_up_dot(0)
    terms_up(0)
    back_up_norm(0)
    reduce1[1, "A", 1].s3()
    reduce1[1, "A", 2].s2()
    back_out(0)
    terms_out(0)
    back_attend(0)
    reduce2[1, "BC"].items[2].s2()
    reduce2[1, "BC"].items[1].s3()
    reduce3[1, "BC"].items[1].spread()
    reduce1[0, "C", 0].s2()
    reduce1[0, "C", 1].s2()
    reduce1[0, "B", 0].s2()
    reduce1[0, "B", 2].s2()
    reduce2[1, "BC"].items[0].s3()
    reduce3[1, "BC"].items[0].spread()
    reduce2[1, "BC"].items[2].s3()
    reduce3[1, "BC"].items[2].spread()
    reduce1[0, "C", 2].s2()
    reduce3[1, "BC"].items[1].collect()
    reduce1[1, "A", 0].s3()
    reduce2[1, "A"].items[0].s1()
    back_rim(0)
    reduce1[0, "B", 1].s2()
    terms_qkv(0)
    reduce3[1, "BC"].items[2].collect()
    reduce1[0, "B", 2].s3()
    reduce1[0, "B", 1].s3()
    reduce1[0, "A", 2].s2()
    reduce3[1, "BC"].items[0].collect()
    reduce1[1, "A", 2].s3()
    for item in sum((many(1, p).items for p in "BC"), []) + reduce2[1, "BC"].items + reduce3[1, "BC"].items:
        drain([c for c in (item.c1, item.c2, item.c3, item.c4, item.c5, item.c6) if c is not None])
    reduce1[0, "A", 0].s2()
    everything = (slice(None),) * 6
    reduce1[0, "C", 0].s3()
    reduce1[0, "A", 1].s2()
    reduce1[0, "B", 0].s3()
    reduce1[0, "C", 2].s3()
    restored = [
        local(park.at[0], DS.at[everything + (pl.ds(0, 1536),)]),
        local(park.at[1], RS.at[everything + (pl.ds(0, 1536),)]),
    ]
    reduce2[1, "A"].items[1].s1()
    reduce2[0, "BC"].items[2].s1()
    reduce1[0, "C", 1].s3()
    for c in restored:
        c.wait()
    reduce2[1, "A"].items[0].s2()
    reduce2[0, "BC"].items[0].s1()
    back_qkv_dot(0)
    back_qkv_norm(0)
    ln_y()
    reduce2[0, "BC"].items[1].s1()
    reduce2[1, "A"].items[2].s1()
    reduce1[0, "A", 2].s3()
    reduce2[1, "A"].items[1].s2()
    reduce2[0, "A"].items[2].spread()
    reduce2[1, "A"].items[0].s3()
    reduce1[0, "A", 0].s3()
    reduce2[0, "A"].items[0].spread()
    reduce2[0, "BC"].items[0].s2()
    reduce2[0, "BC"].items[2].s2()
    ln_z()
    reduce1[0, "A", 1].s3()
    reduce2[0, "A"].items[1].spread()
    reduce3[1, "A"].items[0].spread()
    reduce2[1, "A"].items[2].s2()
    reduce2[0, "BC"].items[1].s2()
    reduce2[0, "A"].items[0].collect()
    reduce3[0, "A"].items[0].spread()
    ln_x()
    reduce2[1, "A"].items[1].s3()
    reduce2[0, "BC"].items[0].s3()
    reduce3[0, "BC"].items[0].spread()
    reduce3[1, "A"].items[1].spread()
    reduce2[0, "BC"].items[2].s3()
    reduce3[0, "BC"].items[2].spread()
    reduce2[0, "A"].items[2].collect()
    reduce3[0, "A"].items[2].spread()
    reduce2[0, "A"].items[1].collect()
    reduce3[0, "A"].items[1].spread()
    reduce2[0, "BC"].items[1].s3()
    reduce2[1, "A"].items[2].s3()
    reduce3[0, "BC"].items[1].spread()
    reduce3[1, "A"].items[2].spread()
    reduce3[0, "BC"].items[2].collect()
    reduce3[1, "A"].items[0].collect()
    reduce3[1, "A"].items[1].collect()
    reduce3[0, "A"].items[0].collect()
    reduce3[0, "BC"].items[0].collect()
    reduce3[0, "A"].items[1].collect()
    reduce3[0, "A"].items[2].collect()
    ln_end()
    reduce3[1, "A"].items[2].collect()
    reduce3[0, "BC"].items[1].collect()
    drain(list(pending.values()))


def results(act, dtok, fin, fln, act_out, dtok_out, d_qkv, d_out, d_up, d_down, d_gain, d_bias, turned):
    dom = lax.axis_index("dom")
    head = lax.axis_index("head")
    act_out[...] = act[...]
    dtok_out[...] = dtok[...]

    def put(dst, a, n, total, base):
        dst[:, :, pl.ds(base, n)] = fin[:, 0:8, pl.ds(a, n)]
        dst[:, :, pl.ds(total + base, n)] = fin[:, 8:16, pl.ds(a, n)]

    for r in range(3):
        put(d_qkv, cols_of(1, "A", r)[0], 512, 1536, r * 512)
        a, n = cols_of(1, "C", r)
        d_down[:, :, pl.ds(down_at[r], n)] = fin[:, :, pl.ds(a, n)]
    put(d_out, cols_of(1, "B", OUT)[0], 512, 512, 0)
    for r, at in UP:
        put(d_up, cols_of(1, "B", r)[0], 512, 1024, at)
    place = (dom * 8 + head) % 16
    turned[...] = pltpu.roll(fln[...], (128 - place * 8) % 128, 1)
    for k in range(4):
        d_gain[k // 2, k % 2:k % 2 + 1, :] = turned[k:k + 1, 0:8]
        d_bias[k // 2, k % 2:k % 2 + 1, :] = turned[4 + k:5 + k, 0:8]


def shards(
    tokens, w_qkv, w_out, w_up, w_down, norm_gain, norm_bias, seg_start, live_count, cotangent
):
    seg = seg_start.reshape(1, rows)
    vmem = pl.BlockSpec(memory_space=pltpu.VMEM)
    smem = pl.BlockSpec(memory_space=pltpu.SMEM)
    hbm = pl.BlockSpec(memory_space=pl.ANY)
    grid = (4, 2, 2, 2, 2, 16)

    def v(shape, kind=bf16):
        return pltpu.VMEM(shape, kind)

    def s(shape, kind):
        return jax.ShapeDtypeStruct(shape, kind)

    narrow, wide = (8, 64, 128), (8, 128, 128)
    out = pl.pallas_call(
        kernel,
        out_shape=(
            s((rows, width), bf16), s((rows, width), bf16), s((2, 16, 4096), f32),
            s((8, 128), f32), s((2,) + grid + (1536,), bf16),
        ),
        in_specs=[vmem, hbm, hbm, hbm, hbm, vmem, vmem, vmem, smem, vmem],
        out_specs=(vmem, vmem, vmem, vmem, hbm),
        scratch_shapes=[
            v((2,) + grid + (4096 + ln_cols,)), v((2,) + grid + (4096,)),
            v(grid + (2560,)), v(grid + (2560,)),
            v((4, 8, 256), f32), v((4, 8, 128), f32), v((7, 8, 128), f32),
            v((2,) + narrow), v((2,) + narrow), v((2,) + narrow), v((2,) + wide),
            v((2,) + narrow), v((2,) + narrow), v((2,) + narrow), v((2,) + wide),
            v(narrow), v(narrow), v(narrow), v(wide),
            v((2, rows, 1024)), v((2, rows, 2048)), v((2, rows, 1024)), v((2, rows, 3072)),
            v((2, rows, 3072)), v((2, lead, 3072)), v((2, lead, 2048)), v((2, lead, 2048)),
            v((lead, 2048), f32), v((lead, width)), v((2, lead, width)),
            v((rows, width), f32), v((2, rows, width), f32), v((rows, width), f32), v((rows, width), f32),
            v((2, rows, 2048)), v((rows, 2048)), v((rows, width)), v((rows, width)),
            v((rows, 256), f32), v((8, width), f32), v((8, width), f32),
            pltpu.SemaphoreType.DMA((n_send,)), pltpu.SemaphoreType.DMA((6 * n_recv + n_share + n_misc + 3 * n_far,)),
            pltpu.SemaphoreType.DMA((12,)), pltpu.SemaphoreType.REGULAR,
            pltpu.SemaphoreType.REGULAR((2,)),
        ],
        name="layers",
        compiler_params=pltpu.CompilerParams(
            collective_id=0, has_side_effects=True, vmem_limit_bytes=64 * 2 ** 20
        ),
    )(tokens, w_qkv, w_out, w_up, w_down, norm_gain, norm_bias, seg, live_count, cotangent)
    act, dtok, fin, fln, _ = out
    shapes = [a.shape for a in (w_qkv, w_out, w_up, w_down, norm_gain, norm_bias)]
    return pl.pallas_call(
        results,
        out_shape=(s((rows, width), bf16), s((rows, width), bf16)) + tuple(s(a, f32) for a in shapes),
        in_specs=[vmem] * 4,
        out_specs=(vmem,) * 8,
        scratch_shapes=[v((8, 128), f32)],
        name="results",
    )(act, dtok, fin, fln)


def solution(mesh):
    return jax.shard_map(
        shards,
        mesh=mesh,
        in_specs=(
            P(("dom", "head"), None),
            P(None, ("dom", "head"), None),
            P(None, ("dom", "head"), None),
            P(None, ("dom", "head"), None),
            P(None, ("dom", "head"), None),
            P(None, None, ("dom", "head")),
            P(None, None, ("dom", "head")),
            P(("dom", "head")),
            P("dom"),
            P(("dom", "head"), None),
        ),
        out_specs=(
            P(("dom", "head"), None),
            P(("dom", "head"), None),
            P(None, ("dom", "head"), None),
            P(None, ("dom", "head"), None),
            P(None, ("dom", "head"), None),
            P(None, ("dom", "head"), None),
            P(None, None, ("dom", "head")),
            P(None, None, ("dom", "head")),
        ),
        check_vma=False,
    )
```

```python
import jax
import jax.numpy as jnp
from jax import lax
from jax.experimental import pallas as pl
from jax.experimental.pallas import tpu as pltpu
from jax.sharding import PartitionSpec as P

HEADS = 8
HEAD_DIM = 128
eps = 1e-05
neg_fill = -1000000000.0
lead = 16
rows = 128
width = 1024
n_send = 48
n_recv = 26
n_share = 40
n_far = 7
n_misc = 18

MESH = pl.DeviceIdType.MESH
bf16 = jnp.bfloat16
f32 = jnp.float32
AXES = ("x", "y", "z")

REGION = 1408
OUT, UP = 1, ((0, 0), (2, 512))
ln_cols = 128


def cols_of(layer, part, region):
    shift = ln_cols if (layer == 0 and region == 2) else 0
    base = region * REGION
    if part == "A":
        return base, 512 + shift
    if part == "B":
        return base + 512 + shift, 512
    return base + 1024 + shift, (384, 384, 256)[region]


down_at = (0, 384, 768)
down_len = (384, 384, 256)
sum_base = (0, 896, 1792)


def contract_last(a, b):
    return lax.dot_general(a, b, (((1,), (1,)), ((), ())), preferred_element_type=f32)


def contract_rows(a, b):
    return lax.dot_general(a, b, (((0,), (0,)), ((), ())), preferred_element_type=f32)


def dot(a, b):
    return jnp.dot(a, b, preferred_element_type=f32)


def kernel(
    tokens, w_qkv, w_out, w_up, w_down, norm_gain, norm_bias, seg, live_count, cot,
    act_out, dtok_out, FIN, FLN, park,
    W0, W1, DS, RS, LY, LZ, LX,
    TN, TA, TS, TF, UN, UA, US, UF, SN, SA, SS, SF,
    GRES, GHID, GBR, GQKV, QKV, LEAD, RIMS, RIMR, TAIL, XL, NL,
    X1, MID, GR, GS, GP, ACT, ATT, NRM, MASK, LNP, LNG,
    ss, rs, ls, gfree, rfree,
):
    dom = lax.axis_index("dom")
    head = lax.axis_index("head")
    me = {"y": dom // 4, "z": (head // 4) * 2 + (dom // 2) % 2, "x": head % 4, "c": dom % 2}
    core = me["c"]
    W = (W0, W1)

    def device(o):
        return (o["y"] * 4 + (o["z"] % 2) * 2 + o["c"], (o["z"] // 2) * 4 + o["x"])

    def near(axis, step):
        o = dict(me)
        o[axis] = (o[axis] + step + 4) % 4
        return device(o)

    sibling = (dom + 1 - 2 * core, head)
    after = (dom, (head + 1) % 8)
    before = (dom, (head + 7) % 8)
    neighbours = [near(a, s) for a in AXES for s in (1, -1)]

    pending = {}
    order = []
    turns = {}
    count = [0, 0]
    pools = {}
    for k, a in enumerate(AXES):
        pools[a, 1] = (2 * k * n_recv, n_recv)
        pools[a, -1] = ((2 * k + 1) * n_recv, n_recv)
        pools[a, 2] = (6 * n_recv + n_share + n_misc + k * n_far, n_far)
    pools["share"] = (6 * n_recv, n_share)
    pools["misc"] = (6 * n_recv + n_share, n_misc)

    def turn_of(way):
        k = turns.get(way, 0)
        turns[way] = k + 1
        base, size = pools[way]
        return base + k % size

    def send(src, dst, to, way, recv=None):
        k = count[0] % n_send
        count[0] += 1
        if len(order) >= n_send:
            drain([order[-n_send]])
        c = pltpu.make_async_remote_copy(
            src_ref=src, dst_ref=dst, send_sem=ss.at[k],
            recv_sem=rs.at[turn_of(way) if recv is None else recv],
            device_id=to, device_id_type=MESH,
        )
        c.start()
        pending[id(c)] = c
        order.append(c)
        return c

    def step_to(src, dst, axis, way):
        return send(src, dst, near(axis, way), (axis, way))

    def local(src, dst):
        k = count[1] % 12
        count[1] += 1
        c = pltpu.make_async_copy(src, dst, ls.at[k])
        c.start()
        return c

    def drain(copies):
        for c in copies:
            if id(c) in pending:
                c.wait_send()
                del pending[id(c)]

    def w_slab(layer, region, phase, j, a, n):
        axes = (AXES[(region + 1) % 3], AXES[(region + 2) % 3], AXES[region])
        at = dict(me)
        for k in range(phase):
            at[axes[k]] = None
        at[axes[phase]] = j
        y, z, x = at["y"], at["z"], at["x"]
        full = slice(None)
        return W[layer].at[
            core,
            full if y is None else y,
            full if z is None else z % 2,
            full if z is None else z // 2,
            full if x is None else x // 2,
            full if x is None else x % 2,
            full,
            pl.ds(a, n),
        ]

    class Gather:
        def __init__(self, layer, region, phase, a, n, share):
            self.key = (layer, region, phase)
            self.a, self.n, self.share = a, n, share
            self.axis = (AXES[(region + 1) % 3], AXES[(region + 2) % 3], AXES[region])[phase]
            self.i = me[self.axis]
            self.half = ((n // 128 + 1) // 2) * 128
            self.shares = []
            self.sent = []
            self.c2 = []

        def spread(self):
            s = self.slab(0)
            self.c1 = [step_to(s, s, self.axis, k) for k in (1, -1, 2)]

        def gathered(self):
            for c in self.c1:
                c.wait_recv()

        def slab(self, step, a=None, n=None):
            a = self.a if a is None else a
            n = self.n if n is None else n
            return w_slab(*self.key, (self.i + step + 4) % 4, a, n)

        def hand(self, step):
            if self.share:
                s = self.slab(step)
                self.shares.append(send(s, s, sibling, "share", self.share_sem))

        def s1(self):
            if self.share:
                self.share_sem = turn_of("share")
            s = self.slab(0)
            self.c1 = [step_to(s, s, self.axis, 1), step_to(s, s, self.axis, -1)]
            self.hand(0)

        def s2(self):
            lo = (self.a, self.half)
            hi = (self.a + self.half, self.n - self.half)
            self.c1[0].wait_recv()
            s = self.slab(-1, *lo)
            self.c2 = [step_to(s, s, self.axis, 1)]
            self.c1[1].wait_recv()
            s = self.slab(1, *hi)
            self.c2.append(step_to(s, s, self.axis, -1))
            self.hand(-1)
            self.hand(1)

        def s3(self):
            for c in self.c2:
                c.wait_recv()
            self.hand(2)
            self.sent = self.c1 + self.c2 + self.shares

        def ready(self):
            layer, a, n = self.key[0], self.a, self.n
            got = W[layer].at[1 - core, :, :, :, :, :, :, pl.ds(a, n)]
            pltpu.make_async_remote_copy(
                src_ref=got, dst_ref=got, send_sem=ss.at[0], recv_sem=rs.at[self.share_sem],
                device_id=sibling, device_id_type=MESH,
            ).wait_recv()

    class Many:
        def __init__(self, items):
            self.items = items

        def __getattr__(self, name):
            def call():
                for item in self.items:
                    getattr(item, name)()
            return call

    first, second, last = {}, {}, {}
    for layer in (0, 1):
        spans = []
        for region in range(3):
            c, cn = cols_of(layer, "C", region)
            spans.append((region * REGION, c + cn - region * REGION))
        first[layer] = Many([Gather(layer, r, 0, *spans[r], False) for r in range(3)])
        second[layer] = Many([Gather(layer, r, 1, *spans[r], False) for r in range(3)])
        for part in "ABC":
            last[layer, part] = Many(
                [Gather(layer, r, 2, *cols_of(layer, part, r), True) for r in range(3)]
            )

    def d_index(prefix, cols):
        full = slice(None)
        at = []
        for k in range(3):
            p = prefix[k] if k < len(prefix) else None
            if k == 0:
                at.append(full if p is None else p)
            else:
                at += [full, full] if p is None else [p // 2, p % 2]
        return tuple(at) + (full, cols)

    class Sums:
        def __init__(self, d, r, a, n):
            self.d, self.r, self.a, self.n = d, r, a, n

        def at(self, which, prefix, cols):
            ref, lead_at = which
            return ref, lead_at + d_index(prefix, cols)

        def D(self, prefix, cols):
            return self.at(self.d, prefix, cols)

        def R(self, prefix, cols):
            return self.at(self.r, prefix, cols)

    def sums_of(layer, part, region):
        if layer == 0:
            a, n = cols_of(1, part, region)
            return Sums((W1, (0,)), (W1, (1,)), a, n)
        if part == "A":
            a, _ = cols_of(0, part, region)
            return Sums((W0, (0,)), (W0, (1,)), a, 512)
        a = sum_base[region] + (0 if part == "B" else 512)
        return Sums((DS, ()), (RS, ()), a, 512 if part == "B" else down_len[region])

    def joined(layer, region):
        b, c = sums_of(layer, "B", region), sums_of(layer, "C", region)
        return Sums(b.d, b.r, b.a, b.n + c.n)

    class Reduce:
        def __init__(self, sums, region, phase, finish=None):
            self.s, self.region, self.phase, self.finish = sums, region, phase, finish
            self.axes = (AXES[region], AXES[(region + 2) % 3], AXES[(region + 1) % 3])
            self.axis = self.axes[phase]
            self.i = me[self.axis]
            self.own = tuple(me[a] for a in self.axes[:phase])
            self.slots = (3,) * phase
            n = sums.n
            half = ((n // 128 + 1) // 2) * 128
            self.lo = pl.ds(sums.a, half)
            self.hi = pl.ds(sums.a + half, n - half) if half < n else None
            self.all = pl.ds(sums.a, n)

        def d(self, step, cols):
            return self.s.D(self.own + ((self.i + step + 4) % 4,), cols)

        def r(self, slot, cols):
            return self.s.R(self.slots + (slot,), cols)

        def push(self, step, slot, cols, way):
            if cols is None:
                return None
            ref, at = self.d(step, cols)
            to, to_at = self.r(slot, cols)
            return step_to(ref.at[at], to.at[to_at], self.axis, way)

        def s1(self):
            self.c1 = self.push(2, 2, self.lo, 1)
            self.c2 = self.push(2, 2, self.hi, -1)
            self.c3 = self.push(1, 0, self.hi, 1)
            self.c4 = self.push(-1, 1, self.lo, -1)

        def spread(self):
            self.c1 = self.push(1, 0, self.all, 1)
            self.c2 = self.push(-1, 1, self.all, -1)
            self.c3 = self.push(2, 2, self.all, 2)
            self.c4 = self.c5 = self.c6 = None

        def collect(self):
            for c in (self.c1, self.c2, self.c3):
                c.wait_recv()
            self.total((0, 1, 2))

        def add_in(self, step, slot, cols):
            ref, at = self.d(step, cols)
            other, other_at = self.r(slot, cols)
            ref[at] = (ref[at].astype(f32) + other[other_at].astype(f32)).astype(bf16)

        def s2(self):
            self.c1.wait_recv()
            self.add_in(1, 2, self.lo)
            self.c5 = self.push(1, 0, self.lo, 1)
            self.c6 = None
            if self.hi is not None:
                self.c2.wait_recv()
                self.add_in(-1, 2, self.hi)
                self.c6 = self.push(-1, 1, self.hi, -1)

        def s3(self):
            for c in (self.c3, self.c4, self.c5, self.c6):
                if c is not None:
                    c.wait_recv()
            self.total((0, 1))

        def total(self, slots):
            ref, at = self.d(0, self.all)
            total = ref[at].astype(f32)
            for slot in slots:
                other, other_at = self.r(slot, self.all)
                total = total + other[other_at].astype(f32)
            if self.finish is None:
                ref[at] = total.astype(bf16)
            else:
                self.finish(total)

    def finish_at(layer, a):
        def put(total):
            FIN[layer, :, pl.ds(a, total.shape[-1])] = total
        return put

    reduce1, reduce2, reduce3 = {}, {}, {}
    for layer in (0, 1):
        for part in "ABC":
            for r in range(3):
                reduce1[layer, part, r] = Reduce(sums_of(layer, part, r), r, 0)
        reduce2[layer, "A"] = Many([Reduce(sums_of(layer, "A", r), r, 1) for r in range(3)])
        reduce3[layer, "A"] = Many([
            Reduce(sums_of(layer, "A", r), r, 2, finish_at(layer, cols_of(1, "A", r)[0])) for r in range(3)
        ])
        reduce2[layer, "BC"] = Many([Reduce(joined(layer, r), r, 1) for r in range(3)])
        reduce3[layer, "BC"] = Many([
            Reduce(joined(layer, r), r, 2, finish_at(layer, cols_of(1, "B", r)[0])) for r in range(3)
        ])

    def ln_send(src, dst, **moves):
        o = dict(me)
        for axis, step in moves.items():
            o[axis] = (o[axis] + step) % (2 if axis == "c" else 4)
        return send(src, dst, device(o), "misc")

    def ln_y():
        for k in (1, 2, 3):
            to = lax.rem(me["y"] + k, 4)
            src = LNG.at[:, pl.ds(pl.multiple_of(to * 256, 256), 256)]
            shared["ln_y", k] = ln_send(src, LY.at[k - 1], y=k)

    def ln_z():
        total = LNG[:, pl.ds(pl.multiple_of(me["y"] * 256, 256), 256)]
        for k in (1, 2, 3):
            shared["ln_y", k].wait_recv()
            total = total + LY[k - 1]
        LY[3] = total
        for k in (1, 2, 3):
            to = lax.rem(me["z"] + k, 2)
            src = LY.at[3, :, pl.ds(pl.multiple_of(to * 128, 128), 128)]
            shared["ln_z", k] = ln_send(src, LZ.at[k - 1], z=k)

    others = [(x, c) for x in range(4) for c in range(2) if x or c]

    def ln_x():
        total = LY[3, :, pl.ds(pl.multiple_of(lax.rem(me["z"], 2) * 128, 128), 128)]
        for k in (1, 2, 3):
            shared["ln_z", k].wait_recv()
            total = total + LZ[k - 1]
        LZ[3] = total
        for k, (x, c) in enumerate(others):
            shared["ln_x", k] = ln_send(LZ.at[3], LX.at[k], x=x, c=c)

    def ln_end():
        total = LZ[3]
        for k in range(7):
            shared["ln_x", k].wait_recv()
            total = total + LX[k]
        FLN[...] = total

    def many(layer, part, regions=(0, 1, 2)):
        return Many([reduce1[layer, part, r] for r in regions])

    def w_half(layer, h, a, n, ys=(0, 1, 2, 3)):
        parts = [
            W[layer][c, y, z, :, :, h, :, pl.ds(a, n)].reshape(64, n)
            for y in ys for z in (0, 1) for c in (0, 1)
        ]
        return jnp.concatenate(parts, axis=0)

    def w_down_rows(layer, a, n, ys=(0, 1, 2, 3)):
        parts = [
            W[layer][c, y, z, :, :, :, :, pl.ds(a, n)].reshape(128, n)
            for y in ys for z in (0, 1) for c in (0, 1)
        ]
        return jnp.concatenate(parts, axis=0)

    def settle(layer, part):
        drain(sum([item.sent for item in last[layer, part].items], []))
        for r in range(3):
            if part == "B" or part == "A":
                a, _ = cols_of(layer, part, r)

                @pl.loop(0, 16)
                def _(k):
                    c, y, z = k // 8, (k // 2) % 4, k % 2
                    for zh in (0, 1):
                        for xp in (0, 1):
                            even = W[layer][c, y, z, zh, xp, 0, :, pl.ds(a, 512)].astype(f32)
                            odd = W[layer][c, y, z, zh, xp, 1, :, pl.ds(a, 512)].astype(f32)
                            W[layer][c, y, z, zh, xp, 0, :, pl.ds(a, 512)] = jnp.concatenate(
                                [even[:8], odd[:8]], axis=0).astype(bf16)
                            W[layer][c, y, z, zh, xp, 1, :, pl.ds(a, 512)] = jnp.concatenate(
                                [even[8:], odd[8:]], axis=0).astype(bf16)

    block = 32

    def live_rows(r):
        place = lax.broadcasted_iota(jnp.int32, (block, 1), 0) + (head * rows + r * block)
        return (place < live_count[0]).astype(f32)

    def live_all():
        place = lax.broadcasted_iota(jnp.int32, (rows, 1), 0) + head * rows
        return (place < live_count[0]).astype(f32)

    def stats(v):
        mean = jnp.mean(v, axis=-1, keepdims=True)
        centred = v - mean
        spread = jnp.mean(centred * centred, axis=-1, keepdims=True)
        r = lax.rsqrt(spread + eps)
        return centred * r, r

    def norm(load, which, dst):
        gain = LNP[which:which + 1, :]
        shift = LNP[4 + which:5 + which, :]

        @pl.loop(0, rows // block)
        def _(r):
            at = pl.ds(pl.multiple_of(r * block, block), block)
            n, _ = stats(load(at))
            dst[at, :] = (n * gain + shift).astype(bf16)

    def norm_back(load, which, old, new, low):
        gain = LNP[which:which + 1, :]

        def step(r, carry):
            to_gain, to_shift = carry
            at = pl.ds(pl.multiple_of(r * block, block), block)
            n, scale = stats(load(at))
            gs = GS[at, :]
            e = gs * gain
            m1 = jnp.mean(e, axis=-1, keepdims=True)
            m2 = jnp.mean(e * n, axis=-1, keepdims=True)
            g = old(at) + scale * (e - m1 - n * m2)
            new(at, g)
            if low is not None:
                low[at, :] = (live_rows(r) * g).astype(bf16)
            to_gain = to_gain + jnp.sum((gs * n).reshape(block // 8, 8, width), axis=0)
            to_shift = to_shift + jnp.sum(gs.reshape(block // 8, 8, width), axis=0)
            return to_gain, to_shift

        zero = jnp.zeros((8, width), f32)
        to_gain, to_shift = lax.fori_loop(0, rows // block, step, (zero, zero))
        LNG[which:which + 1, :] = jnp.sum(to_gain, axis=0, keepdims=True)
        LNG[4 + which:5 + which, :] = jnp.sum(to_shift, axis=0, keepdims=True)

    def turn(src, keep, stage):
        for b in range(8):
            t = src[:, b * 128:(b + 1) * 128].T
            keep[b] = jnp.where(core == 0, t[:64], t[64:])
            stage[b] = jnp.where(core == 0, t[64:], t[:64])

    def turn_wide(src, keep, stage, blocks):
        for b in blocks:
            v0 = src[:, b * 256:b * 256 + 128]
            v1 = src[:, b * 256 + 128:b * 256 + 256]
            keep[b] = jnp.where(core == 0, v0, v1).T
            stage[b] = jnp.where(core == 0, v1, v0).T

    def both(keep, got):
        k, n = keep.shape[0] * keep.shape[1], keep.shape[2]
        return jnp.concatenate([keep[...].reshape(k, n), got[...].reshape(k, n)], axis=1)

    def pair(ref, a, n):
        return jnp.concatenate([ref[0, :, pl.ds(a, n)], ref[1, :, pl.ds(a, n)]], axis=0)

    def put_terms(sums, region, tile, y, z, x):
        pos = {"y": y, "z": z, "x": x}
        axes = (AXES[region], AXES[(region + 2) % 3], AXES[(region + 1) % 3])
        ref, at = sums.D(tuple(pos[a] for a in axes), pl.ds(sums.a, sums.n))
        ref[at] = tile.astype(bf16)

    def terms(layer, part, region, lhs, ref, columns):
        sums = sums_of(layer, part, region)
        if part == "C":
            value = dot(lhs, pair(ref, down_at[region], down_len[region]))
        else:
            left, right = (dot(lhs, pair(ref, columns(h), 512)) for h in (0, 1))
        for y in range(4):
            for zl in range(2):
                for zh in range(2):
                    for x in range(4):
                        k = ((y * 2 + zl) * 2 + zh) * 4 + x
                        if part == "C":
                            tile = value[k * 16:k * 16 + 16]
                        else:
                            tile = jnp.concatenate([left[k * 8:k * 8 + 8], right[k * 8:k * 8 + 8]], axis=0)
                        put_terms(sums, region, tile, y, zh * 2 + zl, x)

    scaling = HEAD_DIM ** (-0.5)

    def window(layer, h, which):
        at = pl.ds(h * 384 + which * 128, 128)
        return jnp.concatenate(
            [QKV[layer, :, at], LEAD[layer, :, at], jnp.zeros((128 - lead, 128), bf16)], axis=0
        )

    def probs(layer, h):
        q = QKV[layer, :, pl.ds(h * 384, 128)]
        k = window(layer, h, 1)
        s = contract_last(q, k) * scaling
        s = jnp.where(MASK[...] > 0, s, neg_fill)
        e = jnp.exp(s - jnp.max(s, axis=-1, keepdims=True))
        return q, k, e / jnp.sum(e, axis=-1, keepdims=True)

    def attend(layer, heads):
        for h in heads:
            _, _, p = probs(layer, h)
            ATT[:, h * 128:(h + 1) * 128] = dot(p.astype(bf16), window(layer, h, 2)).astype(bf16)

    def attend_back(layer):
        for h in range(HEADS):
            q, k, p = probs(layer, h)
            v = window(layer, h, 2)
            do = ATT[:, h * 128:(h + 1) * 128]
            gv = contract_rows(p.astype(bf16), do)
            gp = contract_last(do, v)
            gs = (p * (gp - jnp.sum(p * gp, axis=-1, keepdims=True))).astype(bf16)
            gq = dot(gs, k) * scaling
            gk = contract_rows(gs, q) * scaling
            GQKV[0, :, h * 384:h * 384 + 128] = gq.astype(bf16)
            GQKV[0, :, h * 384 + 128:h * 384 + 256] = gk[:128].astype(bf16)
            GQKV[0, :, h * 384 + 256:h * 384 + 384] = gv[:128].astype(bf16)
            TAIL[:, h * 256:h * 256 + 128] = gk[112:128]
            TAIL[:, h * 256 + 128:h * 256 + 256] = gv[112:128]
            RIMS[layer, :, h * 256:h * 256 + 128] = gk[128:144].astype(bf16)
            RIMS[layer, :, h * 256 + 128:h * 256 + 256] = gv[128:144].astype(bf16)

    def add_rim(layer):
        for h in range(HEADS):
            at = pl.ds(h * 256, 256)
            total = TAIL[:, at] + RIMR[layer, :, at].astype(f32)
            GQKV[0, 112:128, h * 384 + 128:h * 384 + 384] = total.astype(bf16)

    shared = {}

    def x_at(layer):
        if layer == 0:
            return lambda at: tokens[at, :].astype(f32)
        return lambda at: X1[at, :]

    def forward_norm(layer):
        norm(x_at(layer), 2 * layer, NRM)
        if layer == 0:
            shared["x", 0].wait_recv()
            n, _ = stats(XL[...].astype(f32))
            NL[0] = (n * LNP[0:1, :] + LNP[4:5, :]).astype(bf16)
        else:
            shared["x", 1] = send(NRM.at[pl.ds(rows - lead, lead), :], NL.at[1], after, "misc")
            drain([shared["n", 0]])
        turn(NRM, TN.at[layer], SN)
        shared["n", layer] = send(SN, UN.at[layer], sibling, "share")

    def forward_qkv(layer):
        if layer == 1:
            shared["x", 1].wait_recv()
        n = jnp.concatenate([NRM[...], NL[layer]], axis=0)
        for h in (0, 1):
            for r in range(3):
                a, _ = cols_of(layer, "A", r)
                at = pl.ds(h * 1536 + r * 512, 512)
                value = dot(n, w_half(layer, h, a, 512)).astype(bf16)
                QKV[layer, :, at] = value[:rows]
                LEAD[layer, :, at] = value[rows:]

    def forward_attend(layer):
        attend(layer, range(4, 8))
        if layer == 1:
            drain([shared["a", 0]])
        turn(ATT, TA.at[layer], SA)
        shared["a", layer] = send(SA, UA.at[layer], sibling, "share")

    def forward_up(layer):
        a_in = ATT[...]
        live = live_all()
        load = x_at(layer)
        a, _ = cols_of(layer, "B", OUT)
        for h in (0, 1):
            at = pl.ds(h * 512, 512)
            x = tokens[:, at].astype(f32) if layer == 0 else X1[:, at]
            MID[layer, :, at] = x + live * dot(a_in, w_half(layer, h, a, 512))
        if layer == 1:
            drain([shared["x", 1]])
        norm(lambda at: MID[layer, at, :], 2 * layer + 1, NRM)
        n = NRM[...]
        if layer == 1:
            drain([shared["f", 0, 0], shared["f", 0, 1]])
        for h in (0, 1):
            for r, base in UP:
                a, _ = cols_of(layer, "B", r)
                at = pl.ds(h * 1024 + base, 512)
                u = dot(n, w_half(layer, h, a, 512))
                cdf = 0.5 * (1.0 + lax.erf(u * (0.5 ** 0.5)))
                ACT[:, at] = (u * cdf).astype(bf16)
                slope = cdf + u * (jnp.exp(u * u * (-0.5)) * 0.3989422804014327)
                GP[layer, :, at] = slope.astype(bf16)
            turn_wide(ACT, TF.at[layer], SF, range(4 * h, 4 * h + 4))
            part = pl.ds(4 * h, 4)
            shared["f", layer, h] = send(SF.at[part], UF.at[layer, part], sibling, "share")
        if layer == 1:
            drain([shared["s", 0]])
        turn(NRM, TS.at[layer], SS)
        shared["s", layer] = send(SS, US.at[layer], sibling, "share")

    def forward_down(layer):
        live = live_all()
        a_in = ACT[...]
        for r in range(3):
            a, n = cols_of(layer, "C", r)
            at = pl.ds(down_at[r], n)
            v = MID[layer, :, at] + live * dot(a_in, w_down_rows(layer, a, n))
            if layer == 0:
                X1[:, at] = v
            else:
                act_out[:, at] = v.astype(bf16)

    def back_result(layer):
        if layer == 1:
            GRES[0] = (live_all() * cot[...].astype(f32)).astype(bf16)
        shared["res", layer] = send(GRES.at[0], GRES.at[1], sibling, "share")

    def terms_down(layer):
        shared["f", layer, 0].wait_recv()
        shared["f", layer, 1].wait_recv()
        shared["res", layer].wait_recv()
        lhs = both(TF.at[layer], UF.at[layer])
        for r in range(3):
            terms(layer, "C", r, lhs, GRES, None)
            reduce1[layer, "C", r].s1()

    def back_down(layer):
        g = GRES[0]
        for y in range(4):
            w = jnp.concatenate(
                [w_down_rows(layer, *cols_of(layer, "C", r), ys=(y,)) for r in range(3)], axis=1
            )
            at = pl.ds(y * 512, 512)
            GHID[0, :, at] = (contract_last(g, w) * GP[layer, :, at].astype(f32)).astype(bf16)
            if y % 2:
                part = pl.ds((y // 2) * 1024, 1024)
                shared["hid", layer, y // 2] = send(
                    GHID.at[0, :, part], GHID.at[1, :, part], sibling, "share")

    def terms_up(layer):
        shared["hid", layer, 0].wait_recv()
        shared["hid", layer, 1].wait_recv()
        shared["s", layer].wait_recv()
        lhs = both(TS.at[layer], US.at[layer])
        for r, base in UP:
            terms(layer, "B", r, lhs, GHID, lambda h, base=base: h * 1024 + base)
            reduce1[layer, "B", r].s1()

    def back_up_dot(layer):
        g = GHID[0]
        for y in range(4):
            w = jnp.concatenate(
                [w_half(layer, h, cols_of(layer, "B", r)[0], 512, ys=(y,)) for h in (0, 1) for r, _ in UP],
                axis=1,
            )
            GS[:, y * 256:(y + 1) * 256] = contract_last(g, w)

    def back_up_norm(layer):
        def old(at):
            return cot[at, :].astype(f32) if layer == 1 else GR[at, :]

        def new(at, g):
            GR[at, :] = g

        norm_back(lambda at: MID[layer, at, :], 2 * layer + 1, old, new, GBR.at[0])
        shared["br", layer] = send(GBR.at[0], GBR.at[1], sibling, "share")

    def terms_out(layer):
        shared["br", layer].wait_recv()
        shared["a", layer].wait_recv()
        terms(layer, "B", OUT, both(TA.at[layer], UA.at[layer]), GBR, lambda h: h * 512)
        reduce1[layer, "B", OUT].s1()

    def back_out(layer):
        g = GBR[0]
        for y in range(4):
            w = jnp.concatenate(
                [w_half(layer, h, cols_of(layer, "B", OUT)[0], 512, ys=(y,)) for h in (0, 1)], axis=1
            )
            ATT[:, y * 256:(y + 1) * 256] = contract_last(g, w).astype(bf16)

    def back_attend(layer):
        attend_back(layer)
        shared["back", layer] = send(RIMS.at[layer], RIMR.at[layer], before, "misc")
        part = pl.ds(0, rows - lead)
        shared["qkv", layer, 0] = send(GQKV.at[0, part], GQKV.at[1, part], sibling, "share")

    def back_rim(layer):
        shared["back", layer].wait_recv()
        add_rim(layer)
        part = pl.ds(rows - lead, lead)
        shared["qkv", layer, 1] = send(GQKV.at[0, part], GQKV.at[1, part], sibling, "share")

    def terms_qkv(layer):
        shared["qkv", layer, 0].wait_recv()
        shared["qkv", layer, 1].wait_recv()
        shared["n", layer].wait_recv()
        lhs = both(TN.at[layer], UN.at[layer])
        for r in range(3):
            terms(layer, "A", r, lhs, GQKV, lambda h, r=r: h * 1536 + r * 512)
            reduce1[layer, "A", r].s1()

    def w_qkv_back(layer, h, r, y):
        if layer == 1:
            return w_half(1, h, cols_of(1, "A", r)[0], 512, ys=(y,))
        parts = [
            ref[y, z, :, :, h, :, pl.ds(r * 512, 512)].reshape(64, 512)
            for z in (0, 1) for ref in (DS, RS)
        ]
        return jnp.concatenate(parts, axis=0)

    def back_qkv_dot(layer):
        g = GQKV[0]
        for y in range(4):
            w = jnp.concatenate([w_qkv_back(layer, h, r, y) for h in (0, 1) for r in range(3)], axis=1)
            GS[:, y * 256:(y + 1) * 256] = contract_last(g, w)

    def back_qkv_norm(layer):
        def old(at):
            return GR[at, :]

        if layer == 1:
            drain([shared["res", 1]])

            def new(at, g):
                GR[at, :] = g

            norm_back(x_at(1), 2, old, new, GRES.at[0])
        else:
            def new(at, g):
                dtok_out[at, :] = g.astype(bf16)

            norm_back(x_at(0), 0, old, new, None)

    stage = [
        local(w_qkv, FIN.at[:, 0:8, 0:3072]),
        local(w_out, FIN.at[:, 0:8, 3072:4096]),
        local(w_up, FIN.at[:, 8:16, 0:2048]),
        local(w_down.at[:, 0:8], FIN.at[:, 8:16, 2048:3072]),
        local(w_down.at[:, 8:16], FIN.at[:, 8:16, 3072:4096]),
    ]
    greeted = neighbours + [sibling, after, before] + [near(a, 2) for a in AXES]
    greeted += [device({**me, "x": (me["x"] + k) % 4, "c": 1 - core}) for k in (1, 2, 3)]
    barrier = pltpu.get_barrier_semaphore()
    for d in greeted:
        pl.semaphore_signal(barrier, inc=1, device_id=d, device_id_type=MESH)
    for c in stage:
        c.wait()
    mine = (core, me["y"], me["z"] % 2, me["z"] // 2, me["x"] // 2, me["x"] % 2)

    place = (dom * 8 + head) % 16

    def ln_tile():
        LNG[...] = jnp.zeros((8, width), f32)
        for k in range(4):
            LNG[k:k + 1, 0:8] = norm_gain[k // 2, k % 2:k % 2 + 1, :]
            LNG[4 + k:5 + k, 0:8] = norm_bias[k // 2, k % 2:k % 2 + 1, :]
        moved = pltpu.roll(LNG[:, 0:128], place * 8, 1)
        return jnp.concatenate([moved, jnp.zeros((8, 128), f32)], axis=0)

    def pack(layer, a, value):
        W[layer][mine + (slice(None), pl.ds(a, value.shape[-1]))] = value.astype(bf16)

    def halves(layer, top, base, n, at):
        return jnp.concatenate(
            [FIN[layer, top:top + 8, pl.ds(base + h * n + at, 512)] for h in (0, 1)], axis=0
        )

    def pack_all(layer):
        for r in range(3):
            a, n = cols_of(layer, "C", r)
            pack(layer, a, jnp.concatenate(
                [FIN[layer, 8:16, pl.ds(2048 + k * 1024 + down_at[r], n)] for k in (0, 1)], axis=0
            ))
            pack(layer, cols_of(layer, "A", r)[0], halves(layer, 0, 0, 1536, r * 512))
        pack(layer, cols_of(layer, "B", OUT)[0], halves(layer, 0, 3072, 512, 0))
        for r, at in UP:
            pack(layer, cols_of(layer, "B", r)[0], halves(layer, 8, 0, 1024, at))

    pack_all(0)
    pack(0, cols_of(0, "A", 2)[0] + 512, ln_tile())
    pl.semaphore_wait(barrier, len(greeted))
    first[0].spread()
    shared["x", 0] = send(tokens.at[pl.ds(rows - lead, lead), :], XL, after, "misc")
    pack_all(1)
    first[1].spread()

    first[0].items[1].gathered()
    second[0].items[1].s1()
    first[0].items[2].gathered()
    second[0].items[2].s1()
    first[0].items[0].gathered()
    second[0].items[0].s1()
    first[1].items[1].gathered()
    first[1].items[2].gathered()
    second[1].items[2].s1()
    first[1].items[0].gathered()
    second[1].items[0].s1()
    second[1].items[1].s1()
    second[0].items[0].s2()
    second[0].items[1].s2()
    back_result(1)
    q_pos = head * rows + lax.broadcasted_iota(jnp.int32, (rows, 256), 0)
    col = lax.broadcasted_iota(jnp.int32, (rows, 256), 1)
    second[0].items[2].s2()
    second[1].items[0].s2()
    k_pos = jnp.where(col < rows, col, jnp.where(col < rows + lead, col - rows - lead, -rows * 16))
    k_pos = k_pos + head * rows
    second[1].items[2].s2()
    begins = jnp.broadcast_to(seg[...].astype(f32), (rows, rows)).T
    second[1].items[1].s2()
    second[0].items[0].s3()
    second[0].items[2].s3()
    last[0, "B"].items[0].s1()
    second[0].items[1].s3()
    last[0, "A"].items[1].s1()
    last[0, "C"].items[2].s1()
    last[0, "A"].items[2].s1()
    last[0, "A"].items[0].s1()
    begins = jnp.concatenate([begins, begins], axis=1)
    last[0, "C"].items[1].s1()
    last[0, "C"].items[0].s1()
    second[1].items[1].s3()
    second[1].items[2].s3()
    last[0, "A"].items[1].s2()
    last[0, "B"].items[1].s1()
    last[0, "B"].items[2].s1()
    last[0, "A"].items[2].s2()
    last[0, "A"].items[1].s3()
    second[1].items[0].s3()
    last[0, "C"].items[1].s2()
    last[0, "A"].items[0].s2()
    last[0, "C"].items[2].s2()
    last[1, "A"].items[0].s1()
    last[0, "A"].items[0].s3()
    MASK[...] = ((k_pos.astype(f32) >= begins) & (k_pos <= q_pos)).astype(f32)

    last[0, "B"].items[2].s2()
    last[0, "B"].items[0].s2()
    last[1, "A"].items[2].s1()
    last[0, "B"].items[1].s2()
    last[0, "A"].items[2].s3()
    last[1, "A"].items[1].s1()
    last[0, "A"].ready()
    last[0, "B"].items[2].s3()
    last[0, "C"].items[0].s2()
    last[1, "B"].items[0].s1()
    last[0, "C"].items[2].s3()
    for item in first[0].items + second[0].items:
        drain(item.c1 + item.c2)
    settle(0, "A")

    last[1, "B"].items[2].s1()
    last[0, "B"].items[1].s3()
    ln_at = pl.ds(cols_of(0, "A", 2)[0] + 512, ln_cols)
    for y in range(4):
        for z in range(2):
            total = jnp.zeros((16, ln_cols), f32)
            for c in (0, 1):
                total = total + jnp.sum(
                    W0[c, y, z, :, :, :, :, ln_at].reshape(8, 16, ln_cols).astype(f32), axis=0
                )
            b = y * 2 + z
            LNP[:, b * 128:(b + 1) * 128] = total[:8]

    last[0, "C"].items[1].s3()
    last[0, "B"].items[0].s3()
    forward_norm(0)
    last[1, "B"].items[1].s1()
    forward_qkv(0)
    attend(0, range(4))
    last[1, "A"].items[2].s2()
    last[1, "A"].items[0].s2()
    last[0, "C"].items[0].s3()
    forward_attend(0)
    last[1, "A"].items[1].s2()
    last[1, "C"].items[0].s1()
    last[0, "B"].ready()
    settle(0, "B")
    forward_up(0)
    last[1, "B"].items[1].s2()
    last[0, "C"].ready()
    last[1, "C"].items[1].s1()
    last[1, "B"].items[2].s2()

    last[1, "A"].items[2].s3()
    last[1, "A"].items[1].s3()
    forward_down(0)
    last[1, "A"].items[0].s3()
    forward_norm(1)
    a_cols = [pl.ds(cols_of(0, "A", r)[0], 512) for r in range(3)]
    last[1, "B"].items[0].s2()
    last[1, "C"].items[2].s1()
    everything = (slice(None),) * 7
    parked = [
        local(W0.at[everything + (a_cols[r],)], park.at[everything + (pl.ds(r * 512, 512),)])
        for r in range(3)
    ]
    last[1, "A"].ready()
    last[1, "B"].items[1].s3()
    for item in first[1].items + second[1].items:
        drain(item.c1 + item.c2)
    settle(1, "A")
    last[1, "B"].items[2].s3()
    forward_qkv(1)
    last[1, "C"].items[0].s2()
    attend(1, range(4))
    last[1, "C"].items[2].s2()
    last[1, "B"].items[0].s3()
    last[1, "C"].items[1].s2()
    forward_attend(1)
    last[1, "B"].ready()
    settle(1, "B")
    last[1, "C"].items[2].s3()
    forward_up(1)
    for c in parked:
        c.wait()
    for d in neighbours:
        pl.semaphore_signal(rfree.at[1], inc=1, device_id=d, device_id_type=MESH)

    last[1, "C"].items[1].s3()
    last[1, "C"].items[0].s3()
    terms_down(1)
    last[1, "C"].ready()
    back_down(1)
    back_up_dot(1)
    terms_up(1)
    back_up_norm(1)
    reduce1[1, "C", 1].s2()
    back_out(1)
    terms_out(1)
    back_attend(1)
    reduce1[1, "B", 2].s2()
    reduce1[1, "B", 0].s2()
    reduce1[1, "C", 0].s2()
    reduce1[1, "B", 1].s2()
    reduce1[1, "C", 2].s2()
    back_rim(1)
    back_qkv_dot(1)
    pl.semaphore_wait(rfree.at[1], 6)
    terms_qkv(1)
    back_qkv_norm(1)
    forward_down(1)

    reduce1[1, "C", 2].s3()
    reduce1[1, "B", 2].s3()
    drain(sum([item.sent for item in last[1, "C"].items], []))
    for d in neighbours:
        pl.semaphore_signal(rfree.at[0], inc=1, device_id=d, device_id_type=MESH)
    drain([shared[k, 1, h] for k in ("hid", "qkv") for h in (0, 1)] + [shared["br", 1]])
    pl.semaphore_signal(gfree, inc=1, device_id=sibling, device_id_type=MESH)

    pl.semaphore_wait(gfree, 1)
    reduce1[1, "A", 0].s2()
    reduce1[1, "A", 2].s2()
    reduce1[1, "B", 1].s3()
    back_result(0)
    reduce1[1, "B", 0].s3()
    reduce1[1, "C", 0].s3()
    reduce2[1, "BC"].items[2].s1()
    back_down(0)
    pl.semaphore_wait(rfree.at[0], 6)
    terms_down(0)
    reduce1[1, "C", 1].s3()
    reduce2[1, "BC"].items[0].s1()
    back_up_dot(0)
    reduce2[1, "BC"].items[2].s2()
    terms_up(0)
    reduce1[0, "C", 1].s2()
    back_up_norm(0)
    reduce2[1, "BC"].items[1].s1()
    reduce1[1, "A", 0].s3()
    reduce1[1, "A", 1].s2()
    back_out(0)
    terms_out(0)
    reduce2[1, "BC"].items[2].s3()
    reduce1[0, "C", 0].s2()
    reduce1[1, "A", 2].s3()
    reduce2[1, "BC"].items[0].s2()
    reduce2[1, "A"].items[0].s1()
    back_attend(0)
    reduce1[0, "B", 2].s2()
    reduce2[1, "BC"].items[1].s2()
    reduce1[1, "A", 1].s3()
    reduce1[0, "C", 1].s3()
    reduce1[0, "C", 2].s2()
    reduce2[1, "A"].items[2].s1()
    reduce2[1, "A"].items[1].s1()
    reduce2[1, "BC"].items[0].s3()
    reduce2[1, "A"].items[0].s2()
    reduce3[1, "BC"].items[2].spread()
    reduce3[1, "BC"].items[0].spread()
    back_rim(0)
    reduce1[0, "B", 0].s2()
    reduce1[0, "C", 0].s3()
    reduce2[1, "BC"].items[1].s3()
    reduce3[1, "BC"].items[1].spread()
    reduce1[0, "B", 1].s2()
    terms_qkv(0)
    reduce1[0, "B", 1].s3()
    reduce1[0, "B", 0].s3()
    reduce3[1, "BC"].items[2].collect()
    reduce1[0, "B", 2].s3()
    reduce2[1, "A"].items[1].s2()
    reduce1[0, "A", 1].s2()
    reduce1[0, "A", 0].s2()
    reduce2[0, "BC"].items[0].s1()
    reduce1[0, "A", 2].s2()
    reduce3[1, "BC"].items[0].collect()
    reduce3[1, "BC"].items[1].collect()
    reduce1[0, "C", 2].s3()
    for item in sum((many(1, p).items for p in "BC"), []) + reduce2[1, "BC"].items + reduce3[1, "BC"].items:
        drain([c for c in (item.c1, item.c2, item.c3, item.c4, item.c5, item.c6) if c is not None])
    reduce2[1, "A"].items[0].s3()
    reduce2[0, "BC"].items[2].s1()
    everything = (slice(None),) * 6
    restored = [
        local(park.at[0], DS.at[everything + (pl.ds(0, 1536),)]),
        local(park.at[1], RS.at[everything + (pl.ds(0, 1536),)]),
    ]
    reduce2[0, "BC"].items[1].s1()
    for c in restored:
        c.wait()
    back_qkv_dot(0)
    back_qkv_norm(0)
    ln_y()
    reduce2[1, "A"].items[2].s2()
    reduce1[0, "A", 0].s3()
    reduce2[0, "A"].items[0].spread()
    reduce3[1, "A"].items[0].spread()
    reduce1[0, "A", 1].s3()
    reduce2[0, "BC"].items[2].s2()
    reduce2[0, "A"].items[1].spread()
    reduce1[0, "A", 2].s3()
    reduce2[1, "A"].items[1].s3()
    reduce2[0, "A"].items[2].spread()
    reduce2[0, "BC"].items[0].s2()
    ln_z()
    reduce2[0, "BC"].items[1].s2()
    reduce2[1, "A"].items[2].s3()
    reduce3[1, "A"].items[2].spread()
    reduce2[0, "BC"].items[2].s3()
    reduce2[0, "A"].items[0].collect()
    reduce3[1, "A"].items[1].spread()
    reduce3[0, "A"].items[0].spread()
    reduce3[0, "BC"].items[2].spread()
    reduce2[0, "A"].items[1].collect()
    reduce3[0, "A"].items[1].spread()
    reduce2[0, "BC"].items[0].s3()
    reduce3[0, "BC"].items[0].spread()
    ln_x()
    reduce2[0, "BC"].items[1].s3()
    reduce3[0, "BC"].items[1].spread()
    reduce2[0, "A"].items[2].collect()
    reduce3[0, "A"].items[2].spread()
    reduce3[0, "A"].items[1].collect()
    reduce3[1, "A"].items[2].collect()
    reduce3[1, "A"].items[1].collect()
    reduce3[0, "A"].items[0].collect()
    reduce3[0, "BC"].items[2].collect()
    reduce3[0, "BC"].items[0].collect()
    reduce3[1, "A"].items[0].collect()
    reduce3[0, "A"].items[2].collect()
    reduce3[0, "BC"].items[1].collect()
    ln_end()
    drain(list(pending.values()))


def results(act, dtok, fin, fln, act_out, dtok_out, d_qkv, d_out, d_up, d_down, d_gain, d_bias, turned):
    dom = lax.axis_index("dom")
    head = lax.axis_index("head")
    act_out[...] = act[...]
    dtok_out[...] = dtok[...]

    def put(dst, a, n, total, base):
        dst[:, :, pl.ds(base, n)] = fin[:, 0:8, pl.ds(a, n)]
        dst[:, :, pl.ds(total + base, n)] = fin[:, 8:16, pl.ds(a, n)]

    for r in range(3):
        put(d_qkv, cols_of(1, "A", r)[0], 512, 1536, r * 512)
        a, n = cols_of(1, "C", r)
        d_down[:, :, pl.ds(down_at[r], n)] = fin[:, :, pl.ds(a, n)]
    put(d_out, cols_of(1, "B", OUT)[0], 512, 512, 0)
    for r, at in UP:
        put(d_up, cols_of(1, "B", r)[0], 512, 1024, at)
    place = (dom * 8 + head) % 16
    turned[...] = pltpu.roll(fln[...], (128 - place * 8) % 128, 1)
    for k in range(4):
        d_gain[k // 2, k % 2:k % 2 + 1, :] = turned[k:k + 1, 0:8]
        d_bias[k // 2, k % 2:k % 2 + 1, :] = turned[4 + k:5 + k, 0:8]


def shards(
    tokens, w_qkv, w_out, w_up, w_down, norm_gain, norm_bias, seg_start, live_count, cotangent
):
    seg = seg_start.reshape(1, rows)
    vmem = pl.BlockSpec(memory_space=pltpu.VMEM)
    smem = pl.BlockSpec(memory_space=pltpu.SMEM)
    hbm = pl.BlockSpec(memory_space=pl.ANY)
    grid = (4, 2, 2, 2, 2, 16)

    def v(shape, kind=bf16):
        return pltpu.VMEM(shape, kind)

    def s(shape, kind):
        return jax.ShapeDtypeStruct(shape, kind)

    narrow, wide = (8, 64, 128), (8, 128, 128)
    out = pl.pallas_call(
        kernel,
        out_shape=(
            s((rows, width), bf16), s((rows, width), bf16), s((2, 16, 4096), f32),
            s((8, 128), f32), s((2,) + grid + (1536,), bf16),
        ),
        in_specs=[vmem, hbm, hbm, hbm, hbm, vmem, vmem, vmem, smem, vmem],
        out_specs=(vmem, vmem, vmem, vmem, hbm),
        scratch_shapes=[
            v((2,) + grid + (4096 + ln_cols,)), v((2,) + grid + (4096,)),
            v(grid + (2560,)), v(grid + (2560,)),
            v((4, 8, 256), f32), v((4, 8, 128), f32), v((7, 8, 128), f32),
            v((2,) + narrow), v((2,) + narrow), v((2,) + narrow), v((2,) + wide),
            v((2,) + narrow), v((2,) + narrow), v((2,) + narrow), v((2,) + wide),
            v(narrow), v(narrow), v(narrow), v(wide),
            v((2, rows, 1024)), v((2, rows, 2048)), v((2, rows, 1024)), v((2, rows, 3072)),
            v((2, rows, 3072)), v((2, lead, 3072)), v((2, lead, 2048)), v((2, lead, 2048)),
            v((lead, 2048), f32), v((lead, width)), v((2, lead, width)),
            v((rows, width), f32), v((2, rows, width), f32), v((rows, width), f32), v((rows, width), f32),
            v((2, rows, 2048)), v((rows, 2048)), v((rows, width)), v((rows, width)),
            v((rows, 256), f32), v((8, width), f32), v((8, width), f32),
            pltpu.SemaphoreType.DMA((n_send,)), pltpu.SemaphoreType.DMA((6 * n_recv + n_share + n_misc + 3 * n_far,)),
            pltpu.SemaphoreType.DMA((12,)), pltpu.SemaphoreType.REGULAR,
            pltpu.SemaphoreType.REGULAR((2,)),
        ],
        name="layers",
        compiler_params=pltpu.CompilerParams(
            collective_id=0, has_side_effects=True, vmem_limit_bytes=64 * 2 ** 20
        ),
    )(tokens, w_qkv, w_out, w_up, w_down, norm_gain, norm_bias, seg, live_count, cotangent)
    act, dtok, fin, fln, _ = out
    shapes = [a.shape for a in (w_qkv, w_out, w_up, w_down, norm_gain, norm_bias)]
    return pl.pallas_call(
        results,
        out_shape=(s((rows, width), bf16), s((rows, width), bf16)) + tuple(s(a, f32) for a in shapes),
        in_specs=[vmem] * 4,
        out_specs=(vmem,) * 8,
        scratch_shapes=[v((8, 128), f32)],
        name="results",
    )(act, dtok, fin, fln)


def solution(mesh):
    return jax.shard_map(
        shards,
        mesh=mesh,
        in_specs=(
            P(("dom", "head"), None),
            P(None, ("dom", "head"), None),
            P(None, ("dom", "head"), None),
            P(None, ("dom", "head"), None),
            P(None, ("dom", "head"), None),
            P(None, None, ("dom", "head")),
            P(None, None, ("dom", "head")),
            P(("dom", "head")),
            P("dom"),
            P(("dom", "head"), None),
        ),
        out_specs=(
            P(("dom", "head"), None),
            P(("dom", "head"), None),
            P(None, ("dom", "head"), None),
            P(None, ("dom", "head"), None),
            P(None, ("dom", "head"), None),
            P(None, ("dom", "head"), None),
            P(None, None, ("dom", "head")),
            P(None, None, ("dom", "head")),
        ),
        check_vma=False,
    )
```
